32 devices in a mesh: dp: 4 (over x, core), fsdp: 8 (over z, y).
Axes of the slice: x: 2, y: 2, z: 4, core: 2. Of those that a mesh axis runs over, the one named last changes fastest.
Arguments:
- frames_in: bfloat16 [1024, 8, 16, 384], P('fsdp', 'dp'), may hold values from -6 to 6
- lengths: int32 [8], P('dp'), may hold values from 256 to 1024, as said below
- w_qkv: bfloat16 [2, 384, 1536], P(None, None, ('dp', 'fsdp')), may hold values from -0.3125 to 0.3125
- w_out: bfloat16 [2, 512, 384], P(None, ('dp', 'fsdp'))
- w_up: bfloat16 [2, 384, 1536], P(None, None, ('dp', 'fsdp')), may hold values from -0.3125 to 0.3125
- b_up: bfloat16 [2, 1536], P(None, ('dp', 'fsdp')), may hold values from -3 to 3
- w_down: bfloat16 [2, 1536, 384], P(None, ('dp', 'fsdp')), may hold values from -0.15625 to 0.15625
- gains: bfloat16 [2, 2, 384], P(None, None, 'fsdp'), may hold values from 0.099609375 to 1.8984375
- b_down: bfloat16 [2, 384], P(None, 'fsdp'), may hold values from -3 to 3
- w_gate: bfloat16 [2, 8, 384], P(None, None, 'fsdp'), may hold values from -0.3125 to 0.3125
- b_gate: bfloat16 [2, 8], replicated, may hold values from -4 to 4
- grad_out: bfloat16 [1024, 8, 16, 384], P('fsdp', 'dp'), may hold values from -6 to 6
Outputs:
- out: bfloat16 [1024, 8, 16, 384], P('fsdp', 'dp')
- grad_input: float32 [1024, 8, 16, 384], P('fsdp', 'dp')
- grad_w_qkv: float32 [2, 384, 1536], P(None, None, ('dp', 'fsdp'))
- grad_w_out: float32 [2, 512, 384], P(None, ('dp', 'fsdp'))
- grad_w_up: float32 [2, 384, 1536], P(None, None, ('dp', 'fsdp'))
- grad_b_up: float32 [2, 1536], P(None, ('dp', 'fsdp'))
- grad_w_down: float32 [2, 1536, 384], P(None, ('dp', 'fsdp'))
- grad_gains: float32 [2, 2, 384], P(None, None, 'fsdp')
- grad_b_down: float32 [2, 384], P(None, 'fsdp')
- grad_w_gate: float32 [2, 8, 384], P(None, None, 'fsdp')
- grad_b_gate: float32 [2, 8], replicated
The draws below stay inside these ranges and needn't reach their ends.
Inputs may be any that keep to these rules, and one draw needn't show every extreme that they name: lengths[c] counts the valid frames of clip c, counted from frame 0; among the 2 clips of each index of dp one has all 1024 frames valid.
All inputs are finite; a program needn't handle non-finite values.
Results may differ from the reference program's by a relative error of at most 0.025.
Values may be sent and summed in bfloat16 or wider, within the bound.
No kernel may reach another device: no remote copies, remote signals or barrier semaphores. Data moves between devices by JAX's collectives and lax.ppermute only.
A program may use at most 512 MiB of HBM per device.

```python
import math
import jax
import jax.numpy as jnp
from jax import lax

D = 384
HEADS = 8
HEAD_DIM = 64
FF = 1536
BANDS = 16
CLIPS_DEV = 2
FRAMES = 1024
CLIPS = 8


def draw_lengths(key, part):
    key = jax.random.fold_in(key, 11)
    pick_key, size_key = jax.random.split(key)
    drawn = jax.random.randint(size_key, (CLIPS,), FRAMES // 4, FRAMES + 1)
    chosen = jax.random.randint(pick_key, (CLIPS // CLIPS_DEV, 1), 0, CLIPS_DEV)
    slot_ids = jnp.arange(CLIPS_DEV, dtype=jnp.int32)[None, :]
    full_clip = (slot_ids == chosen).reshape(CLIPS)
    return jnp.where(full_clip, FRAMES, drawn).astype(jnp.int32)


def draw_w_out(key, part):
    key = jax.random.fold_in(key, 23)
    values = jax.random.truncated_normal(key, -6.0, 6.0, (2, HEADS * HEAD_DIM, D), jnp.float32)
    spread = jnp.sqrt(jnp.array([FRAMES, BANDS], jnp.float32) / (HEADS * HEAD_DIM))
    return (values * spread[:, None, None]).astype(jnp.bfloat16)


def level_of(rng, shape, cuts, smallest, high):
    def one(position, blocks):
        draws = jax.random.uniform(jax.random.fold_in(jax.random.fold_in(rng, 6), position), (blocks,), jnp.float32, smallest / len(cuts), high / len(cuts))
        return jnp.repeat(jnp.exp(draws), shape[position] // blocks).reshape((-1,) + (1,) * (len(shape) - position - 1))

    loudness = one(*cuts[0])
    for cut in cuts[1:]:
        loudness = loudness * one(*cut)
    return loudness


def noise(stream_key, dims, deviation, limit, shards=(), kind=jnp.bfloat16):
    values = deviation * jax.random.normal(stream_key, dims, jnp.float32)
    if shards:
        values = values * level_of(stream_key, dims, shards, -0.22, 0.18)
    return jnp.clip(values, -limit, limit).astype(kind)


def setup_inputs(seed: int = 0) -> dict:
    arg_keys = jax.random.split(jax.random.key(seed), 13)
    return {
        "frames_in": noise(arg_keys[0], (FRAMES, CLIPS, BANDS, D), 1.0, 6.0, ((0, 8), (1, 4))),
        "lengths": draw_lengths(jax.random.fold_in(arg_keys[12], 71), 0),
        "w_qkv": noise(arg_keys[2], (2, D, 3 * HEADS * HEAD_DIM), D ** -0.5, 0.3125, ((2, 32),)),
        "w_out": draw_w_out(jax.random.fold_in(arg_keys[12], 71), 0),
        "w_up": noise(arg_keys[4], (2, D, FF), D ** -0.5, 0.3125, ((2, 32),)),
        "b_up": noise(arg_keys[5], (2, FF), 0.5, 3.0, ((1, 32),)),
        "w_down": noise(arg_keys[6], (2, FF, D), FF ** -0.5, 0.15625, ((1, 32),)),
        "gains": jnp.clip(1.0 + 0.18 * jax.random.normal(arg_keys[7], (2, 2, D), jnp.float32), 0.099609375, 1.8984375).astype(jnp.bfloat16),
        "b_down": noise(arg_keys[8], (2, D), 0.5, 3.0, ((1, 8),)),
        "w_gate": noise(arg_keys[9], (2, HEADS, D), D ** -0.5, 0.3125, ((2, 8),)),
        "b_gate": noise(arg_keys[10], (2, HEADS), 1.0, 4.0),
        "grad_out": noise(arg_keys[11], (FRAMES, CLIPS, BANDS, D), 1.0, 6.0, ((0, 8), (1, 4))),
    }


PRECISION = lax.Precision.HIGHEST
EPSILON = 1e-06
NEGATIVE = -1e+30

@jax.custom_vjp
def low(v):
    return lax.optimization_barrier(v.astype(jnp.bfloat16)).astype(jnp.float32)

@jax.custom_vjp
def low_back(v):
    return v

def low_keep(v):
    return (low(v), None)

def low_pass(kept, grad):
    return (grad,)

def back_keep(v):
    return (v, None)

def back_low(kept, grad):
    return (low(grad),)
low.defvjp(low_keep, low_pass)
low_back.defvjp(back_keep, back_low)

def rotary_table(positions, half_dim):
    freq_steps = jnp.exp(jnp.arange(half_dim, dtype=jnp.float32) * (-math.log(10000.0) / half_dim))
    angles = positions.astype(jnp.float32)[:, None] * freq_steps[None, :]
    return (jnp.cos(angles), jnp.sin(angles))

def rotate(values, cosine, sine):
    half_dim = values.shape[-1] // 2
    first_half = values[..., :half_dim]
    second_half = values[..., half_dim:]
    return jnp.concatenate([first_half * cosine - second_half * sine, second_half * cosine + first_half * sine], axis=-1)

def rms_scale(hidden, gain_vec):
    return hidden * lax.rsqrt(lax.optimization_barrier(jnp.mean(hidden * hidden, axis=-1, keepdims=True)) + EPSILON) * gain_vec

def attend(query_low, key_low, value_low, valid_keys):
    scores = jnp.einsum('qbhe,kbhe->bhqk', query_low, key_low, precision=PRECISION) * HEAD_DIM ** (-0.5)
    scores = jnp.where(valid_keys[:, None, None, :], low_back(scores), NEGATIVE)
    softmax_out = jax.nn.softmax(scores, axis=-1)
    return jnp.einsum('bhqk,kbhe->qbhe', low(softmax_out), value_low, precision=PRECISION)

def block(hidden, params, layer_slot, cosine, sine, mixer):
    w_qkv, w_out, w_up, b_up, w_down, gains, b_down, w_gate, b_gate = params
    leading = hidden.shape[:-1]
    normed = low(rms_scale(hidden, gains[layer_slot, 0]))
    mixed = low_back(jnp.einsum('...d,df->...f', normed, w_qkv[layer_slot], precision=PRECISION))
    mixed = mixed.reshape(leading + (3, HEADS, HEAD_DIM))
    query_low = low(rotate(mixed[..., 0, :, :], cosine, sine))
    key_low = low(rotate(mixed[..., 1, :, :], cosine, sine))
    value_low = low(mixed[..., 2, :, :])
    logits = jnp.einsum('...d,hd->...h', normed, w_gate[layer_slot], precision=PRECISION) + b_gate[layer_slot]
    gate_prob = jax.nn.sigmoid(low_back(logits))
    attended = low(low_back(mixer(query_low, key_low, value_low)))
    gated = low(attended * gate_prob[..., None]).reshape(leading + (HEADS * HEAD_DIM,))
    middle = hidden + low_back(jnp.einsum('...f,fd->...d', gated, w_out[layer_slot], precision=PRECISION))
    normed_two = low(rms_scale(middle, gains[layer_slot, 1]))
    up_proj = low_back(jnp.einsum('...d,df->...f', normed_two, w_up[layer_slot], precision=PRECISION) + b_up[layer_slot])
    activated = low(jax.nn.gelu(up_proj, approximate=False))
    down_proj = jnp.einsum('...f,fd->...d', activated, w_down[layer_slot], precision=PRECISION) + b_down[layer_slot]
    return middle + low_back(down_proj)

def clip_layer(params, clip_input, clip_length):
    frame_total = clip_input.shape[0]
    half_dim = HEAD_DIM // 2
    frame_cos, frame_sin = rotary_table(jnp.arange(frame_total, dtype=jnp.int32), half_dim)
    band_cos, band_sin = rotary_table(jnp.arange(BANDS, dtype=jnp.int32), half_dim)
    valid_frames = jnp.arange(frame_total, dtype=jnp.int32) < clip_length

    def time_mixer(query_low, key_low, value_low):

        def single(element):
            query_one, key_one, value_one = element
            return attend(query_one[:, None], key_one[:, None], value_one[:, None], valid_frames[None, :])[:, 0]
        moved = lax.map(jax.checkpoint(single), (jnp.moveaxis(query_low, 1, 0), jnp.moveaxis(key_low, 1, 0), jnp.moveaxis(value_low, 1, 0)))
        return jnp.moveaxis(moved, 0, 1)

    def band_mixer(query_low, key_low, value_low):
        valid_bands = jnp.ones((frame_total, BANDS), dtype=jnp.bool_)
        result = attend(jnp.moveaxis(query_low, 1, 0), jnp.moveaxis(key_low, 1, 0), jnp.moveaxis(value_low, 1, 0), valid_bands)
        return jnp.moveaxis(result, 0, 1)
    hidden = block(clip_input, params, 0, frame_cos[:, None, None, :], frame_sin[:, None, None, :], time_mixer)
    return block(hidden, params, 1, band_cos[None, :, None, :], band_sin[None, :, None, :], band_mixer)

def forward(inputs, lengths, params):
    per_clip = jnp.moveaxis(inputs, 1, 0)
    layer_fn = jax.checkpoint(lambda element: clip_layer(params, element[0], element[1]))
    return jnp.moveaxis(lax.map(layer_fn, (per_clip, lengths)), 0, 1)

def reference(frames_in, lengths, w_qkv, w_out, w_up, b_up, w_down, gains, b_down, w_gate, b_gate, grad_out):
    params = (w_qkv.astype(jnp.float32), w_out.astype(jnp.float32), w_up.astype(jnp.float32), b_up.astype(jnp.float32), w_down.astype(jnp.float32), gains.astype(jnp.float32), b_down.astype(jnp.float32), w_gate.astype(jnp.float32), b_gate.astype(jnp.float32))
    inputs = frames_in.astype(jnp.float32)
    result, pullback = jax.vjp(lambda tensor, weights: forward(tensor, lengths, weights), inputs, params)
    grad_input, grads = pullback(grad_out.astype(jnp.float32))
    return (result.astype(jnp.bfloat16), grad_input, grads[0], grads[1], grads[2], grads[3], grads[4], grads[5], grads[6], grads[7], grads[8])
```

```python
from functools import partial
import math

import jax
import jax.numpy as jnp
import numpy as np
from jax import lax
from jax.experimental import pallas as pl
from jax.experimental.pallas import tpu as pltpu
from jax.sharding import PartitionSpec as P

HEADS = 8
HEAD_DIM = 64
HALF = HEAD_DIM // 2
HEAD_WIDTH = HEADS * HEAD_DIM
PAIRS = HEADS // 2
LANES = 2 * HEAD_DIM
TILE_FRAMES = 16
EPSILON = 1e-06
NEGATIVE = -1e30
LOG2E = 1.0 / math.log(2.0)
LN2 = math.log(2.0)
QUERY_SCALE = HEAD_DIM**-0.5 * LOG2E
BLOCK_Q = 256

BF = jnp.bfloat16
F32 = jnp.float32


def nn(a, b):
    return jnp.dot(a, b, preferred_element_type=F32)


def nt(a, b):
    return lax.dot_general(a, b, (((1,), (1,)), ((), ())), preferred_element_type=F32)


def tn(a, b):
    return lax.dot_general(a, b, (((0,), (0,)), ((), ())), preferred_element_type=F32)


def rms(hidden):
    scale = lax.rsqrt(jnp.mean(hidden * hidden, axis=-1, keepdims=True) + EPSILON)
    return hidden * scale, scale


def rms_back(unit, scale, gain, grad):
    weighted = grad * gain
    inner = jnp.mean(weighted * unit, axis=-1, keepdims=True)
    return scale * (weighted - unit * inner)


def gelu_pair(up):
    t = 1.0 / (1.0 + (0.3275911 * math.sqrt(0.5)) * jnp.abs(up))
    bell = jnp.exp2((-0.5 * LOG2E) * (up * up))
    poly = t * (
        0.127414796
        + t * (-0.142248368 + t * (0.710706871 + t * (-0.726576013 + t * 0.530702714)))
    )
    tail = poly * bell
    cdf = jnp.where(up >= 0.0, 1.0 - tail, tail)
    return up * cdf, cdf + (up * bell) * (1.0 / math.sqrt(2.0 * math.pi))


def project(normed, w_ext, tables, b_gate):
    cos_q, sin_q, cos_k, sin_k = tables
    width = HEAD_WIDTH
    plain = nt(normed, w_ext[: 2 * width])
    swapped = nt(normed, w_ext[2 * width : 4 * width])
    value = nt(normed, w_ext[4 * width : 5 * width]).astype(BF)
    gate = jax.nn.sigmoid(nt(normed, w_ext[5 * width :]) + b_gate)
    queries, keys = [], []
    for pair in range(2 * PAIRS):
        at = slice(pair * LANES, (pair + 1) * LANES)
        cos, sin = (cos_q, sin_q) if pair < PAIRS else (cos_k, sin_k)
        turned = (plain[:, at] * cos + swapped[:, at] * sin).astype(BF)
        (queries if pair < PAIRS else keys).append(turned)
    return queries, keys, value, gate


def attend_block(query, key_aug, value_one, extra_q, low, high, slot):
    own, other = (low, high) if slot == 0 else (high, low)
    query_own = query * own
    scores = nt(query_own + extra_q * other, key_aug)
    top = jnp.max(scores, axis=-1, keepdims=True)
    probs = jnp.exp2(scores - top).astype(BF)
    mixed = nn(probs, value_one)
    total = mixed[:, LANES:]
    lse = top + jnp.log2(total)
    hi = lse.astype(BF)
    rest = lse - hi.astype(F32)
    mid = rest.astype(BF)
    lo = (rest - mid.astype(F32)).astype(BF)
    return mixed[:, :LANES] / total, query_own, (hi, mid, lo)


def keep_query(query_own, terms, extra_q, picks, other):
    hi, mid, lo = terms
    return query_own + other * (extra_q - hi * picks[0] - mid * picks[1] - lo * picks[2])


def attend_back_block(query_aug, key_aug, value_aug, grad_aug, key_t):
    probs = jnp.exp2(nt(key_aug, query_aug))
    grad_scores = (probs * nt(value_aug, grad_aug)).astype(BF)
    grad_value = nn(probs.astype(BF), grad_aug)
    grad_key = nn(grad_scores, query_aug)
    grad_query_t = nn(key_t, grad_scores)
    return grad_query_t, grad_key, grad_value


def unrotate(grad, cos, sin, swap_t):
    return grad * cos + nn((grad * sin).astype(BF), swap_t)


def lane_masks():
    lane = lax.broadcasted_iota(jnp.int32, (1, LANES), 1)
    inner = lane % HEAD_DIM
    low = jnp.where(lane < HEAD_DIM, 1.0, 0.0).astype(BF)
    high = jnp.where(lane < HEAD_DIM, 0.0, 1.0).astype(BF)
    picks = tuple(jnp.where(inner == k, 1.0, 0.0).astype(BF) for k in range(3))
    return low, high, picks, inner


def pair_back(queries, keys, values, grads, low, high, picks, extra_k, block_q):
    rows = keys.shape[0]
    key_t = keys.T
    is_low = lax.broadcasted_iota(jnp.int32, (1, LANES), 1) < HEAD_DIM
    two = picks[0] + picks[1]
    query_parts, key_sums, value_sums = [], [], []
    for slot in range(2):
        own, other = (low, high) if slot == 0 else (high, low)
        key_aug = keys * own + extra_k * other
        value_aug = values * own + two * other
        key_sum = value_sum = None
        parts = []
        for start in range(0, rows, block_q):
            at = slice(start, start + block_q)
            grad_query_t, grad_key, grad_value = attend_back_block(
                queries[slot][at],
                key_aug,
                value_aug,
                grads[slot][at],
                key_t[slot * HEAD_DIM : (slot + 1) * HEAD_DIM],
            )
            key_sum = grad_key if key_sum is None else key_sum + grad_key
            value_sum = grad_value if value_sum is None else value_sum + grad_value
            parts.append(grad_query_t)
        query_parts.append(parts)
        key_sums.append(key_sum)
        value_sums.append(value_sum)
    blocks = [
        jnp.concatenate([one, two_], axis=0).T for one, two_ in zip(query_parts[0], query_parts[1])
    ]
    grad_query = jnp.concatenate(blocks, axis=0) if len(blocks) > 1 else blocks[0]
    grad_key = jnp.where(is_low, key_sums[0], key_sums[1]) * LN2
    grad_value = jnp.where(is_low, value_sums[0], value_sums[1])
    return grad_query * HEAD_DIM**-0.5, grad_key, grad_value


def feed_forward(middle, gain, w_up, b_up, w_down, b_down):
    unit, scale = rms(middle)
    normed = (unit * gain).astype(BF)
    act, slope = gelu_pair(nt(normed, w_up) + b_up)
    act = act.astype(BF)
    return middle + (nn(act, w_down) + b_down), normed, unit, scale, act, slope


def branch_back(grad_branch, w_out, attended, gate, sum_heads, sum_swapped):
    grad_gated = nt(grad_branch, w_out)
    att = attended.astype(F32)
    grad_att = (grad_gated * gate).astype(BF)
    logit_terms = (grad_gated * att * (gate * (1.0 - gate))).astype(BF)
    grad_logit = nn(logit_terms, sum_heads).astype(BF)
    delta = nn((grad_att.astype(F32) * att).astype(BF), sum_swapped)
    return grad_att, grad_logit, delta


def grads_with_delta(grad_att, delta, low, high, picks):
    hi = delta.astype(BF)
    mid = (delta - hi.astype(F32)).astype(BF)
    extra = -(hi * picks[0] + mid * picks[1])
    return grad_att * low + extra * high, grad_att * high + extra * low


def col_sum(values):
    return jnp.sum(values.astype(F32), axis=0, keepdims=True)


def flat(ref):
    value = ref[...]
    return value.reshape(-1, value.shape[-1])


def permute_kernel(perm_ref, x_ref, o_ref):
    moved = nn(perm_ref[...], flat(x_ref))
    o_ref[...] = moved.astype(o_ref.dtype).reshape(o_ref.shape)


def to_sequences(frames, clip, perm):
    rows, _, bands, width = frames.shape
    return pl.pallas_call(
        permute_kernel,
        grid=(rows // TILE_FRAMES,),
        in_specs=[
            pl.BlockSpec(perm.shape, lambda i: (0, 0)),
            pl.BlockSpec((TILE_FRAMES, 1, bands, width), lambda i: (i, clip, 0, 0)),
        ],
        out_specs=pl.BlockSpec((bands, TILE_FRAMES, width), lambda i: (0, i, 0)),
        out_shape=jax.ShapeDtypeStruct((bands, rows, width), BF),
        name="frames_to_sequences",
    )(perm, frames)


def fill_kernel(perm_ref, x_ref, *refs):
    permute_kernel(perm_ref, x_ref, refs[-1])


def to_frames(sequences, clip, clips, perm_back, target):
    bands, rows, width = sequences.shape
    return pl.pallas_call(
        fill_kernel,
        grid=(rows // TILE_FRAMES,),
        in_specs=[
            pl.BlockSpec(perm_back.shape, lambda i: (0, 0)),
            pl.BlockSpec((bands, TILE_FRAMES, width), lambda i: (0, i, 0)),
        ]
        + [pl.BlockSpec(memory_space=pl.ANY)] * len(target),
        out_specs=pl.BlockSpec((TILE_FRAMES, 1, bands, width), lambda i: (i, clip, 0, 0)),
        out_shape=jax.ShapeDtypeStruct((rows, clips, bands, width), F32),
        input_output_aliases={2: 0} if target else {},
        name="sequences_to_frames",
    )(perm_back, sequences, *target)


def const_spec(array):
    zeros = (0,) * array.ndim
    return pl.BlockSpec(array.shape, lambda *_: zeros, pipeline_mode=pl.Buffered(1))


def cost(rows, per_row, nbytes):
    return pl.CostEstimate(flops=int(2 * rows * per_row), bytes_accessed=nbytes, transcendentals=0)


def params(megabytes, semantics=None):
    return pltpu.CompilerParams(vmem_limit_bytes=megabytes << 20, dimension_semantics=semantics)


def extend_weights(w_ref, wg_ref, scratch):
    width = HEAD_WIDTH
    scratch[: 2 * width] = w_ref[: 2 * width]
    for start in range(0, 2 * width, HEAD_DIM):
        at = 2 * width + start
        scratch[at : at + HALF] = -w_ref[start + HALF : start + HEAD_DIM]
        scratch[at + HALF : at + HEAD_DIM] = w_ref[start : start + HALF]
    scratch[4 * width : 5 * width] = w_ref[2 * width :]
    gates = wg_ref[...].astype(F32)
    for head in range(HEADS):
        at = 5 * width + head * HEAD_DIM
        row = jnp.broadcast_to(gates[head : head + 1], (HEAD_DIM, gates.shape[1]))
        scratch[at : at + HEAD_DIM] = row.astype(BF)


def project_kernel(
    x_ref, cq, sq, ck, sk, wq_ref, wg_ref, gain_ref, bg_ref, qkv_ref, gate_ref, w_ref
):
    seqs = x_ref.shape[1]

    @pl.when(pl.program_id(0) == 0)
    def _():
        extend_weights(wq_ref, wg_ref, w_ref)

    unit, _ = rms(flat(x_ref).astype(F32))
    normed = (unit * gain_ref[...]).astype(BF)

    def table(ref):
        value = ref[...]
        if seqs > 1:
            value = jnp.broadcast_to(value[:, None], (value.shape[0], seqs) + value.shape[1:])
        return value.reshape(-1, LANES)

    queries, keys, value, gate = project(
        normed, w_ref, (table(cq), table(sq), table(ck), table(sk)), bg_ref[...]
    )
    lead = qkv_ref.shape[:-1]
    for pair, tensor in enumerate(queries + keys):
        qkv_ref[..., pair * LANES : (pair + 1) * LANES] = tensor.reshape(lead + (LANES,))
    qkv_ref[..., 2 * HEAD_WIDTH :] = value.reshape(lead + (HEAD_WIDTH,))
    gate_ref[...] = gate.astype(gate_ref.dtype).reshape(gate_ref.shape)


def source_block(groups, seqs, rows, target):
    block = max(1, target // (seqs * rows))
    return math.gcd(groups, block)


def time_project(x, tables, wq, wg, gain, b_gate):
    groups, seqs, rows, width = x.shape
    sb = source_block(groups, seqs, rows, 512)

    def rows_spec(lanes):
        return pl.BlockSpec((sb, seqs, rows, lanes), lambda i: (i, 0, 0, 0))

    table_spec = pl.BlockSpec((sb, rows, LANES), lambda i: (i, 0, 0))
    return pl.pallas_call(
        project_kernel,
        grid=(groups // sb,),
        in_specs=[rows_spec(width)]
        + [table_spec] * 4
        + [const_spec(wq), const_spec(wg), const_spec(gain), const_spec(b_gate)],
        out_specs=[rows_spec(3 * HEAD_WIDTH), rows_spec(HEAD_WIDTH)],
        scratch_shapes=[pltpu.VMEM((6 * HEAD_WIDTH, width), BF)],
        out_shape=[
            jax.ShapeDtypeStruct((groups, seqs, rows, 3 * HEAD_WIDTH), BF),
            jax.ShapeDtypeStruct((groups, seqs, rows, HEAD_WIDTH), BF),
        ],
        compiler_params=params(56),
        cost_estimate=cost(groups * seqs * rows, 6 * HEAD_WIDTH * width * 2, 1 << 20),
        name="time_project",
    )(x, *tables, wq, wg, gain, b_gate)


def time_extra(rows, length, inner):
    position = lax.broadcasted_iota(jnp.int32, (rows, LANES), 0)
    blocked = jnp.where(position >= length, NEGATIVE, 0.0)
    ones = jnp.where(inner < 3, 1.0, 0.0)
    extra_k = jnp.where(inner == 3, blocked, jnp.broadcast_to(ones, (rows, LANES))).astype(BF)
    extra_q = jnp.where(inner == 3, 1.0, 0.0).astype(BF)
    return extra_q, extra_k


def time_attend_kernel(len_ref, q_ref, k_ref, v_ref, att_ref, keep_ref):
    low, high, picks, inner = lane_masks()
    keys, values = flat(k_ref), flat(v_ref)
    rows = keys.shape[0]
    extra_q, extra_k = time_extra(rows, len_ref[pl.program_id(0)], inner)
    ones = jnp.ones((rows, LANES), BF)
    queries = flat(q_ref)
    block = math.gcd(rows, BLOCK_Q)
    per_source = q_ref.shape[2]
    key_augs = (keys * low + extra_k * high, keys * high + extra_k * low)
    value_ones = (
        jnp.concatenate([values * low, ones], axis=1),
        jnp.concatenate([values * high, ones], axis=1),
    )
    for start in range(0, rows, block):
        query = queries[start : start + block]
        src = slice(start // per_source, (start + block) // per_source)
        shape = (block // per_source, 1, per_source, LANES)
        total = None
        for slot in range(2):
            out, query_own, terms = attend_block(
                query, key_augs[slot], value_ones[slot], extra_q, low, high, slot
            )
            kept = keep_query(query_own, terms, extra_q, picks, (high, low)[slot])
            keep_ref[src, :, :, slot * LANES : (slot + 1) * LANES] = kept.reshape(shape)
            total = out if total is None else total + out
        att_ref[src] = total.astype(BF).reshape(shape)


def time_attend(qkv, lens):
    groups, seqs, rows, _ = qkv.shape

    def spec(lanes, first):
        return pl.BlockSpec((groups, 1, rows, lanes), lambda s, p, *_: (0, s, 0, first + p))

    return pl.pallas_call(
        time_attend_kernel,
        grid_spec=pltpu.PrefetchScalarGridSpec(
            num_scalar_prefetch=1,
            grid=(seqs, PAIRS),
            in_specs=[spec(LANES, 0), spec(LANES, PAIRS), spec(LANES, 2 * PAIRS)],
            out_specs=[spec(LANES, 0), spec(2 * LANES, 0)],
        ),
        out_shape=[
            jax.ShapeDtypeStruct((groups, seqs, rows, HEAD_WIDTH), BF),
            jax.ShapeDtypeStruct((groups, seqs, rows, 2 * HEAD_WIDTH), BF),
        ],
        compiler_params=params(56),
        cost_estimate=cost(groups * seqs * rows, groups * rows * HEADS * 2 * 256 * 2, 1 << 20),
        name="time_attend",
    )(lens, qkv, qkv, qkv)


def time_mlp_kernel(
    x_ref, att_ref, gate_ref, wo, wu, wd, gain, bu, bd, h_ref, mid_ref, act_ref, slope_ref
):
    gated = (flat(att_ref).astype(F32) * flat(gate_ref).astype(F32)).astype(BF)
    middle = flat(x_ref).astype(F32) + nn(gated, wo[...])
    result, _, _, _, act, slope = feed_forward(middle, gain[...], wu[...], bu[...], wd[...], bd[...])
    h_ref[...] = result.astype(BF).reshape(h_ref.shape)
    mid_ref[...] = middle.reshape(mid_ref.shape)
    act_ref[...] = act.reshape(act_ref.shape)
    slope_ref[...] = slope.astype(BF).reshape(slope_ref.shape)


def time_mlp(x, attended, gate, weights):
    groups, seqs, rows, width = x.shape
    hidden = weights[1].shape[0]
    sb = source_block(groups, seqs, rows, 512)

    def rows_spec(lanes):
        return pl.BlockSpec((sb, seqs, rows, lanes), lambda i: (i, 0, 0, 0))

    def out(lanes, dtype):
        return jax.ShapeDtypeStruct((groups, seqs, rows, lanes), dtype)

    return pl.pallas_call(
        time_mlp_kernel,
        grid=(groups // sb,),
        in_specs=[rows_spec(width), rows_spec(HEAD_WIDTH), rows_spec(HEAD_WIDTH)]
        + [const_spec(w) for w in weights],
        out_specs=[rows_spec(width), rows_spec(width), rows_spec(hidden), rows_spec(hidden)],
        out_shape=[out(width, BF), out(width, F32), out(hidden, BF), out(hidden, BF)],
        compiler_params=params(56),
        cost_estimate=cost(groups * seqs * rows, width * (HEAD_WIDTH + 2 * hidden) * 3, 1 << 20),
        name="time_mlp",
    )(x, attended, gate, *weights)


def accumulate(first, pairs, sources):
    @pl.when(first)
    def _():
        for (ref, _), source in zip(pairs, sources):
            ref[...] = source[...]

    for ref, value in pairs:
        ref[...] += value


def time_mlp_back_kernel(
    g_ref, mid_ref, act_ref, slope_ref, att_ref, gate_ref,
    wo, wu, wd, gain_ref, heads, swapped,
    in_down, in_up, in_out, in_bias, in_vec,
    gmid_ref, gatt_ref, logit_ref, a_down, a_up, a_out, a_bias, a_vec,
):
    first = pl.program_id(0) == 0
    gain = gain_ref[...]
    grad_last = flat(g_ref)
    act = flat(act_ref)
    grad_up = (nt(grad_last, wd[...]) * flat(slope_ref).astype(F32)).astype(BF)
    unit, scale = rms(flat(mid_ref))
    normed = (unit * gain).astype(BF)
    grad_normed = nn(grad_up, wu[...])
    gradient = grad_last.astype(F32)
    grad_middle = gradient + rms_back(unit, scale, gain, grad_normed)
    grad_branch = grad_middle.astype(BF)
    att = flat(att_ref)
    gate = flat(gate_ref).astype(F32)
    gated = (att.astype(F32) * gate).astype(BF)
    grad_att, grad_logit, delta = branch_back(
        grad_branch, wo[...], att, gate, heads[...], swapped[...]
    )
    low, high, picks, _ = lane_masks()
    lead = gatt_ref.shape[:-1]
    for pair in range(PAIRS):
        at = slice(pair * LANES, (pair + 1) * LANES)
        both = grads_with_delta(grad_att[:, at], delta[:, at], low, high, picks)
        for slot in range(2):
            where = 2 * pair + slot
            gatt_ref[..., where * LANES : (where + 1) * LANES] = both[slot].reshape(lead + (LANES,))
    gmid_ref[...] = grad_middle.reshape(gmid_ref.shape)
    logit_ref[...] = grad_logit.reshape(logit_ref.shape)
    vec = jnp.concatenate([col_sum(gradient), col_sum(grad_normed * unit)], axis=0)
    accumulate(
        first,
        (
            (a_down, tn(grad_last, act)),
            (a_up, tn(normed, grad_up)),
            (a_out, tn(grad_branch, gated)),
            (a_bias, col_sum(grad_up)),
            (a_vec, vec),
        ),
        (in_down, in_up, in_out, in_bias, in_vec),
    )


def time_mlp_back(grad, middle, act, slope, attended, gate, weights, sums, starts):
    groups, seqs, rows, width = grad.shape
    hidden = act.shape[-1]
    sb = source_block(groups, seqs, rows, 512)

    def rows_spec(lanes):
        return pl.BlockSpec((sb, seqs, rows, lanes), lambda i: (i, 0, 0, 0))

    def out(lanes, dtype):
        return jax.ShapeDtypeStruct((groups, seqs, rows, lanes), dtype)

    consts = tuple(weights) + tuple(sums) + tuple(starts)
    return pl.pallas_call(
        time_mlp_back_kernel,
        grid=(groups // sb,),
        in_specs=[rows_spec(width), rows_spec(width), rows_spec(hidden), rows_spec(hidden)]
        + [rows_spec(HEAD_WIDTH)] * 2
        + [const_spec(w) for w in consts],
        out_specs=[rows_spec(width), rows_spec(2 * HEAD_WIDTH), rows_spec(LANES)]
        + [const_spec(s) for s in starts],
        out_shape=[out(width, F32), out(2 * HEAD_WIDTH, BF), out(LANES, BF)]
        + [jax.ShapeDtypeStruct(s.shape, s.dtype) for s in starts],
        compiler_params=params(60),
        cost_estimate=cost(groups * seqs * rows, width * (HEAD_WIDTH + 2 * hidden) * 5, 1 << 20),
        name="time_mlp_back",
    )(grad, middle, act, slope, attended, gate, *consts)


def time_attend_back_kernel(
    len_ref, keep_ref, k_ref, v_ref, gatt_ref, cos_ref, sin_ref, swap_ref, dq_ref, dk_ref, dv_ref
):
    low, high, picks, inner = lane_masks()
    keys, values = flat(k_ref), flat(v_ref)
    rows = keys.shape[0]
    _, extra_k = time_extra(rows, len_ref[pl.program_id(0)], inner)
    kept, grads = flat(keep_ref), flat(gatt_ref)
    grad_query, grad_key, grad_value = pair_back(
        (kept[:, :LANES], kept[:, LANES:]),
        keys,
        values,
        (grads[:, :LANES], grads[:, LANES:]),
        low,
        high,
        picks,
        extra_k,
        math.gcd(rows, BLOCK_Q),
    )
    cos, sin, swap_t = flat(cos_ref), flat(sin_ref), swap_ref[...]
    dq_ref[...] = unrotate(grad_query, cos, sin, swap_t).astype(BF).reshape(dq_ref.shape)
    dk_ref[...] = unrotate(grad_key, cos, sin, swap_t).astype(BF).reshape(dk_ref.shape)
    dv_ref[...] = grad_value.astype(BF).reshape(dv_ref.shape)


def time_attend_back(kept, qkv, grad_aug, lens, cos, sin, swap_t):
    groups, seqs, rows, _ = qkv.shape

    def spec(lanes, first):
        return pl.BlockSpec((groups, 1, rows, lanes), lambda s, p, *_: (0, s, 0, first + p))

    def fixed(array):
        zeros = (0,) * array.ndim
        return pl.BlockSpec(array.shape, lambda s, p, *_: zeros, pipeline_mode=pl.Buffered(1))

    out = jax.ShapeDtypeStruct((groups, seqs, rows, HEAD_WIDTH), BF)
    return pl.pallas_call(
        time_attend_back_kernel,
        grid_spec=pltpu.PrefetchScalarGridSpec(
            num_scalar_prefetch=1,
            grid=(seqs, PAIRS),
            in_specs=[
                spec(2 * LANES, 0),
                spec(LANES, PAIRS),
                spec(LANES, 2 * PAIRS),
                spec(2 * LANES, 0),
                fixed(cos),
                fixed(sin),
                fixed(swap_t),
            ],
            out_specs=[spec(LANES, 0)] * 3,
        ),
        out_shape=[out] * 3,
        compiler_params=params(60),
        cost_estimate=cost(groups * seqs * rows, groups * rows * HEADS * 5 * 256 * 3 // 2, 1 << 20),
        name="time_attend_back",
    )(lens, kept, qkv, qkv, grad_aug, cos, sin, swap_t)


def time_project_back_kernel(
    x_ref, dq_ref, dk_ref, dv_ref, logit_ref, gmid_ref,
    wq, wg, gain_ref, in_qkv, in_gate, in_vec, in_bias,
    gx_ref, a_qkv, a_gate, a_vec, a_bias,
):
    gain = gain_ref[...]
    unit, scale = rms(flat(x_ref).astype(F32))
    normed = (unit * gain).astype(BF)
    packed = jnp.concatenate([flat(dq_ref), flat(dk_ref), flat(dv_ref)], axis=1)
    logit = flat(logit_ref)
    grad_normed = nn(packed, wq[...]) + nn(logit, wg[...])
    grad_x = flat(gmid_ref) + rms_back(unit, scale, gain, grad_normed)
    gx_ref[...] = grad_x.astype(BF).reshape(gx_ref.shape)
    accumulate(
        pl.program_id(0) == 0,
        (
            (a_qkv, tn(normed, packed)),
            (a_gate, tn(logit, normed)),
            (a_vec, col_sum(grad_normed * unit)),
            (a_bias, col_sum(logit)),
        ),
        (in_qkv, in_gate, in_vec, in_bias),
    )


def time_project_back(x, grads, logit, grad_middle, weights, starts):
    groups, seqs, rows, width = x.shape
    sb = source_block(groups, seqs, rows, 512)

    def rows_spec(lanes):
        return pl.BlockSpec((sb, seqs, rows, lanes), lambda i: (i, 0, 0, 0))

    consts = tuple(weights) + tuple(starts)
    return pl.pallas_call(
        time_project_back_kernel,
        grid=(groups // sb,),
        in_specs=[rows_spec(width)]
        + [rows_spec(HEAD_WIDTH)] * 3
        + [rows_spec(LANES), rows_spec(width)]
        + [const_spec(w) for w in consts],
        out_specs=[rows_spec(width)] + [const_spec(s) for s in starts],
        out_shape=[jax.ShapeDtypeStruct((groups, seqs, rows, width), BF)]
        + [jax.ShapeDtypeStruct(s.shape, s.dtype) for s in starts],
        compiler_params=params(60),
        cost_estimate=cost(groups * seqs * rows, width * 6 * HEAD_WIDTH * 5 // 2, 1 << 20),
        name="time_project_back",
    )(x, *grads, logit, grad_middle, *consts)


def band_kernel(
    h_ref, g_ref, perm_ref, back_ref, cq, sq, ck, sk, exq_ref, exk_ref, swap_ref, heads, swapped,
    wq, wo, wu, wd, wg, gain0_ref, gain1_ref, bu, bd, bg,
    in_qkv, in_up, in_down, in_out, in_gate, in_bias, in_vec, in_gbias, *refs,
):
    out_ref, gh_ref, a_qkv, a_up, a_down, a_out, a_gate, a_bias, a_vec, a_gbias, w_ext = refs[-11:]
    first = pl.program_id(0) == 0

    @pl.when(first)
    def _():
        extend_weights(wq, wg, w_ext)

    gain0, gain1 = gain0_ref[...], gain1_ref[...]
    low, high, picks, _ = lane_masks()
    hidden = flat(h_ref).astype(F32)
    unit0, scale0 = rms(hidden)
    normed0 = (unit0 * gain0).astype(BF)
    queries, keys, value, gate = project(
        normed0, w_ext, (cq[...], sq[...], ck[...], sk[...]), bg[...]
    )
    extra_q, extra_k = exq_ref[...], exk_ref[...]
    ones = jnp.ones((value.shape[0], LANES), BF)
    parts, kept, values = [], [], []
    for pair in range(PAIRS):
        value_pair = value[:, pair * LANES : (pair + 1) * LANES]
        total, both = None, []
        for slot in range(2):
            own, other = (low, high) if slot == 0 else (high, low)
            out, query_own, terms = attend_block(
                queries[pair],
                keys[pair] * own + extra_k * other,
                jnp.concatenate([value_pair * own, ones], axis=1),
                extra_q,
                low,
                high,
                slot,
            )
            both.append(keep_query(query_own, terms, extra_q, picks, other))
            total = out if total is None else total + out
        parts.append(total.astype(BF))
        kept.append(both)
        values.append(value_pair)
    attended = jnp.concatenate(parts, axis=1)
    gated = (attended.astype(F32) * gate).astype(BF)
    middle = hidden + nn(gated, wo[...])
    result, normed1, unit1, scale1, act, slope = feed_forward(
        middle, gain1, wu[...], bu[...], wd[...], bd[...]
    )
    out_ref[...] = nn(back_ref[...], result.astype(BF)).astype(BF).reshape(out_ref.shape)

    gradient = nn(perm_ref[...], flat(g_ref))
    grad_last = gradient.astype(BF)
    grad_up = (nt(grad_last, wd[...]) * slope).astype(BF)
    grad_normed1 = nn(grad_up, wu[...])
    grad_middle = gradient + rms_back(unit1, scale1, gain1, grad_normed1)
    grad_branch = grad_middle.astype(BF)
    grad_att, grad_logit, delta = branch_back(
        grad_branch, wo[...], attended, gate, heads[...], swapped[...]
    )
    swap_t = swap_ref[...]
    grads_q, grads_k, grads_v = [], [], []
    for pair in range(PAIRS):
        at = slice(pair * LANES, (pair + 1) * LANES)
        both = grads_with_delta(grad_att[:, at], delta[:, at], low, high, picks)
        grad_query, grad_key, grad_value = pair_back(
            kept[pair], keys[pair], values[pair], both, low, high, picks, extra_k, extra_k.shape[0]
        )
        grads_q.append(unrotate(grad_query, ck[...], sk[...], swap_t).astype(BF))
        grads_k.append(unrotate(grad_key, ck[...], sk[...], swap_t).astype(BF))
        grads_v.append(grad_value.astype(BF))
    packed = jnp.concatenate(grads_q + grads_k + grads_v, axis=1)
    width = HEAD_WIDTH
    grad_normed0 = (
        nn(packed[:, : 2 * width], w_ext[: 2 * width])
        + nn(packed[:, 2 * width :], w_ext[4 * width : 5 * width])
        + nn(grad_logit, wg[...])
    )
    grad_hidden = grad_middle + rms_back(unit0, scale0, gain0, grad_normed0)
    gh_ref[...] = grad_hidden.astype(BF).reshape(gh_ref.shape)
    vec = jnp.concatenate(
        [col_sum(gradient), col_sum(grad_normed1 * unit1), col_sum(grad_normed0 * unit0)], axis=0
    )
    accumulate(
        first,
        (
            (a_qkv, tn(normed0, packed)),
            (a_up, tn(normed1, grad_up)),
            (a_down, tn(grad_last, act)),
            (a_out, tn(grad_branch, gated)),
            (a_gate, tn(grad_logit, normed0)),
            (a_bias, col_sum(grad_up)),
            (a_vec, vec),
            (a_gbias, col_sum(grad_logit)),
        ),
        (in_qkv, in_up, in_down, in_out, in_gate, in_bias, in_vec, in_gbias),
    )


def band_layer(hidden, grad_out, clip, consts, starts, final):
    bands, rows, width = hidden.shape
    consts = tuple(consts) + tuple(starts)
    seq_spec = pl.BlockSpec((bands, TILE_FRAMES, width), lambda i: (0, i, 0))
    frame_spec = pl.BlockSpec((TILE_FRAMES, 1, bands, width), lambda i: (i, clip, 0, 0))
    return pl.pallas_call(
        band_kernel,
        grid=(rows // TILE_FRAMES,),
        in_specs=[seq_spec, frame_spec]
        + [const_spec(c) for c in consts]
        + [pl.BlockSpec(memory_space=pl.ANY)] * len(final),
        out_specs=[frame_spec, seq_spec] + [const_spec(s) for s in starts],
        out_shape=[
            jax.ShapeDtypeStruct(grad_out.shape, BF),
            jax.ShapeDtypeStruct((bands, rows, width), BF),
        ]
        + [jax.ShapeDtypeStruct(s.shape, s.dtype) for s in starts],
        scratch_shapes=[pltpu.VMEM((6 * HEAD_WIDTH, width), BF)],
        input_output_aliases={2 + len(consts): 0} if final else {},
        compiler_params=params(62),
        cost_estimate=cost(bands * rows, width * (4 * HEAD_WIDTH + 2 * starts[1].shape[1]) * 13, 1 << 20),
        name="band_layer",
    )(hidden, grad_out, *consts, *final)


def flip_kernel(*refs):
    half = len(refs) // 2
    for source, target in zip(refs[:half], refs[half:]):
        target[...] = source[...].T.astype(BF)


def flip(arrays):
    return pl.pallas_call(
        flip_kernel,
        out_shape=[jax.ShapeDtypeStruct(a.shape[::-1], BF) for a in arrays],
        compiler_params=params(56),
        cost_estimate=cost(4096, 256, 1 << 20),
        name="flip_sums",
    )(*arrays)


def rotary_tables(positions):
    steps = np.exp(np.arange(HALF, dtype=np.float32) * np.float32(-math.log(10000.0) / HALF))
    angles = positions.astype(np.float32)[:, None] * steps[None, :]
    cos = np.tile(np.cos(angles), (1, LANES // HALF)).astype(np.float32)
    sin = np.tile(np.sin(angles), (1, LANES // HALF)).astype(np.float32)
    scale = np.float32(QUERY_SCALE)
    return cos * scale, sin * scale, cos, sin


def tile_permutation(bands):
    rows = bands * TILE_FRAMES
    row = np.arange(rows)
    source = (row % TILE_FRAMES) * bands + row // TILE_FRAMES
    return (source[:, None] == row[None, :]).astype(BF)


def head_sums():
    lane = np.arange(HEAD_WIDTH)
    heads = (lane[:, None] // HEAD_DIM == np.arange(LANES)[None, :]).astype(BF)
    swapped = (lane[:, None] // HEAD_DIM == (lane[None, :] // HEAD_DIM) ^ 1).astype(BF)
    return heads, swapped


def swap_matrix():
    lane = np.arange(LANES)
    same = lane[:, None] // HEAD_DIM == lane[None, :] // HEAD_DIM
    i, j = lane[:, None] % HEAD_DIM, lane[None, :] % HEAD_DIM
    forward = np.where(j == i + HALF, 1.0, 0.0) + np.where(j == i - HALF, -1.0, 0.0)
    return np.where(same, forward, 0.0).T.astype(BF)


def band_extras(bands):
    rows = bands * TILE_FRAMES
    frame = np.arange(rows) % TILE_FRAMES
    inner = np.arange(LANES) % HEAD_DIM
    mine = inner[None, :] == 4 + frame[:, None]
    slot = (inner >= 4) & (inner < 4 + TILE_FRAMES)
    extra_k = np.where(slot[None, :] & ~mine, NEGATIVE, 0.0)
    extra_k = np.where(inner[None, :] < 3, 1.0, extra_k)
    return mine.astype(BF), extra_k.astype(BF)


def xor_pairs(count, bit):
    return [(i, i ^ bit) for i in range(count)]


def gather_all(block):
    steps = []
    for axis in ("fsdp", "dp"):
        size = lax.axis_size(axis)
        bits = [1 << k for k in range(1, size.bit_length() - 1)] + [1]
        steps += [(axis, bit) for bit in bits if bit < size]
    tensor, order = block, []
    for axis, bit in steps:
        other = lax.ppermute(tensor, axis, xor_pairs(lax.axis_size(axis), bit))
        mine_first = (lax.axis_index(axis) // bit) % 2 == 0
        tensor = jnp.stack(
            [jnp.where(mine_first, tensor, other), jnp.where(mine_first, other, tensor)]
        )
        order.insert(0, (axis, bit))
    wanted = sorted(range(len(order)), key=lambda k: (order[k][0] != "dp", -order[k][1]))
    rank = len(order)
    tensor = tensor.transpose(*wanted, rank, rank + 1)
    return tensor.reshape((lax.axis_size("dp"), lax.axis_size("fsdp")) + block.shape)


def after(tensors, done):
    return lax.optimization_barrier((tensors, done))[0]


def pick(tensor, index):
    return lax.dynamic_index_in_dim(tensor, index, 0, keepdims=False)


def reduce_all(blocks):
    dp, groups = lax.axis_size("dp"), lax.axis_size("fsdp")
    core, chip = lax.axis_index("dp") % 2, lax.axis_index("dp") // 2
    me = lax.axis_index("fsdp")
    tensor = blocks.astype(BF).reshape((dp // 2, 2, groups) + blocks.shape[1:]).swapaxes(0, 1)

    def shed(tensor, place, axis, size, unit):
        total = pick(tensor, place).astype(F32)
        for step in range(1, size):
            moved = lax.ppermute(
                pick(tensor, place ^ step), axis, xor_pairs(lax.axis_size(axis), step * unit)
            )
            total = total + moved.astype(F32)
        return total

    tensor = shed(tensor, core, "dp", 2, 1).astype(BF)
    tensor = shed(tensor, chip, "dp", dp // 2, 2).astype(BF)
    return shed(tensor, me, "fsdp", groups, 1)


def sums_for_all(matrices, rows, bias=None, gate_bias=None):
    dp, groups = lax.axis_size("dp"), lax.axis_size("fsdp")
    devices, width = dp * groups, rows.shape[1]
    parts = [m.reshape(devices, -1, width) for m in matrices]
    count, shard = rows.shape[0], width // groups
    small = rows.reshape(count, groups, shard).swapaxes(0, 1).reshape(1, groups, count * shard)
    small = [jnp.broadcast_to(small, (dp, groups, count * shard)).reshape(devices, -1)]
    if bias is not None:
        small.append(bias.reshape(devices, -1))
    if gate_bias is not None:
        small.append(jnp.broadcast_to(gate_bias, (devices, gate_bias.shape[-1])))
    small = jnp.concatenate(small, axis=1).astype(BF)
    filled = sum(p.shape[1] for p in parts)
    total = -(-(filled * width + small.shape[1]) // (16 * width)) * 16
    small = jnp.pad(small, ((0, 0), (0, (total - filled) * width - small.shape[1])))
    return jnp.concatenate(parts + [small.reshape(devices, -1, width)], axis=1)


def split_sums(summed, sizes, width, lengths):
    parts, start = [], 0
    for size in sizes:
        parts.append(summed[start : start + size])
        start += size
    flat_part, start, vectors = summed[start:].reshape(-1), 0, []
    for length in lengths:
        vectors.append(flat_part[start : start + length])
        start += length
    return parts, vectors


def on_device(
    frames_in, lengths, w_qkv, w_out, w_up, b_up, w_down, gains, b_down, w_gate, b_gate, grad_out
):
    rows, clips, bands, width = frames_in.shape
    dp, groups = lax.axis_size("dp"), lax.axis_size("fsdp")
    position = lax.axis_index("fsdp")
    everyone = ("dp", "fsdp")
    devices, shard = dp * groups, width // groups
    hidden = w_up.shape[2] * devices
    seq_count = clips * bands // groups
    by_clip = bands % groups == 0
    chunk_count = clips if by_clip else 1
    chunk_seqs = seq_count // chunk_count

    wq_t, wu_t = w_qkv.swapaxes(1, 2), w_up.swapaxes(1, 2)
    sizes = [wq_t.shape[1], wu_t.shape[1], w_down.shape[1], w_out.shape[1]]
    small = jnp.concatenate(
        [gains.reshape(-1), b_down.reshape(-1), w_gate.reshape(-1), b_up.reshape(-1)]
    )
    total = -(-(sizes[0] * width + small.shape[0]) // (16 * width)) * 16
    small_rows = total - sizes[0]
    small = jnp.pad(small, (0, small_rows * width - small.shape[0])).reshape(-1, width)
    first = gather_all(jnp.concatenate([wq_t[0], small], axis=0))
    wq = first[:, :, : sizes[0]].reshape(-1, width)
    small = first[:, :, sizes[0] :].reshape(dp, groups, -1)
    vector_count = 4 + 2 + 2 * HEADS
    vectors = small[0, :, : vector_count * shard].reshape(groups, vector_count, shard)
    vectors = vectors.swapaxes(0, 1).reshape(vector_count, width)
    gains_full = vectors[:4].reshape(2, 2, 1, width).astype(F32)
    b_down_full = vectors[4:6].reshape(2, 1, width).astype(F32)
    gates_full = jnp.pad(
        vectors[6:].reshape(2, HEADS, width), ((0, 0), (0, LANES - HEADS), (0, 0))
    )
    b_up_full = small[:, :, vector_count * shard :][:, :, : 2 * sizes[1]]
    b_up_full = b_up_full.reshape(devices, 2, -1).swapaxes(0, 1).reshape(2, 1, -1).astype(F32)
    b_gate_full = jnp.repeat(b_gate.astype(F32), HEAD_DIM, axis=1)[:, None]

    def unpack(gathered, parts):
        cut, found = 0, []
        for size in parts:
            found.append(gathered[:, cut : cut + size].reshape(-1, width))
            cut += size
        return found

    rest = jnp.concatenate([wu_t[0], w_down[0], w_out[0]], axis=0)
    second = jnp.concatenate([wq_t[1], wu_t[1], w_down[1], w_out[1]], axis=0)

    perm = tile_permutation(bands)
    heads, swapped = head_sums()
    swap_t = swap_matrix()
    frame_tables = rotary_tables(np.arange(groups * rows))
    frame_tables = tuple(t.reshape(groups, rows, LANES) for t in frame_tables)
    band_tables = rotary_tables(np.arange(bands * TILE_FRAMES) // TILE_FRAMES)
    extra_q, extra_k = band_extras(bands)

    def exchange(tensor):
        return lax.all_to_all(tensor, "fsdp", split_axis=0, concat_axis=0, tiled=True)

    clip_seqs = [to_sequences(frames_in, clip, perm) for clip in range(clips)]
    if by_clip:
        chunks = [seqs.reshape(groups, chunk_seqs, rows, width) for seqs in clip_seqs]
    else:
        chunks = [jnp.concatenate(clip_seqs).reshape(groups, chunk_seqs, rows, width)]
    saved, returned = [], []
    arrived = [exchange(chunk) for chunk in chunks]
    rest = lax.all_gather(rest, everyone, axis=0)
    arrived[0], wq, second = lax.optimization_barrier((arrived[0], wq, second))
    second = lax.all_gather(second, everyone, axis=0)
    wu, wd, wo = unpack(rest, sizes[1:])
    mlp_weights = (wo, wu, wd, gains_full[0, 1], b_up_full[0], b_down_full[0])
    for chunk in range(chunk_count):
        x = arrived[chunk]
        if by_clip:
            lens = jnp.broadcast_to(lengths[chunk], (chunk_seqs,))
        else:
            lens = lengths[(position * chunk_seqs + jnp.arange(chunk_seqs)) // bands]
        qkv, gate = time_project(
            x, frame_tables, wq, gates_full[0], gains_full[0, 0], b_gate_full[0]
        )
        attended, kept = time_attend(qkv, lens)
        h1, middle, act, slope = time_mlp(x, attended, gate, mlp_weights)
        saved.append((x, lens, qkv, gate, attended, kept, middle, act, slope))
        returned.append(exchange(h1))
    if by_clip:
        band_inputs = [h.reshape(bands, rows, width) for h in returned]
    else:
        whole = returned[0].reshape(clips, bands, rows, width)
        band_inputs = [whole[clip] for clip in range(clips)]

    wq1, wu1, wd1, wo1 = unpack(second, sizes)
    consts = (
        (perm, perm.T) + band_tables + (extra_q, extra_k, swap_t, heads, swapped)
        + (wq1, wo1, wu1, wd1, gates_full[1], gains_full[1, 0], gains_full[1, 1])
        + (b_up_full[1], b_down_full[1], b_gate_full[1])
    )
    sums = tuple(
        jnp.zeros(shape, F32)
        for shape in (
            (width, 3 * HEAD_WIDTH), (width, hidden), (width, hidden), (width, HEAD_WIDTH),
            (LANES, width), (1, hidden), (3, width), (1, LANES),
        )
    )
    final = []
    grads = []
    for clip in range(clips):
        done, grad_hidden, *sums = band_layer(
            band_inputs[clip], grad_out, clip, consts, sums, final
        )
        final = [done]
        grads.append(grad_hidden)
    b_qkv, b_up_, b_down_, b_out, b_gate_, b_bias, b_vec, b_gbias = sums
    band_rows = jnp.concatenate([b_vec[2:3], b_vec[1:2], b_vec[0:1], b_gate_[:HEADS]])
    band_sums = reduce_all(
        sums_for_all(flip([b_qkv, b_up_, b_down_, b_out]), band_rows, b_bias, b_gbias[:, :HEADS])
    )

    if by_clip:
        grads = [g.reshape(groups, chunk_seqs, rows, width) for g in grads]
    else:
        grads = [jnp.concatenate(grads).reshape(groups, chunk_seqs, rows, width)]
    grads = [exchange(g) for g in grads]
    sums = tuple(
        jnp.zeros(shape, F32)
        for shape in ((width, hidden), (width, hidden), (width, HEAD_WIDTH), (1, hidden), (2, width))
    )
    sums_back = tuple(
        jnp.zeros(shape, F32)
        for shape in ((width, 3 * HEAD_WIDTH), (LANES, width), (1, width), (1, LANES))
    )
    sequences, mlp_sums, previous = [], None, None

    def finish(chunk, packed_grads, logit, grad_middle, sums_back):
        grad_x, *sums_back = time_project_back(
            saved[chunk][0], packed_grads, logit, grad_middle,
            (wq, gates_full[0], gains_full[0, 0]), sums_back,
        )
        sequences.append(exchange(grad_x).reshape(-1, bands, rows, width))
        return sums_back

    for chunk in range(chunk_count):
        x, lens, qkv, gate, attended, kept, middle, act, slope = saved[chunk]
        grad_middle, grad_aug, logit, *sums = time_mlp_back(
            grads[chunk], middle, act, slope, attended, gate,
            (wo, wu, wd, gains_full[0, 1]), (heads, swapped), sums,
        )
        if chunk == chunk_count - 1:
            t_down, t_up, t_out, t_bias, t_vec = sums
            flipped = sums_for_all(
                flip([t_up, t_down, t_out]), jnp.concatenate([t_vec[1:2], t_vec[0:1]]), t_bias
            )
            flipped, grad_aug, band_sums = lax.optimization_barrier((flipped, grad_aug, band_sums))
            mlp_sums = reduce_all(flipped)
        if previous is not None:
            sums_back = finish(*previous, sums_back)
        packed_grads = time_attend_back(
            kept, qkv, grad_aug, lens, frame_tables[2], frame_tables[3], swap_t
        )
        previous = (chunk, packed_grads, logit, grad_middle)
    packed_grads, mlp_sums = lax.optimization_barrier((previous[1], mlp_sums))
    sums = finish(previous[0], packed_grads, *previous[2:], sums_back)
    t_qkv, t_gate, t_vec0, t_gbias = sums
    qkv_sums = reduce_all(
        sums_for_all(
            flip([t_qkv]), jnp.concatenate([t_vec0, t_gate[:HEADS]]), None, t_gbias[:, :HEADS]
        )
    )
    sequences = [s[k] for s in sequences for k in range(s.shape[0])]
    grad_input = []
    for clip in range(clips):
        grad_input = [to_frames(sequences[clip], clip, clips, perm.T, grad_input)]

    gate_len = HEADS * shard
    (bq, bu, bd, bo), (bg0, bg1, bbd, bgate, bbu, bgb) = split_sums(
        band_sums, sizes, width, (shard, shard, shard, gate_len, sizes[1], HEADS)
    )
    (tu, td, to), (tg1, tbd, tbu) = split_sums(mlp_sums, sizes[1:], width, (shard, shard, sizes[1]))
    (tq,), (tg0, tgate, tgb) = split_sums(qkv_sums, sizes[:1], width, (shard, gate_len, HEADS))
    return (
        final[0],
        grad_input[0],
        jnp.stack([tq.T, bq.T]),
        jnp.stack([to, bo]),
        jnp.stack([tu.T, bu.T]),
        jnp.stack([tbu, bbu]),
        jnp.stack([td, bd]),
        jnp.stack([jnp.stack([tg0, tg1]), jnp.stack([bg0, bg1])]),
        jnp.stack([tbd, bbd]),
        jnp.stack([tgate, bgate]).reshape(2, HEADS, shard),
        jnp.stack([tgb, bgb]),
    )


def solution(mesh):
    everyone = ("dp", "fsdp")
    rows = P("fsdp", "dp", None, None)
    last, middle = P(None, None, everyone), P(None, everyone, None)
    return jax.shard_map(
        on_device,
        mesh=mesh,
        in_specs=(
            rows, P("dp"), last, middle, last, P(None, everyone), middle,
            P(None, None, "fsdp"), P(None, "fsdp"), P(None, None, "fsdp"), P(), rows,
        ),
        out_specs=(
            rows, rows, last, middle, last, P(None, everyone), middle,
            P(None, None, "fsdp"), P(None, "fsdp"), P(None, None, "fsdp"), P(),
        ),
        check_vma=False,
    )
```

```python
from functools import partial
import math

import jax
import jax.numpy as jnp
import numpy as np
from jax import lax
from jax.experimental import pallas as pl
from jax.experimental.pallas import tpu as pltpu
from jax.sharding import PartitionSpec as P

HEADS = 8
HEAD_DIM = 64
HALF = HEAD_DIM // 2
HEAD_WIDTH = HEADS * HEAD_DIM
PAIRS = HEADS // 2
LANES = 2 * HEAD_DIM
TILE_FRAMES = 16
EPSILON = 1e-06
NEGATIVE = -1e30
LOG2E = 1.0 / math.log(2.0)
LN2 = math.log(2.0)
QUERY_SCALE = HEAD_DIM**-0.5 * LOG2E
BLOCK_Q = 128
BLOCK_Q_BACK = 256
BAND_FRAMES = 32
ROW_TARGET = 512
MOVE_FRAMES = 32

BF = jnp.bfloat16
F32 = jnp.float32


def nn(a, b):
    return jnp.dot(a, b, preferred_element_type=F32)


def nt(a, b):
    return lax.dot_general(a, b, (((1,), (1,)), ((), ())), preferred_element_type=F32)


def tn(a, b):
    return lax.dot_general(a, b, (((0,), (0,)), ((), ())), preferred_element_type=F32)


def rms(hidden):
    scale = lax.rsqrt(jnp.mean(hidden * hidden, axis=-1, keepdims=True) + EPSILON)
    return hidden * scale, scale


def rms_back(unit, scale, gain, grad):
    weighted = grad * gain
    inner = jnp.mean(weighted * unit, axis=-1, keepdims=True)
    return scale * (weighted - unit * inner)


def gelu_pair(up):
    cdf = 0.5 + 0.5 * lax.erf(up * math.sqrt(0.5))
    bell = jnp.exp2((-0.5 * LOG2E) * (up * up))
    return up * cdf, cdf + (up * bell) * (1.0 / math.sqrt(2.0 * math.pi))


def project(normed, w_ext, tables, b_gate):
    cos_q, sin_q, cos_k, sin_k = tables
    width = HEAD_WIDTH
    plain = nt(normed, w_ext[: 2 * width])
    swapped = nt(normed, w_ext[2 * width : 4 * width])
    value = nt(normed, w_ext[4 * width : 5 * width]).astype(BF)
    gate = jax.nn.sigmoid(nt(normed, w_ext[5 * width :]) + b_gate)
    queries, keys = [], []
    for pair in range(2 * PAIRS):
        at = slice(pair * LANES, (pair + 1) * LANES)
        cos, sin = (cos_q, sin_q) if pair < PAIRS else (cos_k, sin_k)
        turned = (plain[:, at] * cos + swapped[:, at] * sin).astype(BF)
        (queries if pair < PAIRS else keys).append(turned)
    return queries, keys, value, gate


def attend_pair(query, key_augs, value_ones, extra_q, low, high):
    outs, inverses, kept = [], [], []
    for slot in range(2):
        own, other = (low, high) if slot == 0 else (high, low)
        scores = nt(query * own + extra_q * other, key_augs[slot])
        probs = jnp.exp2(scores - jnp.max(scores, axis=-1, keepdims=True)).astype(BF)
        mixed = nn(probs, value_ones[slot])
        inverse = 1.0 / mixed[:, LANES:]
        outs.append(mixed[:, :LANES] * inverse)
        inverses.append(inverse)
        kept.append(probs)
    is_low = lax.broadcasted_iota(jnp.int32, (1, LANES), 1) < HEAD_DIM
    return outs[0] + outs[1], jnp.where(is_low, *inverses), kept


def pair_operands(keys, values, extra_k, low, high):
    ones = jnp.ones(values.shape, BF)
    key_augs = (keys * low + extra_k * high, keys * high + extra_k * low)
    value_ones = (
        jnp.concatenate([values * low, ones], axis=1),
        jnp.concatenate([values * high, ones], axis=1),
    )
    return key_augs, value_ones


def unrotate(grad, cos, sin, swap_t):
    return grad * cos + nn((grad * sin).astype(BF), swap_t)


def lane_masks():
    lane = lax.broadcasted_iota(jnp.int32, (1, LANES), 1)
    inner = lane % HEAD_DIM
    low = jnp.where(lane < HEAD_DIM, 1.0, 0.0).astype(BF)
    high = jnp.where(lane < HEAD_DIM, 0.0, 1.0).astype(BF)
    picks = tuple(jnp.where(inner == k, 1.0, 0.0).astype(BF) for k in range(2))
    return low, high, picks, inner


def pair_back(probs_of, queries, keys, values, grads, low, high, picks, block_q):
    rows = queries.shape[0]
    query_t = queries.T
    grad_t = (grads[0] * low + grads[1] * high).T
    is_low = lax.broadcasted_iota(jnp.int32, (1, LANES), 1) < HEAD_DIM
    two = picks[0] + picks[1]
    query_parts, key_sums, value_sums = [], [], []
    for slot in range(2):
        own, other = (low, high) if slot == 0 else (high, low)
        value_aug = values * own + two * other
        head = slice(slot * HEAD_DIM, (slot + 1) * HEAD_DIM)
        key_sum = value_sum = None
        parts = []
        for start in range(0, rows, block_q):
            at = slice(start, start + block_q)
            probs = probs_of(slot, at)
            grad_scores = (probs.astype(F32) * nt(grads[slot][at], value_aug)).astype(BF)
            grad_value = nn(grad_t[head, at], probs)
            grad_key = nn(query_t[head, at], grad_scores)
            parts.append(nn(grad_scores, keys))
            key_sum = grad_key if key_sum is None else key_sum + grad_key
            value_sum = grad_value if value_sum is None else value_sum + grad_value
        query_parts.append(parts)
        key_sums.append(key_sum)
        value_sums.append(value_sum)
    blocks = [jnp.where(is_low, *both) for both in zip(*query_parts)]
    grad_query = jnp.concatenate(blocks, axis=0) if len(blocks) > 1 else blocks[0]
    grad_key = jnp.concatenate(key_sums, axis=0).T * LN2
    return grad_query * HEAD_DIM**-0.5, grad_key, jnp.concatenate(value_sums, axis=0).T


def feed_forward(middle, gain, w_up, b_up, w_down, b_down):
    unit, scale = rms(middle)
    normed = (unit * gain).astype(BF)
    act, slope = gelu_pair(nt(normed, w_up) + b_up)
    act, slope = act.astype(BF), slope.astype(BF)
    return middle + (nn(act, w_down) + b_down), normed, unit, scale, act, slope


def branch_back(grad_branch, w_out, attended, gate, inverse, sum_heads, sum_swapped):
    grad_gated = nt(grad_branch, w_out)
    att = attended.astype(F32)
    grad_att = (grad_gated * (gate * inverse)).astype(BF)
    logit_terms = (grad_gated * att * (gate * (1.0 - gate))).astype(BF)
    grad_logit = nn(logit_terms, sum_heads).astype(BF)
    delta = nn((grad_att.astype(F32) * att).astype(BF), sum_swapped)
    return grad_att, grad_logit, delta


def grads_with_delta(grad_att, delta, low, high, picks):
    hi = delta.astype(BF)
    mid = (delta - hi.astype(F32)).astype(BF)
    extra = -(hi * picks[0] + mid * picks[1])
    return grad_att * low + extra * high, grad_att * high + extra * low


def col_sum(values):
    return jnp.sum(values.astype(F32), axis=0, keepdims=True)


def flat(ref):
    value = ref[...]
    return value.reshape(-1, value.shape[-1])


def gather_kernel(perm_ref, x_ref, o_ref):
    for start in range(0, x_ref.shape[0], TILE_FRAMES):
        span = slice(start, start + TILE_FRAMES)
        moved = nn(perm_ref[...], flat(x_ref.at[span])).astype(BF)
        o_ref[:, span] = moved.reshape((-1, TILE_FRAMES) + moved.shape[1:])


def to_sequences(frames, clip, perm):
    rows, _, bands, width = frames.shape
    step = math.gcd(rows, MOVE_FRAMES)
    return pl.pallas_call(
        gather_kernel,
        grid=(rows // step,),
        in_specs=[
            pl.BlockSpec(perm.shape, lambda i: (0, 0)),
            pl.BlockSpec((step, 1, bands, width), lambda i: (i, clip, 0, 0)),
        ],
        out_specs=pl.BlockSpec((bands, step, width), lambda i: (0, i, 0)),
        out_shape=jax.ShapeDtypeStruct((bands, rows, width), BF),
        name="frames_to_sequences",
    )(perm, frames)


def fill_kernel(perm_ref, x_ref, *refs):
    o_ref = refs[-1]
    for start in range(0, o_ref.shape[0], TILE_FRAMES):
        span = slice(start, start + TILE_FRAMES)
        moved = nn(perm_ref[...], flat(x_ref.at[:, span]))
        o_ref[span] = moved.reshape((TILE_FRAMES,) + o_ref.shape[1:])


def to_frames(sequences, clip, clips, perm_back, target):
    bands, rows, width = sequences.shape
    step = math.gcd(rows, MOVE_FRAMES)
    return pl.pallas_call(
        fill_kernel,
        grid=(rows // step,),
        in_specs=[
            pl.BlockSpec(perm_back.shape, lambda i: (0, 0)),
            pl.BlockSpec((bands, step, width), lambda i: (0, i, 0)),
        ]
        + [pl.BlockSpec(memory_space=pl.ANY)] * len(target),
        out_specs=pl.BlockSpec((step, 1, bands, width), lambda i: (i, clip, 0, 0)),
        out_shape=jax.ShapeDtypeStruct((rows, clips, bands, width), F32),
        input_output_aliases={2: 0} if target else {},
        name="sequences_to_frames",
    )(perm_back, sequences, *target)


def const_spec(array):
    zeros = (0,) * array.ndim
    return pl.BlockSpec(array.shape, lambda *_: zeros, pipeline_mode=pl.Buffered(1))


def cost(rows, per_row, nbytes):
    return pl.CostEstimate(flops=int(2 * rows * per_row), bytes_accessed=nbytes, transcendentals=0)


def params(megabytes, semantics=None):
    return pltpu.CompilerParams(vmem_limit_bytes=megabytes << 20, dimension_semantics=semantics)


def extend_weights(w_ref, wg_ref, scratch):
    width = HEAD_WIDTH
    scratch[: 2 * width] = w_ref[: 2 * width]
    for start in range(0, 2 * width, HEAD_DIM):
        at = 2 * width + start
        scratch[at : at + HALF] = -w_ref[start + HALF : start + HEAD_DIM]
        scratch[at + HALF : at + HEAD_DIM] = w_ref[start : start + HALF]
    scratch[4 * width : 5 * width] = w_ref[2 * width :]
    gates = wg_ref[...].astype(F32)
    for head in range(HEADS):
        at = 5 * width + head * HEAD_DIM
        row = jnp.broadcast_to(gates[head : head + 1], (HEAD_DIM, gates.shape[1]))
        scratch[at : at + HEAD_DIM] = row.astype(BF)


def project_kernel(
    x_ref, cq, sq, ck, sk, wq_ref, wg_ref, gain_ref, bg_ref, qkv_ref, gate_ref, w_ref
):
    seqs = x_ref.shape[1]

    @pl.when(pl.program_id(0) == 0)
    def _():
        extend_weights(wq_ref, wg_ref, w_ref)

    unit, _ = rms(flat(x_ref).astype(F32))
    normed = (unit * gain_ref[...]).astype(BF)

    def table(ref):
        value = ref[...]
        if seqs > 1:
            value = jnp.broadcast_to(value[:, None], (value.shape[0], seqs) + value.shape[1:])
        return value.reshape(-1, LANES)

    queries, keys, value, gate = project(
        normed, w_ref, (table(cq), table(sq), table(ck), table(sk)), bg_ref[...]
    )
    lead = qkv_ref.shape[:-1]
    for pair, tensor in enumerate(queries + keys):
        qkv_ref[..., pair * LANES : (pair + 1) * LANES] = tensor.reshape(lead + (LANES,))
    qkv_ref[..., 2 * HEAD_WIDTH :] = value.reshape(lead + (HEAD_WIDTH,))
    gate_ref[...] = gate.astype(gate_ref.dtype).reshape(gate_ref.shape)


def source_block(groups, seqs, rows, target):
    block = max(1, target // (seqs * rows))
    return math.gcd(groups, block)


def time_project(x, tables, wq, wg, gain, b_gate):
    groups, seqs, rows, width = x.shape
    sb = source_block(groups, seqs, rows, ROW_TARGET)

    def rows_spec(lanes):
        return pl.BlockSpec((sb, seqs, rows, lanes), lambda i: (i, 0, 0, 0))

    table_spec = pl.BlockSpec((sb, rows, LANES), lambda i: (i, 0, 0))
    return pl.pallas_call(
        project_kernel,
        grid=(groups // sb,),
        in_specs=[rows_spec(width)]
        + [table_spec] * 4
        + [const_spec(wq), const_spec(wg), const_spec(gain), const_spec(b_gate)],
        out_specs=[rows_spec(3 * HEAD_WIDTH), rows_spec(HEAD_WIDTH)],
        scratch_shapes=[pltpu.VMEM((6 * HEAD_WIDTH, width), BF)],
        out_shape=[
            jax.ShapeDtypeStruct((groups, seqs, rows, 3 * HEAD_WIDTH), BF),
            jax.ShapeDtypeStruct((groups, seqs, rows, HEAD_WIDTH), BF),
        ],
        compiler_params=params(56),
        cost_estimate=cost(groups * seqs * rows, 6 * HEAD_WIDTH * width * 2, 1 << 20),
        name="time_project",
    )(x, *tables, wq, wg, gain, b_gate)


def time_attend_kernel(len_ref, q_ref, k_ref, v_ref, att_ref, inv_ref, p_ref):
    low, high, _, inner = lane_masks()
    keys, values, queries = flat(k_ref), flat(v_ref), flat(q_ref)
    rows = keys.shape[0]
    position = lax.broadcasted_iota(jnp.int32, (rows, LANES), 0)
    beyond = position >= len_ref[pl.program_id(0)]
    extra_k = jnp.where((inner == 0) & beyond, NEGATIVE, 0.0).astype(BF)
    extra_q = jnp.where(inner == 0, 1.0, 0.0).astype(BF)
    block = math.gcd(rows, BLOCK_Q)
    per_source = q_ref.shape[2]
    key_augs, value_ones = pair_operands(keys, values, extra_k, low, high)
    for start in range(0, rows, block):
        at = slice(start, start + block)
        src = slice(start // per_source, (start + block) // per_source)
        shape = (block // per_source, 1, per_source, LANES)
        out, inverse, kept = attend_pair(queries[at], key_augs, value_ones, extra_q, low, high)
        for slot in range(2):
            p_ref[0, slot, at] = kept[slot]
        att_ref[src] = out.astype(BF).reshape(shape)
        inv_ref[src] = inverse.reshape(shape)


def time_attend(qkv, lens):
    groups, seqs, rows, _ = qkv.shape
    frames = groups * rows

    def spec(first):
        return pl.BlockSpec((groups, 1, rows, LANES), lambda s, p, *_: (0, s, 0, first + p))

    return pl.pallas_call(
        time_attend_kernel,
        grid_spec=pltpu.PrefetchScalarGridSpec(
            num_scalar_prefetch=1,
            grid=(seqs, PAIRS),
            in_specs=[spec(0), spec(PAIRS), spec(2 * PAIRS)],
            out_specs=[
                spec(0),
                spec(0),
                pl.BlockSpec((1, 2, frames, frames), lambda s, p, *_: (s, p, 0, 0)),
            ],
        ),
        out_shape=[
            jax.ShapeDtypeStruct((groups, seqs, rows, HEAD_WIDTH), BF),
            jax.ShapeDtypeStruct((groups, seqs, rows, HEAD_WIDTH), F32),
            jax.ShapeDtypeStruct((seqs, HEADS, frames, frames), BF),
        ],
        compiler_params=params(60),
        cost_estimate=cost(
            groups * seqs * rows, groups * rows * HEADS * 2 * 256 * 2, 1 << 20
        ),
        name="time_attend",
    )(lens, qkv, qkv, qkv)


def time_mlp_kernel(
    x_ref, att_ref, gate_ref, wo, wu, wd, gain, bu, bd, h_ref, mid_ref, act_ref, slope_ref
):
    gated = (flat(att_ref).astype(F32) * flat(gate_ref).astype(F32)).astype(BF)
    middle = flat(x_ref).astype(F32) + nn(gated, wo[...])
    result, _, _, _, act, slope = feed_forward(middle, gain[...], wu[...], bu[...], wd[...], bd[...])
    h_ref[...] = result.astype(BF).reshape(h_ref.shape)
    mid_ref[...] = middle.reshape(mid_ref.shape)
    act_ref[...] = act.reshape(act_ref.shape)
    slope_ref[...] = slope.reshape(slope_ref.shape)


def time_mlp(x, attended, gate, weights):
    groups, seqs, rows, width = x.shape
    hidden = weights[1].shape[0]
    sb = source_block(groups, seqs, rows, ROW_TARGET)

    def rows_spec(lanes):
        return pl.BlockSpec((sb, seqs, rows, lanes), lambda i: (i, 0, 0, 0))

    def out(lanes, dtype):
        return jax.ShapeDtypeStruct((groups, seqs, rows, lanes), dtype)

    return pl.pallas_call(
        time_mlp_kernel,
        grid=(groups // sb,),
        in_specs=[rows_spec(width), rows_spec(HEAD_WIDTH), rows_spec(HEAD_WIDTH)]
        + [const_spec(w) for w in weights],
        out_specs=[rows_spec(width), rows_spec(width), rows_spec(hidden), rows_spec(hidden)],
        out_shape=[out(width, BF), out(width, F32), out(hidden, BF), out(hidden, BF)],
        compiler_params=params(56),
        cost_estimate=cost(groups * seqs * rows, width * (HEAD_WIDTH + 2 * hidden) * 3, 1 << 20),
        name="time_mlp",
    )(x, attended, gate, *weights)


def accumulate(first, pairs):
    @pl.when(first)
    def _():
        for ref, _ in pairs:
            ref[...] = jnp.zeros_like(ref)

    for ref, value in pairs:
        ref[...] += value


def time_mlp_back_kernel(
    g_ref, mid_ref, act_ref, slope_ref, att_ref, gate_ref, inv_ref,
    wo, wu, wd, gain_ref, heads, swapped,
    gmid_ref, gatt_ref, logit_ref, a_down, a_up, a_out, a_bias, a_vec,
):
    first = pl.program_id(0) == 0
    gain = gain_ref[...]
    grad_last = flat(g_ref)
    act = flat(act_ref)
    grad_up = (nt(grad_last, wd[...]) * flat(slope_ref).astype(F32)).astype(BF)
    unit, scale = rms(flat(mid_ref))
    normed = (unit * gain).astype(BF)
    grad_normed = nn(grad_up, wu[...])
    gradient = grad_last.astype(F32)
    grad_middle = gradient + rms_back(unit, scale, gain, grad_normed)
    grad_branch = grad_middle.astype(BF)
    att = flat(att_ref)
    gate = flat(gate_ref).astype(F32)
    gated = (att.astype(F32) * gate).astype(BF)
    grad_att, grad_logit, delta = branch_back(
        grad_branch, wo[...], att, gate, flat(inv_ref), heads[...], swapped[...]
    )
    low, high, picks, _ = lane_masks()
    lead = gatt_ref.shape[:-1]
    for pair in range(PAIRS):
        at = slice(pair * LANES, (pair + 1) * LANES)
        both = grads_with_delta(grad_att[:, at], delta[:, at], low, high, picks)
        for slot in range(2):
            where = 2 * pair + slot
            gatt_ref[..., where * LANES : (where + 1) * LANES] = both[slot].reshape(lead + (LANES,))
    gmid_ref[...] = grad_middle.reshape(gmid_ref.shape)
    logit_ref[...] = grad_logit.reshape(logit_ref.shape)
    vec = jnp.concatenate([col_sum(gradient), col_sum(grad_normed * unit)], axis=0)
    accumulate(
        first,
        (
            (a_down, tn(grad_last, act)),
            (a_up, tn(normed, grad_up)),
            (a_out, tn(grad_branch, gated)),
            (a_bias, col_sum(grad_up)),
            (a_vec, vec),
        ),
    )


def sum_shapes(*shapes):
    return [jax.ShapeDtypeStruct(shape, F32) for shape in shapes]


def time_mlp_back(grad, middle, act, slope, attended, gate, inverse, weights, sums):
    groups, seqs, rows, width = grad.shape
    hidden = act.shape[-1]
    sb = source_block(groups, seqs, rows, ROW_TARGET)

    def rows_spec(lanes):
        return pl.BlockSpec((sb, seqs, rows, lanes), lambda i: (i, 0, 0, 0))

    def out(lanes, dtype):
        return jax.ShapeDtypeStruct((groups, seqs, rows, lanes), dtype)

    consts = tuple(weights) + tuple(sums)
    starts = sum_shapes((width, hidden), (width, hidden), (width, HEAD_WIDTH), (1, hidden), (2, width))
    return pl.pallas_call(
        time_mlp_back_kernel,
        grid=(groups // sb,),
        in_specs=[rows_spec(width), rows_spec(width), rows_spec(hidden), rows_spec(hidden)]
        + [rows_spec(HEAD_WIDTH)] * 3
        + [const_spec(w) for w in consts],
        out_specs=[rows_spec(width), rows_spec(2 * HEAD_WIDTH), rows_spec(LANES)]
        + [const_spec(s) for s in starts],
        out_shape=[out(width, F32), out(2 * HEAD_WIDTH, BF), out(LANES, BF)]
        + starts,
        compiler_params=params(60),
        cost_estimate=cost(groups * seqs * rows, width * (HEAD_WIDTH + 2 * hidden) * 5, 1 << 20),
        name="time_mlp_back",
    )(grad, middle, act, slope, attended, gate, inverse, *consts)


def time_attend_back_kernel(
    p_ref, q_ref, k_ref, v_ref, gatt_ref, cos_ref, sin_ref, swap_ref, dq_ref, dk_ref, dv_ref
):
    low, high, picks, _ = lane_masks()
    grads = flat(gatt_ref)
    grad_query, grad_key, grad_value = pair_back(
        lambda slot, at: p_ref[0, slot, at],
        flat(q_ref),
        flat(k_ref),
        flat(v_ref),
        (grads[:, :LANES], grads[:, LANES:]),
        low,
        high,
        picks,
        math.gcd(grads.shape[0], BLOCK_Q_BACK),
    )
    cos, sin, swap_t = flat(cos_ref), flat(sin_ref), swap_ref[...]
    dq_ref[...] = unrotate(grad_query, cos, sin, swap_t).astype(BF).reshape(dq_ref.shape)
    dk_ref[...] = unrotate(grad_key, cos, sin, swap_t).astype(BF).reshape(dk_ref.shape)
    dv_ref[...] = grad_value.astype(BF).reshape(dv_ref.shape)


def time_attend_back(probs, qkv, grad_aug, cos, sin, swap_t):
    groups, seqs, rows, _ = qkv.shape
    frames = groups * rows

    def spec(lanes, first):
        return pl.BlockSpec((groups, 1, rows, lanes), lambda s, p: (0, s, 0, first + p))

    out = jax.ShapeDtypeStruct((groups, seqs, rows, HEAD_WIDTH), BF)
    return pl.pallas_call(
        time_attend_back_kernel,
        grid=(seqs, PAIRS),
        in_specs=[
            pl.BlockSpec((1, 2, frames, frames), lambda s, p: (s, p, 0, 0)),
            spec(LANES, 0),
            spec(LANES, PAIRS),
            spec(LANES, 2 * PAIRS),
            spec(2 * LANES, 0),
            const_spec(cos),
            const_spec(sin),
            const_spec(swap_t),
        ],
        out_specs=[spec(LANES, 0)] * 3,
        out_shape=[out] * 3,
        compiler_params=params(60),
        cost_estimate=cost(
            groups * seqs * rows, groups * rows * HEADS * 5 * 256 * 3 // 2, 1 << 20
        ),
        name="time_attend_back",
    )(probs, qkv, qkv, qkv, grad_aug, cos, sin, swap_t)


def time_project_back_kernel(
    x_ref, dq_ref, dk_ref, dv_ref, logit_ref, gmid_ref,
    wq, wg, gain_ref,
    gx_ref, a_qkv, a_gate, a_vec, a_bias,
):
    gain = gain_ref[...]
    unit, scale = rms(flat(x_ref).astype(F32))
    normed = (unit * gain).astype(BF)
    packed = jnp.concatenate([flat(dq_ref), flat(dk_ref), flat(dv_ref)], axis=1)
    logit = flat(logit_ref)
    grad_normed = nn(packed, wq[...]) + nn(logit, wg[...])
    grad_x = flat(gmid_ref) + rms_back(unit, scale, gain, grad_normed)
    gx_ref[...] = grad_x.astype(BF).reshape(gx_ref.shape)
    accumulate(
        pl.program_id(0) == 0,
        (
            (a_qkv, tn(normed, packed)),
            (a_gate, tn(logit, normed)),
            (a_vec, col_sum(grad_normed * unit)),
            (a_bias, col_sum(logit)),
        ),
    )


def time_project_back(x, grads, logit, grad_middle, weights):
    groups, seqs, rows, width = x.shape
    starts = sum_shapes((width, 3 * HEAD_WIDTH), (LANES, width), (1, width), (1, LANES))
    sb = source_block(groups, seqs, rows, ROW_TARGET)

    def rows_spec(lanes):
        return pl.BlockSpec((sb, seqs, rows, lanes), lambda i: (i, 0, 0, 0))

    consts = tuple(weights)
    return pl.pallas_call(
        time_project_back_kernel,
        grid=(groups // sb,),
        in_specs=[rows_spec(width)]
        + [rows_spec(HEAD_WIDTH)] * 3
        + [rows_spec(LANES), rows_spec(width)]
        + [const_spec(w) for w in consts],
        out_specs=[rows_spec(width)] + [const_spec(s) for s in starts],
        out_shape=[jax.ShapeDtypeStruct((groups, seqs, rows, width), BF)]
        + starts,
        compiler_params=params(60),
        cost_estimate=cost(groups * seqs * rows, width * 6 * HEAD_WIDTH * 5 // 2, 1 << 20),
        name="time_project_back",
    )(x, *grads, logit, grad_middle, *consts)


def band_kernel(
    h_ref, g_ref, perm_ref, back_ref, cq, sq, ck, sk, exq_ref, exk_ref, swap_ref, heads, swapped,
    wq, wo, wu, wd, wg, gain0_ref, gain1_ref, bu, bd, bg,
    *refs,
):
    out_ref, gh_ref, a_qkv, a_up, a_down, a_out, a_gate, a_bias, a_vec, a_gbias, w_ext = refs[-11:]
    first = pl.program_id(0) == 0

    @pl.when(first)
    def _():
        extend_weights(wq, wg, w_ext)

    gain0, gain1 = gain0_ref[...], gain1_ref[...]
    low, high, picks, _ = lane_masks()
    bands, frames, _ = h_ref.shape
    spans = [slice(k, k + TILE_FRAMES) for k in range(0, frames, TILE_FRAMES)]
    size = bands * TILE_FRAMES
    tiles = [slice(k * size, (k + 1) * size) for k in range(len(spans))]

    def stacked(values, axis=0):
        return values[0] if len(values) == 1 else jnp.concatenate(values, axis=axis)

    def table(ref):
        return stacked([ref[...]] * len(spans))

    hidden = stacked([flat(h_ref.at[:, span]) for span in spans]).astype(F32)
    unit0, scale0 = rms(hidden)
    normed0 = (unit0 * gain0).astype(BF)
    queries, keys, value, gate = project(
        normed0, w_ext, (table(cq), table(sq), table(ck), table(sk)), bg[...]
    )
    extra_q, extra_k = exq_ref[...], exk_ref[...]
    attended, inverse, kept = [], [], []
    for tile in tiles:
        outs, inverses = [], []
        for pair in range(PAIRS):
            at = slice(pair * LANES, (pair + 1) * LANES)
            key_augs, value_ones = pair_operands(
                keys[pair][tile], value[tile, at], extra_k, low, high
            )
            out, one_over, probs = attend_pair(
                queries[pair][tile], key_augs, value_ones, extra_q, low, high
            )
            outs.append(out.astype(BF))
            inverses.append(one_over)
            kept.append(probs)
        attended.append(jnp.concatenate(outs, axis=1))
        inverse.append(jnp.concatenate(inverses, axis=1))
    attended, inverse = stacked(attended), stacked(inverse)
    gated = (attended.astype(F32) * gate).astype(BF)
    middle = hidden + nn(gated, wo[...])
    result, normed1, unit1, scale1, act, slope = feed_forward(
        middle, gain1, wu[...], bu[...], wd[...], bd[...]
    )
    result = result.astype(BF)
    gradient = []
    for span, tile in zip(spans, tiles):
        out = nn(back_ref[...], result[tile]).astype(BF)
        out_ref[span] = out.reshape((TILE_FRAMES,) + out_ref.shape[1:])
        gradient.append(nn(perm_ref[...], flat(g_ref.at[span])))
    gradient = stacked(gradient)
    grad_last = gradient.astype(BF)
    grad_up = (nt(grad_last, wd[...]) * slope.astype(F32)).astype(BF)
    grad_normed1 = nn(grad_up, wu[...])
    grad_middle = gradient + rms_back(unit1, scale1, gain1, grad_normed1)
    grad_branch = grad_middle.astype(BF)
    grad_att, grad_logit, delta = branch_back(
        grad_branch, wo[...], attended, gate, inverse, heads[...], swapped[...]
    )
    swap_t = swap_ref[...]
    packed = []
    for index, tile in enumerate(tiles):
        grads_q, grads_k, grads_v = [], [], []
        for pair in range(PAIRS):
            at = slice(pair * LANES, (pair + 1) * LANES)
            both = grads_with_delta(grad_att[tile, at], delta[tile, at], low, high, picks)
            grad_query, grad_key, grad_value = pair_back(
                lambda slot, _, probs=kept[index * PAIRS + pair]: probs[slot],
                queries[pair][tile], keys[pair][tile], value[tile, at], both,
                low, high, picks, size,
            )
            grads_q.append(unrotate(grad_query, ck[...], sk[...], swap_t).astype(BF))
            grads_k.append(unrotate(grad_key, ck[...], sk[...], swap_t).astype(BF))
            grads_v.append(grad_value.astype(BF))
        packed.append(jnp.concatenate(grads_q + grads_k + grads_v, axis=1))
    packed = stacked(packed)
    width = HEAD_WIDTH
    grad_normed0 = (
        nn(packed[:, : 2 * width], w_ext[: 2 * width])
        + nn(packed[:, 2 * width :], w_ext[4 * width : 5 * width])
        + nn(grad_logit, wg[...])
    )
    grad_hidden = grad_middle + rms_back(unit0, scale0, gain0, grad_normed0)
    for span, tile in zip(spans, tiles):
        gh_ref[:, span] = grad_hidden[tile].astype(BF).reshape(bands, TILE_FRAMES, -1)
    vec = jnp.concatenate(
        [col_sum(gradient), col_sum(grad_normed1 * unit1), col_sum(grad_normed0 * unit0)], axis=0
    )
    accumulate(
        first,
        (
            (a_qkv, tn(normed0, packed)),
            (a_up, tn(normed1, grad_up)),
            (a_down, tn(grad_last, act)),
            (a_out, tn(grad_branch, gated)),
            (a_gate, tn(grad_logit, normed0)),
            (a_bias, col_sum(grad_up)),
            (a_vec, vec),
            (a_gbias, col_sum(grad_logit)),
        ),
    )


def band_layer(hidden, grad_out, clip, consts, inner, final):
    bands, rows, width = hidden.shape
    consts = tuple(consts)
    starts = sum_shapes(
        (width, 3 * HEAD_WIDTH), (width, inner), (width, inner), (width, HEAD_WIDTH),
        (LANES, width), (1, inner), (3, width), (1, LANES),
    )
    frames = math.gcd(rows, BAND_FRAMES)
    seq_spec = pl.BlockSpec((bands, frames, width), lambda i: (0, i, 0))
    frame_spec = pl.BlockSpec((frames, 1, bands, width), lambda i: (i, clip, 0, 0))
    return pl.pallas_call(
        band_kernel,
        grid=(rows // frames,),
        in_specs=[seq_spec, frame_spec]
        + [const_spec(c) for c in consts]
        + [pl.BlockSpec(memory_space=pl.ANY)] * len(final),
        out_specs=[frame_spec, seq_spec] + [const_spec(s) for s in starts],
        out_shape=[
            jax.ShapeDtypeStruct(grad_out.shape, BF),
            jax.ShapeDtypeStruct((bands, rows, width), BF),
        ]
        + starts,
        scratch_shapes=[pltpu.VMEM((6 * HEAD_WIDTH, width), BF)],
        input_output_aliases={2 + len(consts): 0} if final else {},
        compiler_params=params(62),
        cost_estimate=cost(bands * rows, width * (4 * HEAD_WIDTH + 2 * inner) * 13, 1 << 20),
        name="band_layer",
    )(hidden, grad_out, *consts, *final)


def flip_kernel(terms, *refs):
    target, start = refs[-1], 0
    count = (len(refs) - 1) // terms
    devices, _, width = target.shape
    for index in range(count):
        total = refs[index][...]
        for term in range(1, terms):
            total = total + refs[term * count + index][...]
        size = total.shape[1] // devices
        rows = total.T.astype(target.dtype).reshape(devices, size, width)
        target[:, start : start + size] = rows
        start += size


def flip(groups, devices, dtype, weight=256):
    width = groups[0][0].shape[0]
    sizes = [array.shape[1] // devices for array in groups[0]]
    if any(size % 16 for size in sizes):
        parts = [add_up(list(arrays)).T.astype(dtype) for arrays in zip(*groups)]
        return jnp.concatenate([p.reshape(devices, -1, width) for p in parts], axis=1)
    return pl.pallas_call(
        partial(flip_kernel, len(groups)),
        out_shape=jax.ShapeDtypeStruct((devices, sum(sizes), width), dtype),
        compiler_params=params(56),
        cost_estimate=cost(4096, weight, 1 << 20),
        name="flip_sums",
    )(*[array for group in groups for array in group])


def add_up(arrays):
    return sum(arrays[1:], arrays[0])


def rotary_tables(positions):
    steps = np.exp(np.arange(HALF, dtype=np.float32) * np.float32(-math.log(10000.0) / HALF))
    angles = positions.astype(np.float32)[:, None] * steps[None, :]
    cos = np.tile(np.cos(angles), (1, LANES // HALF)).astype(np.float32)
    sin = np.tile(np.sin(angles), (1, LANES // HALF)).astype(np.float32)
    scale = np.float32(QUERY_SCALE)
    return cos * scale, sin * scale, cos, sin


def tile_permutation(bands):
    rows = bands * TILE_FRAMES
    row = np.arange(rows)
    source = (row % TILE_FRAMES) * bands + row // TILE_FRAMES
    return (source[:, None] == row[None, :]).astype(BF)


def head_sums():
    lane = np.arange(HEAD_WIDTH)
    heads = (lane[:, None] // HEAD_DIM == np.arange(LANES)[None, :]).astype(BF)
    swapped = (lane[:, None] // HEAD_DIM == (lane[None, :] // HEAD_DIM) ^ 1).astype(BF)
    return heads, swapped


def swap_matrix():
    lane = np.arange(LANES)
    same = lane[:, None] // HEAD_DIM == lane[None, :] // HEAD_DIM
    i, j = lane[:, None] % HEAD_DIM, lane[None, :] % HEAD_DIM
    forward = np.where(j == i + HALF, 1.0, 0.0) + np.where(j == i - HALF, -1.0, 0.0)
    return np.where(same, forward, 0.0).T.astype(BF)


def band_extras(bands):
    rows = bands * TILE_FRAMES
    frame = np.arange(rows) % TILE_FRAMES
    inner = np.arange(LANES) % HEAD_DIM
    mine = inner[None, :] == frame[:, None]
    slot = inner < TILE_FRAMES
    extra_k = np.where(slot[None, :] & ~mine, NEGATIVE, 0.0)
    return mine.astype(BF), extra_k.astype(BF)


def xor_pairs(count, bit):
    return [(i, i ^ bit) for i in range(count)]


def gather_first(block, split, unpack, chunks, send):
    chunk, later = chunks[0], chunks[1:]
    steps = []
    for axis in ("fsdp", "dp"):
        size = lax.axis_size(axis)
        bits = [1 << k for k in range(1, size.bit_length() - 1)] + [1]
        steps += [(axis, bit) for bit in bits if bit < size]

    def double(tensor, axis, bit):
        other = lax.ppermute(tensor, axis, xor_pairs(lax.axis_size(axis), bit))
        mine_first = (lax.axis_index(axis) // bit) % 2 == 0
        return jnp.stack(
            [jnp.where(mine_first, tensor, other), jnp.where(mine_first, other, tensor)]
        )

    order = list(reversed(steps))
    wanted = sorted(range(len(order)), key=lambda k: (order[k][0] != "dp", -order[k][1]))

    def arrange(tensor):
        rank = len(order)
        tensor = tensor.transpose(*wanted, rank, rank + 1)
        return tensor.reshape((lax.axis_size("dp"), lax.axis_size("fsdp")) + tensor.shape[-2:])

    tensor = block
    for index, (axis, bit) in enumerate(steps[:-1]):
        tensor = double(tensor, axis, bit)
        if index == 1:
            tensor, chunk = lax.optimization_barrier((tensor, chunk))
            chunk = send(chunk)
        if index == 2:
            tensor, later = lax.optimization_barrier((tensor, later))
    rest = unpack(arrange(double(tensor[..., split:, :], *steps[-1])))
    tensor, chunk, rest = lax.optimization_barrier((tensor[..., :split, :], chunk, rest))
    return arrange(double(tensor, *steps[-1])), rest, [chunk] + later


def after(tensors, done):
    return lax.optimization_barrier((tensors, done))[0]


def pick(tensor, index):
    return lax.dynamic_index_in_dim(tensor, index, 0, keepdims=False)


def shed(tensor, place, axis, unit):
    parts = [
        lax.ppermute(
            pick(tensor, place ^ step), axis, xor_pairs(lax.axis_size(axis), step * unit)
        )
        for step in range(1, tensor.shape[0])
    ]
    return pick(tensor, place), parts


def gain(pending, before):
    own, parts = pending
    parts, before = lax.optimization_barrier((parts, before))
    total = own.astype(F32)
    for part in parts:
        total = total + part.astype(F32)
    return total, before


def shed_cores(blocks):
    dp, groups = lax.axis_size("dp"), lax.axis_size("fsdp")
    tensor = blocks.astype(BF).reshape((dp // 2, 2, groups) + blocks.shape[1:]).swapaxes(0, 1)
    return shed(tensor, lax.axis_index("dp") % 2, "dp", 1)


def shed_chips(total):
    return shed(total.astype(BF), lax.axis_index("dp") // 2, "dp", 2)


def shed_last(total):
    return shed(total.astype(BF), lax.axis_index("fsdp"), "fsdp", 1)


def vector_parts(rows, bias, gate_bias):
    dp, groups = lax.axis_size("dp"), lax.axis_size("fsdp")
    devices, count, shard = dp * groups, rows.shape[0], rows.shape[1] // groups
    own = rows.reshape(count, groups, shard).swapaxes(0, 1).reshape(1, groups, count * shard)
    own = jnp.broadcast_to(own, (dp, groups, count * shard)).reshape(devices, -1)
    gate_bias = jnp.broadcast_to(gate_bias, (devices, gate_bias.shape[-1]))
    return jnp.concatenate([own, bias.reshape(devices, -1), gate_bias], axis=1).astype(BF)


def cut(tensor, sizes):
    parts, start = [], 0
    for size in sizes:
        parts.append(tensor[start : start + size])
        start += size
    return parts


def on_device(
    frames_in, lengths, w_qkv, w_out, w_up, b_up, w_down, gains, b_down, w_gate, b_gate, grad_out
):
    rows, clips, bands, width = frames_in.shape
    dp, groups = lax.axis_size("dp"), lax.axis_size("fsdp")
    position = lax.axis_index("fsdp")
    everyone = ("dp", "fsdp")
    devices, shard = dp * groups, width // groups
    hidden = w_up.shape[2] * devices
    seq_count = clips * bands // groups
    by_clip = bands % groups == 0
    chunk_count = clips if by_clip else 1
    chunk_seqs = seq_count // chunk_count

    wq_t, wu_t = w_qkv.swapaxes(1, 2), w_up.swapaxes(1, 2)
    sizes = [wq_t.shape[1], wu_t.shape[1], w_down.shape[1], w_out.shape[1]]
    small = jnp.concatenate(
        [gains.reshape(-1), b_down.reshape(-1), w_gate.reshape(-1), b_up.reshape(-1)]
    )
    total = -(-(sizes[0] * width + small.shape[0]) // (16 * width)) * 16
    small_rows = total - sizes[0]
    small = jnp.pad(small, (0, small_rows * width - small.shape[0])).reshape(-1, width)
    perm = tile_permutation(bands)
    clip_seqs = [to_sequences(frames_in, clip, perm) for clip in range(clips)]
    first = after(jnp.concatenate([wq_t[0], small], axis=0), clip_seqs[0])
    if by_clip:
        chunks = [seqs.reshape(groups, chunk_seqs, rows, width) for seqs in clip_seqs]
    else:
        chunks = [jnp.concatenate(clip_seqs).reshape(groups, chunk_seqs, rows, width)]
    def exchange(tensor):
        return lax.all_to_all(tensor, "fsdp", split_axis=0, concat_axis=0, tiled=True)

    def unpack_small(small):
        small = small.reshape(dp, groups, -1)
        vector_count = 4 + 2 + 2 * HEADS
        vectors = small[0, :, : vector_count * shard].reshape(groups, vector_count, shard)
        vectors = vectors.swapaxes(0, 1).reshape(vector_count, width)
        gates = jnp.pad(
            vectors[6:].reshape(2, HEADS, width), ((0, 0), (0, LANES - HEADS), (0, 0))
        )
        bias = small[:, :, vector_count * shard :][:, :, : 2 * sizes[1]]
        bias = bias.reshape(devices, 2, -1).swapaxes(0, 1).reshape(2, 1, -1).astype(F32)
        return (
            [[vectors[2 * t + k].reshape(1, width).astype(F32) for k in range(2)] for t in range(2)],
            [vectors[4 + t].reshape(1, width).astype(F32) for t in range(2)],
            [gates[t] for t in range(2)],
            [bias[t] for t in range(2)],
            [jnp.repeat(b_gate[t].astype(F32), HEAD_DIM)[None] for t in range(2)],
        )

    wq, small, chunks = gather_first(first, sizes[0], unpack_small, chunks, exchange)
    wq = wq.reshape(-1, width)
    gains_full, b_down_full, gates_full, b_up_full, b_gate_full = small

    def unpack(gathered, parts):
        cut, found = 0, []
        for size in parts:
            found.append(gathered[:, cut : cut + size].reshape(-1, width))
            cut += size
        return found

    rest = jnp.concatenate([wu_t[0], w_down[0], w_out[0]], axis=0)
    second = jnp.concatenate([wq_t[1], wu_t[1], w_down[1], w_out[1]], axis=0)

    heads, swapped = head_sums()
    swap_t = swap_matrix()
    frame_tables = rotary_tables(np.arange(groups * rows))
    frame_tables = tuple(t.reshape(groups, rows, LANES) for t in frame_tables)
    band_tables = rotary_tables(np.arange(bands * TILE_FRAMES) // TILE_FRAMES)
    extra_q, extra_k = band_extras(bands)

    saved, returned = [], []
    arrived = [chunks[0]] + [exchange(chunk) for chunk in chunks[1:]]
    rest = lax.all_gather(rest, everyone, axis=0)
    arrived[0], wq, second = lax.optimization_barrier((arrived[0], wq, second))
    second = lax.all_gather(second, everyone, axis=0)
    wu, wd, wo = unpack(rest, sizes[1:])
    mlp_weights = (wo, wu, wd, gains_full[0][1], b_up_full[0], b_down_full[0])
    for chunk in range(chunk_count):
        x = arrived[chunk]
        if by_clip:
            lens = jnp.broadcast_to(lengths[chunk], (chunk_seqs,))
        else:
            lens = lengths[(position * chunk_seqs + jnp.arange(chunk_seqs)) // bands]
        qkv, gate = time_project(
            x, frame_tables, wq, gates_full[0], gains_full[0][0], b_gate_full[0]
        )
        attended, inverse, probs = time_attend(qkv, lens)
        h1, middle, act, slope = time_mlp(x, attended, gate, mlp_weights)
        saved.append((x, qkv, gate, attended, inverse, probs, middle, act, slope))
        returned.append(exchange(h1))
    if by_clip:
        band_inputs = [h.reshape(bands, rows, width) for h in returned]
    else:
        whole = returned[0].reshape(clips, bands, rows, width)
        band_inputs = [whole[clip] for clip in range(clips)]

    wq1, wu1, wd1, wo1 = unpack(second, sizes)
    consts = (
        (perm, perm.T) + band_tables + (extra_q, extra_k, swap_t, heads, swapped)
        + (wq1, wo1, wu1, wd1, gates_full[1], gains_full[1][0], gains_full[1][1])
        + (b_up_full[1], b_down_full[1], b_gate_full[1])
    )
    final = []
    grads, sums = [], []
    for clip in range(clips):
        done, grad_hidden, *parts = band_layer(
            band_inputs[clip], grad_out, clip, consts, hidden, final
        )
        final = [done]
        grads.append(grad_hidden)
        sums.append(parts)
    band_parts = sums
    b_gate_, b_bias, b_vec, b_gbias = (add_up(t) for t in list(zip(*sums))[4:])
    band_rows = jnp.concatenate([b_vec[2:3], b_vec[1:2], b_vec[0:1], b_gate_[:HEADS]])
    band_vectors = vector_parts(band_rows, b_bias, b_gbias[:, :HEADS])

    if by_clip:
        grads = [g.reshape(groups, chunk_seqs, rows, width) for g in grads]
    else:
        grads = [jnp.concatenate(grads).reshape(groups, chunk_seqs, rows, width)]
    grads = [exchange(g) for g in grads]
    band_sums = flip([parts[:4] for parts in band_parts], devices, BF)
    band_sums, grads[0] = lax.optimization_barrier((band_sums, grads[0]))
    band_sums = lax.psum_scatter(
        band_sums.reshape(-1, width), everyone, scatter_dimension=0, tiled=True
    )
    sums, sums_back, halves = [], [], []
    for chunk in range(chunk_count):
        x, qkv, gate, attended, inverse, probs, middle, act, slope = saved[chunk]
        grad_middle, grad_aug, logit, *parts = time_mlp_back(
            grads[chunk], middle, act, slope, attended, gate, inverse,
            (wo, wu, wd, gains_full[0][1]), (heads, swapped),
        )
        sums.append(parts)
        halves.append((grad_middle, grad_aug, logit))
    last_chunk = chunk_count - 1
    t_bias, t_vec = (add_up(t) for t in list(zip(*sums))[3:])
    mlp_sums = flip([(up, down, out) for down, up, out, _, _ in sums], devices, BF)
    sequences = []
    for chunk in range(chunk_count):
        x, qkv, gate, attended, inverse, probs, middle, act, slope = saved[chunk]
        grad_middle, grad_aug, logit = halves[chunk]
        if chunk == 0:
            mlp_sums, grad_aug = lax.optimization_barrier((mlp_sums, grad_aug))
            mlp_sums = shed_cores(mlp_sums)
        else:
            grad_aug, grad_x = lax.optimization_barrier((grad_aug, grad_x))
        packed_grads = time_attend_back(
            probs, qkv, grad_aug, frame_tables[2], frame_tables[3], swap_t
        )
        if chunk == 0:
            mlp_sums, packed_grads = gain(mlp_sums, packed_grads)
            mlp_sums = shed_chips(mlp_sums)
        if chunk == last_chunk:
            mlp_sums, packed_grads = gain(mlp_sums, packed_grads)
        grad_x, *parts = time_project_back(
            x, packed_grads, logit, grad_middle, (wq, gates_full[0], gains_full[0][0])
        )
        sums_back.append(parts)
        sequences.append(exchange(grad_x).reshape(-1, bands, rows, width))
    t_gate, t_vec0, t_gbias = (add_up(t) for t in list(zip(*sums_back))[1:])
    time_rows = jnp.concatenate([t_vec0, t_vec[1:2], t_vec[0:1], t_gate[:HEADS]])
    time_vectors = vector_parts(time_rows, t_bias, t_gbias[:, :HEADS])
    vectors = jnp.concatenate([time_vectors, band_vectors], axis=1)
    sequences[0], sums_back = lax.optimization_barrier((sequences[0], sums_back))
    last = flip([parts[:1] for parts in sums_back], devices, BF, 6 << 20)
    total = -(-(sizes[0] * width + vectors.shape[1]) // (16 * width)) * 16 - sizes[0]
    vectors = jnp.pad(vectors, ((0, 0), (0, total * width - vectors.shape[1])))
    sequences = [s[k] for s in sequences for k in range(s.shape[0])]
    grad_input = to_frames(sequences[0], 0, clips, perm.T, [])
    last = jnp.concatenate([last, vectors.reshape(devices, total, width)], axis=1)
    last, _ = gain(shed_cores(last), ())
    last, grad_input = gain(shed_chips(last), grad_input)
    last, _ = gain(shed_last(jnp.concatenate([mlp_sums, last], axis=1)), ())
    mlp_sums, last = last[: sum(sizes[1:])], last[sum(sizes[1:]) :]
    grad_input = [grad_input]
    for clip in range(1, clips):
        grad_input = [to_frames(sequences[clip], clip, clips, perm.T, grad_input)]

    tq, vectors = last[: sizes[0]], last[sizes[0] :].reshape(-1)
    bq, bu, bd, bo = cut(band_sums.astype(F32), sizes)
    tu, td, to = cut(mlp_sums, sizes[1:])
    lengths_each = (2 * shard, shard, HEADS * shard, sizes[1], HEADS)
    time_parts = cut(vectors, lengths_each)
    band_parts = cut(vectors[sum(lengths_each) :], lengths_each)
    g_gains, g_b_down, g_gate, g_b_up, g_b_gate = (
        jnp.stack(both) for both in zip(time_parts, band_parts)
    )
    return (
        final[0],
        grad_input[0],
        jnp.stack([tq.T, bq.T]),
        jnp.stack([to, bo]),
        jnp.stack([tu.T, bu.T]),
        g_b_up,
        jnp.stack([td, bd]),
        g_gains.reshape(2, 2, shard),
        g_b_down,
        g_gate.reshape(2, HEADS, shard),
        g_b_gate,
    )


def solution(mesh):
    everyone = ("dp", "fsdp")
    rows = P("fsdp", "dp", None, None)
    last, middle = P(None, None, everyone), P(None, everyone, None)
    return jax.shard_map(
        on_device,
        mesh=mesh,
        in_specs=(
            rows, P("dp"), last, middle, last, P(None, everyone), middle,
            P(None, None, "fsdp"), P(None, "fsdp"), P(None, None, "fsdp"), P(), rows,
        ),
        out_specs=(
            rows, rows, last, middle, last, P(None, everyone), middle,
            P(None, None, "fsdp"), P(None, "fsdp"), P(None, None, "fsdp"), P(),
        ),
        check_vma=False,
    )
```

```python
from functools import partial
import math

import jax
import jax.numpy as jnp
import numpy as np
from jax import lax
from jax.experimental import pallas as pl
from jax.experimental.pallas import tpu as pltpu
from jax.sharding import PartitionSpec as P

HEADS = 8
HEAD_DIM = 64
HALF = HEAD_DIM // 2
HEAD_WIDTH = HEADS * HEAD_DIM
PAIRS = HEADS // 2
LANES = 2 * HEAD_DIM
TILE_FRAMES = 16
EPSILON = 1e-06
NEGATIVE = -1e30
LOG2E = 1.0 / math.log(2.0)
LN2 = math.log(2.0)
QUERY_SCALE = HEAD_DIM**-0.5 * LOG2E
BLOCK_Q = 128
BLOCK_Q_BACK = 256
BAND_FRAMES = 32
ROW_TARGET = 512
MOVE_FRAMES = 32

BF = jnp.bfloat16
F32 = jnp.float32


def nn(a, b):
    return jnp.dot(a, b, preferred_element_type=F32)


def nt(a, b):
    return lax.dot_general(a, b, (((1,), (1,)), ((), ())), preferred_element_type=F32)


def tn(a, b):
    return lax.dot_general(a, b, (((0,), (0,)), ((), ())), preferred_element_type=F32)


def rms(hidden):
    scale = lax.rsqrt(jnp.mean(hidden * hidden, axis=-1, keepdims=True) + EPSILON)
    return hidden * scale, scale


def rms_back(unit, scale, gain, grad):
    weighted = grad * gain
    inner = jnp.mean(weighted * unit, axis=-1, keepdims=True)
    return scale * (weighted - unit * inner)


def gelu_pair(up):
    cdf = 0.5 + 0.5 * lax.erf(up * math.sqrt(0.5))
    bell = jnp.exp2((-0.5 * LOG2E) * (up * up))
    return up * cdf, cdf + (up * bell) * (1.0 / math.sqrt(2.0 * math.pi))


def project(normed, w_ext, tables, b_gate):
    cos_q, sin_q, cos_k, sin_k = tables
    width = HEAD_WIDTH
    plain = nt(normed, w_ext[: 2 * width])
    swapped = nt(normed, w_ext[2 * width : 4 * width])
    value = nt(normed, w_ext[4 * width : 5 * width]).astype(BF)
    gate = jax.nn.sigmoid(nt(normed, w_ext[5 * width :]) + b_gate)
    queries, keys = [], []
    for pair in range(2 * PAIRS):
        at = slice(pair * LANES, (pair + 1) * LANES)
        cos, sin = (cos_q, sin_q) if pair < PAIRS else (cos_k, sin_k)
        turned = (plain[:, at] * cos + swapped[:, at] * sin).astype(BF)
        (queries if pair < PAIRS else keys).append(turned)
    return queries, keys, value, gate


def attend_pair(query, key_augs, value_ones, extra_q, low, high):
    outs, inverses, kept = [], [], []
    for slot in range(2):
        own, other = (low, high) if slot == 0 else (high, low)
        scores = nt(query * own + extra_q * other, key_augs[slot])
        probs = jnp.exp2(scores - jnp.max(scores, axis=-1, keepdims=True)).astype(BF)
        mixed = nn(probs, value_ones[slot])
        inverse = 1.0 / mixed[:, LANES:]
        outs.append(mixed[:, :LANES] * inverse)
        inverses.append(inverse)
        kept.append(probs)
    is_low = lax.broadcasted_iota(jnp.int32, (1, LANES), 1) < HEAD_DIM
    return outs[0] + outs[1], jnp.where(is_low, *inverses), kept


def pair_operands(keys, values, extra_k, low, high):
    ones = jnp.ones(values.shape, BF)
    key_augs = (keys * low + extra_k * high, keys * high + extra_k * low)
    value_ones = (
        jnp.concatenate([values * low, ones], axis=1),
        jnp.concatenate([values * high, ones], axis=1),
    )
    return key_augs, value_ones


def unrotate(grad, cos, sin, swap_t):
    return grad * cos + nn((grad * sin).astype(BF), swap_t)


def lane_masks():
    lane = lax.broadcasted_iota(jnp.int32, (1, LANES), 1)
    inner = lane % HEAD_DIM
    low = jnp.where(lane < HEAD_DIM, 1.0, 0.0).astype(BF)
    high = jnp.where(lane < HEAD_DIM, 0.0, 1.0).astype(BF)
    picks = tuple(jnp.where(inner == k, 1.0, 0.0).astype(BF) for k in range(2))
    return low, high, picks, inner


def pair_back(probs_of, queries, keys, values, grads, low, high, picks, block_q):
    rows = queries.shape[0]
    query_t = queries.T
    grad_t = (grads[0] * low + grads[1] * high).T
    is_low = lax.broadcasted_iota(jnp.int32, (1, LANES), 1) < HEAD_DIM
    two = picks[0] + picks[1]
    query_parts, key_sums, value_sums = [], [], []
    for slot in range(2):
        own, other = (low, high) if slot == 0 else (high, low)
        value_aug = values * own + two * other
        head = slice(slot * HEAD_DIM, (slot + 1) * HEAD_DIM)
        key_sum = value_sum = None
        parts = []
        for start in range(0, rows, block_q):
            at = slice(start, start + block_q)
            probs = probs_of(slot, at)
            grad_scores = (probs.astype(F32) * nt(grads[slot][at], value_aug)).astype(BF)
            grad_value = nn(grad_t[head, at], probs)
            grad_key = nn(query_t[head, at], grad_scores)
            parts.append(nn(grad_scores, keys))
            key_sum = grad_key if key_sum is None else key_sum + grad_key
            value_sum = grad_value if value_sum is None else value_sum + grad_value
        query_parts.append(parts)
        key_sums.append(key_sum)
        value_sums.append(value_sum)
    blocks = [jnp.where(is_low, *both) for both in zip(*query_parts)]
    grad_query = jnp.concatenate(blocks, axis=0) if len(blocks) > 1 else blocks[0]
    grad_key = jnp.concatenate(key_sums, axis=0).T * LN2
    return grad_query * HEAD_DIM**-0.5, grad_key, jnp.concatenate(value_sums, axis=0).T


def feed_forward(middle, gain, w_up, b_up, w_down, b_down):
    unit, scale = rms(middle)
    normed = (unit * gain).astype(BF)
    act, slope = gelu_pair(nt(normed, w_up) + b_up)
    act, slope = act.astype(BF), slope.astype(BF)
    return middle + (nn(act, w_down) + b_down), normed, unit, scale, act, slope


def branch_back(grad_branch, w_out, attended, gate, inverse, sum_heads, sum_swapped):
    grad_gated = nt(grad_branch, w_out)
    att = attended.astype(F32)
    grad_att = (grad_gated * (gate * inverse)).astype(BF)
    logit_terms = (grad_gated * att * (gate * (1.0 - gate))).astype(BF)
    grad_logit = nn(logit_terms, sum_heads).astype(BF)
    delta = nn((grad_att.astype(F32) * att).astype(BF), sum_swapped)
    return grad_att, grad_logit, delta


def grads_with_delta(grad_att, delta, low, high, picks):
    hi = delta.astype(BF)
    mid = (delta - hi.astype(F32)).astype(BF)
    extra = -(hi * picks[0] + mid * picks[1])
    return grad_att * low + extra * high, grad_att * high + extra * low


def col_sum(values):
    return jnp.sum(values.astype(F32), axis=0, keepdims=True)


def flat(ref):
    value = ref[...]
    return value.reshape(-1, value.shape[-1])


def gather_kernel(perm_ref, x_ref, o_ref):
    for start in range(0, x_ref.shape[0], TILE_FRAMES):
        span = slice(start, start + TILE_FRAMES)
        moved = nn(perm_ref[...], flat(x_ref.at[span])).astype(BF)
        o_ref[:, span] = moved.reshape((-1, TILE_FRAMES) + moved.shape[1:])


def to_sequences(frames, clip, perm):
    rows, _, bands, width = frames.shape
    step = math.gcd(rows, MOVE_FRAMES)
    return pl.pallas_call(
        gather_kernel,
        grid=(rows // step,),
        in_specs=[
            pl.BlockSpec(perm.shape, lambda i: (0, 0)),
            pl.BlockSpec((step, 1, bands, width), lambda i: (i, clip, 0, 0)),
        ],
        out_specs=pl.BlockSpec((bands, step, width), lambda i: (0, i, 0)),
        out_shape=jax.ShapeDtypeStruct((bands, rows, width), BF),
        name="frames_to_sequences",
    )(perm, frames)


def fill_kernel(perm_ref, x_ref, *refs):
    o_ref = refs[-1]
    for start in range(0, o_ref.shape[0], TILE_FRAMES):
        span = slice(start, start + TILE_FRAMES)
        moved = nn(perm_ref[...], flat(x_ref.at[:, span]))
        o_ref[span] = moved.reshape((TILE_FRAMES,) + o_ref.shape[1:])


def to_frames(sequences, clip, clips, perm_back, target):
    bands, rows, width = sequences.shape
    step = math.gcd(rows, MOVE_FRAMES)
    return pl.pallas_call(
        fill_kernel,
        grid=(rows // step,),
        in_specs=[
            pl.BlockSpec(perm_back.shape, lambda i: (0, 0)),
            pl.BlockSpec((bands, step, width), lambda i: (0, i, 0)),
        ]
        + [pl.BlockSpec(memory_space=pl.ANY)] * len(target),
        out_specs=pl.BlockSpec((step, 1, bands, width), lambda i: (i, clip, 0, 0)),
        out_shape=jax.ShapeDtypeStruct((rows, clips, bands, width), F32),
        input_output_aliases={2: 0} if target else {},
        name="sequences_to_frames",
    )(perm_back, sequences, *target)


def operand(const):
    return const[0] if isinstance(const, tuple) else const


def row_count(const):
    return const[0].shape[0] * const[2] if isinstance(const, tuple) else const.shape[0]


def const_spec(array):
    if isinstance(array, tuple):
        array, first, size = array
        block = (array.shape[0], size, array.shape[2])
        return pl.BlockSpec(
            block, lambda *_: (0, first // size, 0), pipeline_mode=pl.Buffered(1)
        )
    zeros = (0,) * array.ndim
    return pl.BlockSpec(array.shape, lambda *_: zeros, pipeline_mode=pl.Buffered(1))


def cost(rows, per_row, nbytes):
    return pl.CostEstimate(flops=int(2 * rows * per_row), bytes_accessed=nbytes, transcendentals=0)


def params(megabytes, semantics=None):
    return pltpu.CompilerParams(vmem_limit_bytes=megabytes << 20, dimension_semantics=semantics)


def extend_weights(w_ref, wg_ref, scratch):
    width = HEAD_WIDTH
    w_ref = flat(w_ref)
    scratch[: 2 * width] = w_ref[: 2 * width]
    for start in range(0, 2 * width, HEAD_DIM):
        at = 2 * width + start
        scratch[at : at + HALF] = -w_ref[start + HALF : start + HEAD_DIM]
        scratch[at + HALF : at + HEAD_DIM] = w_ref[start : start + HALF]
    scratch[4 * width : 5 * width] = w_ref[2 * width :]
    gates = wg_ref[...].astype(F32)
    for head in range(HEADS):
        at = 5 * width + head * HEAD_DIM
        row = jnp.broadcast_to(gates[head : head + 1], (HEAD_DIM, gates.shape[1]))
        scratch[at : at + HEAD_DIM] = row.astype(BF)


def project_kernel(
    x_ref, cq, sq, ck, sk, wq_ref, wg_ref, gain_ref, bg_ref, qkv_ref, gate_ref, w_ref
):
    seqs = x_ref.shape[1]

    @pl.when(pl.program_id(0) == 0)
    def _():
        extend_weights(wq_ref, wg_ref, w_ref)

    unit, _ = rms(flat(x_ref).astype(F32))
    normed = (unit * gain_ref[...]).astype(BF)

    def table(ref):
        value = ref[...]
        if seqs > 1:
            value = jnp.broadcast_to(value[:, None], (value.shape[0], seqs) + value.shape[1:])
        return value.reshape(-1, LANES)

    queries, keys, value, gate = project(
        normed, w_ref, (table(cq), table(sq), table(ck), table(sk)), bg_ref[...]
    )
    lead = qkv_ref.shape[:-1]
    for pair, tensor in enumerate(queries + keys):
        qkv_ref[..., pair * LANES : (pair + 1) * LANES] = tensor.reshape(lead + (LANES,))
    qkv_ref[..., 2 * HEAD_WIDTH :] = value.reshape(lead + (HEAD_WIDTH,))
    gate_ref[...] = gate.astype(gate_ref.dtype).reshape(gate_ref.shape)


def source_block(groups, seqs, rows, target):
    block = max(1, target // (seqs * rows))
    return math.gcd(groups, block)


def time_project(x, tables, wq, wg, gain, b_gate):
    groups, seqs, rows, width = x.shape
    sb = source_block(groups, seqs, rows, ROW_TARGET)

    def rows_spec(lanes):
        return pl.BlockSpec((sb, seqs, rows, lanes), lambda i: (i, 0, 0, 0))

    table_spec = pl.BlockSpec((sb, rows, LANES), lambda i: (i, 0, 0))
    return pl.pallas_call(
        project_kernel,
        grid=(groups // sb,),
        in_specs=[rows_spec(width)]
        + [table_spec] * 4
        + [const_spec(wq), const_spec(wg), const_spec(gain), const_spec(b_gate)],
        out_specs=[rows_spec(3 * HEAD_WIDTH), rows_spec(HEAD_WIDTH)],
        scratch_shapes=[pltpu.VMEM((6 * HEAD_WIDTH, width), BF)],
        out_shape=[
            jax.ShapeDtypeStruct((groups, seqs, rows, 3 * HEAD_WIDTH), BF),
            jax.ShapeDtypeStruct((groups, seqs, rows, HEAD_WIDTH), BF),
        ],
        compiler_params=params(56),
        cost_estimate=cost(groups * seqs * rows, 6 * HEAD_WIDTH * width * 2, 1 << 20),
        name="time_project",
    )(x, *tables, wq, wg, gain, b_gate)


def time_attend_kernel(len_ref, q_ref, k_ref, v_ref, att_ref, inv_ref, p_ref):
    low, high, _, inner = lane_masks()
    keys, values, queries = flat(k_ref), flat(v_ref), flat(q_ref)
    rows = keys.shape[0]
    position = lax.broadcasted_iota(jnp.int32, (rows, LANES), 0)
    beyond = position >= len_ref[pl.program_id(0)]
    extra_k = jnp.where((inner == 0) & beyond, NEGATIVE, 0.0).astype(BF)
    extra_q = jnp.where(inner == 0, 1.0, 0.0).astype(BF)
    block = math.gcd(rows, BLOCK_Q)
    per_source = q_ref.shape[2]
    key_augs, value_ones = pair_operands(keys, values, extra_k, low, high)
    for start in range(0, rows, block):
        at = slice(start, start + block)
        src = slice(start // per_source, (start + block) // per_source)
        shape = (block // per_source, 1, per_source, LANES)
        out, inverse, kept = attend_pair(queries[at], key_augs, value_ones, extra_q, low, high)
        for slot in range(2):
            p_ref[0, slot, at] = kept[slot]
        att_ref[src] = out.astype(BF).reshape(shape)
        inv_ref[src] = inverse.reshape(shape)


def time_attend(qkv, lens):
    groups, seqs, rows, _ = qkv.shape
    frames = groups * rows

    def spec(first):
        return pl.BlockSpec((groups, 1, rows, LANES), lambda s, p, *_: (0, s, 0, first + p))

    return pl.pallas_call(
        time_attend_kernel,
        grid_spec=pltpu.PrefetchScalarGridSpec(
            num_scalar_prefetch=1,
            grid=(seqs, PAIRS),
            in_specs=[spec(0), spec(PAIRS), spec(2 * PAIRS)],
            out_specs=[
                spec(0),
                spec(0),
                pl.BlockSpec((1, 2, frames, frames), lambda s, p, *_: (s, p, 0, 0)),
            ],
        ),
        out_shape=[
            jax.ShapeDtypeStruct((groups, seqs, rows, HEAD_WIDTH), BF),
            jax.ShapeDtypeStruct((groups, seqs, rows, HEAD_WIDTH), F32),
            jax.ShapeDtypeStruct((seqs, HEADS, frames, frames), BF),
        ],
        compiler_params=params(60),
        cost_estimate=cost(
            groups * seqs * rows, groups * rows * HEADS * 2 * 256 * 2, 1 << 20
        ),
        name="time_attend",
    )(lens, qkv, qkv, qkv)


def time_mlp_kernel(
    x_ref, att_ref, gate_ref, wo, wu, wd, gain, bu, bd, h_ref, mid_ref, act_ref, slope_ref
):
    gated = (flat(att_ref).astype(F32) * flat(gate_ref).astype(F32)).astype(BF)
    middle = flat(x_ref).astype(F32) + nn(gated, flat(wo))
    result, _, _, _, act, slope = feed_forward(
        middle, gain[...], flat(wu), bu[...], flat(wd), bd[...]
    )
    h_ref[...] = result.astype(BF).reshape(h_ref.shape)
    mid_ref[...] = middle.reshape(mid_ref.shape)
    act_ref[...] = act.reshape(act_ref.shape)
    slope_ref[...] = slope.reshape(slope_ref.shape)


def time_mlp(x, attended, gate, weights):
    groups, seqs, rows, width = x.shape
    hidden = row_count(weights[1])
    sb = source_block(groups, seqs, rows, ROW_TARGET)

    def rows_spec(lanes):
        return pl.BlockSpec((sb, seqs, rows, lanes), lambda i: (i, 0, 0, 0))

    def out(lanes, dtype):
        return jax.ShapeDtypeStruct((groups, seqs, rows, lanes), dtype)

    return pl.pallas_call(
        time_mlp_kernel,
        grid=(groups // sb,),
        in_specs=[rows_spec(width), rows_spec(HEAD_WIDTH), rows_spec(HEAD_WIDTH)]
        + [const_spec(w) for w in weights],
        out_specs=[rows_spec(width), rows_spec(width), rows_spec(hidden), rows_spec(hidden)],
        out_shape=[out(width, BF), out(width, F32), out(hidden, BF), out(hidden, BF)],
        compiler_params=params(56),
        cost_estimate=cost(groups * seqs * rows, width * (HEAD_WIDTH + 2 * hidden) * 3, 1 << 20),
        name="time_mlp",
    )(x, attended, gate, *map(operand, weights))


def accumulate(first, pairs):
    @pl.when(first)
    def _():
        for ref, _ in pairs:
            ref[...] = jnp.zeros_like(ref)

    for ref, value in pairs:
        ref[...] += value


def time_mlp_back_kernel(
    g_ref, mid_ref, act_ref, slope_ref, att_ref, gate_ref, inv_ref,
    wo, wu, wd, gain_ref, heads, swapped,
    gmid_ref, gatt_ref, logit_ref, a_down, a_up, a_out, a_bias, a_vec,
):
    first = pl.program_id(0) == 0
    gain = gain_ref[...]
    grad_last = flat(g_ref)
    act = flat(act_ref)
    grad_up = (nt(grad_last, flat(wd)) * flat(slope_ref).astype(F32)).astype(BF)
    unit, scale = rms(flat(mid_ref))
    normed = (unit * gain).astype(BF)
    grad_normed = nn(grad_up, flat(wu))
    gradient = grad_last.astype(F32)
    grad_middle = gradient + rms_back(unit, scale, gain, grad_normed)
    grad_branch = grad_middle.astype(BF)
    att = flat(att_ref)
    gate = flat(gate_ref).astype(F32)
    gated = (att.astype(F32) * gate).astype(BF)
    grad_att, grad_logit, delta = branch_back(
        grad_branch, flat(wo), att, gate, flat(inv_ref), heads[...], swapped[...]
    )
    low, high, picks, _ = lane_masks()
    lead = gatt_ref.shape[:-1]
    for pair in range(PAIRS):
        at = slice(pair * LANES, (pair + 1) * LANES)
        both = grads_with_delta(grad_att[:, at], delta[:, at], low, high, picks)
        for slot in range(2):
            where = 2 * pair + slot
            gatt_ref[..., where * LANES : (where + 1) * LANES] = both[slot].reshape(lead + (LANES,))
    gmid_ref[...] = grad_middle.reshape(gmid_ref.shape)
    logit_ref[...] = grad_logit.reshape(logit_ref.shape)
    vec = jnp.concatenate([col_sum(gradient), col_sum(grad_normed * unit)], axis=0)
    accumulate(
        first,
        (
            (a_down, tn(grad_last, act)),
            (a_up, tn(normed, grad_up)),
            (a_out, tn(grad_branch, gated)),
            (a_bias, col_sum(grad_up)),
            (a_vec, vec),
        ),
    )


def sum_shapes(*shapes):
    return [jax.ShapeDtypeStruct(shape, F32) for shape in shapes]


def time_mlp_back(grad, middle, act, slope, attended, gate, inverse, weights, sums):
    groups, seqs, rows, width = grad.shape
    hidden = act.shape[-1]
    sb = source_block(groups, seqs, rows, ROW_TARGET)

    def rows_spec(lanes):
        return pl.BlockSpec((sb, seqs, rows, lanes), lambda i: (i, 0, 0, 0))

    def out(lanes, dtype):
        return jax.ShapeDtypeStruct((groups, seqs, rows, lanes), dtype)

    consts = tuple(weights) + tuple(sums)
    starts = sum_shapes((width, hidden), (width, hidden), (width, HEAD_WIDTH), (1, hidden), (2, width))
    return pl.pallas_call(
        time_mlp_back_kernel,
        grid=(groups // sb,),
        in_specs=[rows_spec(width), rows_spec(width), rows_spec(hidden), rows_spec(hidden)]
        + [rows_spec(HEAD_WIDTH)] * 3
        + [const_spec(w) for w in consts],
        out_specs=[rows_spec(width), rows_spec(2 * HEAD_WIDTH), rows_spec(LANES)]
        + [const_spec(s) for s in starts],
        out_shape=[out(width, F32), out(2 * HEAD_WIDTH, BF), out(LANES, BF)]
        + starts,
        compiler_params=params(60),
        cost_estimate=cost(groups * seqs * rows, width * (HEAD_WIDTH + 2 * hidden) * 5, 1 << 20),
        name="time_mlp_back",
    )(grad, middle, act, slope, attended, gate, inverse, *map(operand, consts))


def time_attend_back_kernel(
    p_ref, q_ref, k_ref, v_ref, gatt_ref, cos_ref, sin_ref, swap_ref, dq_ref, dk_ref, dv_ref
):
    low, high, picks, _ = lane_masks()
    grads = flat(gatt_ref)
    grad_query, grad_key, grad_value = pair_back(
        lambda slot, at: p_ref[0, slot, at],
        flat(q_ref),
        flat(k_ref),
        flat(v_ref),
        (grads[:, :LANES], grads[:, LANES:]),
        low,
        high,
        picks,
        math.gcd(grads.shape[0], BLOCK_Q_BACK),
    )
    cos, sin, swap_t = flat(cos_ref), flat(sin_ref), swap_ref[...]
    dq_ref[...] = unrotate(grad_query, cos, sin, swap_t).astype(BF).reshape(dq_ref.shape)
    dk_ref[...] = unrotate(grad_key, cos, sin, swap_t).astype(BF).reshape(dk_ref.shape)
    dv_ref[...] = grad_value.astype(BF).reshape(dv_ref.shape)


def time_attend_back(probs, qkv, grad_aug, cos, sin, swap_t):
    groups, seqs, rows, _ = qkv.shape
    frames = groups * rows

    def spec(lanes, first):
        return pl.BlockSpec((groups, 1, rows, lanes), lambda s, p: (0, s, 0, first + p))

    out = jax.ShapeDtypeStruct((groups, seqs, rows, HEAD_WIDTH), BF)
    return pl.pallas_call(
        time_attend_back_kernel,
        grid=(seqs, PAIRS),
        in_specs=[
            pl.BlockSpec((1, 2, frames, frames), lambda s, p: (s, p, 0, 0)),
            spec(LANES, 0),
            spec(LANES, PAIRS),
            spec(LANES, 2 * PAIRS),
            spec(2 * LANES, 0),
            const_spec(cos),
            const_spec(sin),
            const_spec(swap_t),
        ],
        out_specs=[spec(LANES, 0)] * 3,
        out_shape=[out] * 3,
        compiler_params=params(60),
        cost_estimate=cost(
            groups * seqs * rows, groups * rows * HEADS * 5 * 256 * 3 // 2, 1 << 20
        ),
        name="time_attend_back",
    )(probs, qkv, qkv, qkv, grad_aug, cos, sin, swap_t)


def time_project_back_kernel(
    x_ref, dq_ref, dk_ref, dv_ref, logit_ref, gmid_ref,
    wq, wg, gain_ref,
    gx_ref, a_qkv, a_gate, a_vec, a_bias,
):
    gain = gain_ref[...]
    unit, scale = rms(flat(x_ref).astype(F32))
    normed = (unit * gain).astype(BF)
    packed = jnp.concatenate([flat(dq_ref), flat(dk_ref), flat(dv_ref)], axis=1)
    logit = flat(logit_ref)
    grad_normed = nn(packed, wq[...]) + nn(logit, wg[...])
    grad_x = flat(gmid_ref) + rms_back(unit, scale, gain, grad_normed)
    gx_ref[...] = grad_x.astype(BF).reshape(gx_ref.shape)
    accumulate(
        pl.program_id(0) == 0,
        (
            (a_qkv, tn(normed, packed)),
            (a_gate, tn(logit, normed)),
            (a_vec, col_sum(grad_normed * unit)),
            (a_bias, col_sum(logit)),
        ),
    )


def time_project_back(x, grads, logit, grad_middle, weights):
    groups, seqs, rows, width = x.shape
    starts = sum_shapes((width, 3 * HEAD_WIDTH), (LANES, width), (1, width), (1, LANES))
    sb = source_block(groups, seqs, rows, ROW_TARGET)

    def rows_spec(lanes):
        return pl.BlockSpec((sb, seqs, rows, lanes), lambda i: (i, 0, 0, 0))

    consts = tuple(weights)
    return pl.pallas_call(
        time_project_back_kernel,
        grid=(groups // sb,),
        in_specs=[rows_spec(width)]
        + [rows_spec(HEAD_WIDTH)] * 3
        + [rows_spec(LANES), rows_spec(width)]
        + [const_spec(w) for w in consts],
        out_specs=[rows_spec(width)] + [const_spec(s) for s in starts],
        out_shape=[jax.ShapeDtypeStruct((groups, seqs, rows, width), BF)]
        + starts,
        compiler_params=params(60),
        cost_estimate=cost(groups * seqs * rows, width * 6 * HEAD_WIDTH * 5 // 2, 1 << 20),
        name="time_project_back",
    )(x, *grads, logit, grad_middle, *consts)


def band_kernel(
    h_ref, g_ref, perm_ref, back_ref, cq, sq, ck, sk, exq_ref, exk_ref, swap_ref, heads, swapped,
    wq, wo, wu, wd, wg, gain0_ref, gain1_ref, bu, bd, bg,
    *refs,
):
    out_ref, gh_ref, a_qkv, a_up, a_down, a_out, a_gate, a_bias, a_vec, a_gbias, w_ext = refs[-11:]
    first = pl.program_id(0) == 0

    @pl.when(first)
    def _():
        extend_weights(wq, wg, w_ext)

    gain0, gain1 = gain0_ref[...], gain1_ref[...]
    low, high, picks, _ = lane_masks()
    bands, frames, _ = h_ref.shape
    spans = [slice(k, k + TILE_FRAMES) for k in range(0, frames, TILE_FRAMES)]
    size = bands * TILE_FRAMES
    tiles = [slice(k * size, (k + 1) * size) for k in range(len(spans))]

    def stacked(values, axis=0):
        return values[0] if len(values) == 1 else jnp.concatenate(values, axis=axis)

    def table(ref):
        return stacked([ref[...]] * len(spans))

    hidden = stacked([flat(h_ref.at[:, span]) for span in spans]).astype(F32)
    unit0, scale0 = rms(hidden)
    normed0 = (unit0 * gain0).astype(BF)
    queries, keys, value, gate = project(
        normed0, w_ext, (table(cq), table(sq), table(ck), table(sk)), bg[...]
    )
    extra_q, extra_k = exq_ref[...], exk_ref[...]
    attended, inverse, kept = [], [], []
    for tile in tiles:
        outs, inverses = [], []
        for pair in range(PAIRS):
            at = slice(pair * LANES, (pair + 1) * LANES)
            key_augs, value_ones = pair_operands(
                keys[pair][tile], value[tile, at], extra_k, low, high
            )
            out, one_over, probs = attend_pair(
                queries[pair][tile], key_augs, value_ones, extra_q, low, high
            )
            outs.append(out.astype(BF))
            inverses.append(one_over)
            kept.append(probs)
        attended.append(jnp.concatenate(outs, axis=1))
        inverse.append(jnp.concatenate(inverses, axis=1))
    attended, inverse = stacked(attended), stacked(inverse)
    gated = (attended.astype(F32) * gate).astype(BF)
    middle = hidden + nn(gated, flat(wo))
    result, normed1, unit1, scale1, act, slope = feed_forward(
        middle, gain1, flat(wu), bu[...], flat(wd), bd[...]
    )
    result = result.astype(BF)
    gradient = []
    for span, tile in zip(spans, tiles):
        out = nn(back_ref[...], result[tile]).astype(BF)
        out_ref[span] = out.reshape((TILE_FRAMES,) + out_ref.shape[1:])
        gradient.append(nn(perm_ref[...], flat(g_ref.at[span])))
    gradient = stacked(gradient)
    grad_last = gradient.astype(BF)
    grad_up = (nt(grad_last, flat(wd)) * slope.astype(F32)).astype(BF)
    grad_normed1 = nn(grad_up, flat(wu))
    grad_middle = gradient + rms_back(unit1, scale1, gain1, grad_normed1)
    grad_branch = grad_middle.astype(BF)
    grad_att, grad_logit, delta = branch_back(
        grad_branch, flat(wo), attended, gate, inverse, heads[...], swapped[...]
    )
    swap_t = swap_ref[...]
    packed = []
    for index, tile in enumerate(tiles):
        grads_q, grads_k, grads_v = [], [], []
        for pair in range(PAIRS):
            at = slice(pair * LANES, (pair + 1) * LANES)
            both = grads_with_delta(grad_att[tile, at], delta[tile, at], low, high, picks)
            grad_query, grad_key, grad_value = pair_back(
                lambda slot, _, probs=kept[index * PAIRS + pair]: probs[slot],
                queries[pair][tile], keys[pair][tile], value[tile, at], both,
                low, high, picks, size,
            )
            grads_q.append(unrotate(grad_query, ck[...], sk[...], swap_t).astype(BF))
            grads_k.append(unrotate(grad_key, ck[...], sk[...], swap_t).astype(BF))
            grads_v.append(grad_value.astype(BF))
        packed.append(jnp.concatenate(grads_q + grads_k + grads_v, axis=1))
    packed = stacked(packed)
    width = HEAD_WIDTH
    grad_normed0 = (
        nn(packed[:, : 2 * width], w_ext[: 2 * width])
        + nn(packed[:, 2 * width :], w_ext[4 * width : 5 * width])
        + nn(grad_logit, wg[...])
    )
    grad_hidden = grad_middle + rms_back(unit0, scale0, gain0, grad_normed0)
    for span, tile in zip(spans, tiles):
        gh_ref[:, span] = grad_hidden[tile].astype(BF).reshape(bands, TILE_FRAMES, -1)
    vec = jnp.concatenate(
        [col_sum(gradient), col_sum(grad_normed1 * unit1), col_sum(grad_normed0 * unit0)], axis=0
    )
    accumulate(
        first,
        (
            (a_qkv, tn(normed0, packed)),
            (a_up, tn(normed1, grad_up)),
            (a_down, tn(grad_last, act)),
            (a_out, tn(grad_branch, gated)),
            (a_gate, tn(grad_logit, normed0)),
            (a_bias, col_sum(grad_up)),
            (a_vec, vec),
            (a_gbias, col_sum(grad_logit)),
        ),
    )


def band_layer(hidden, grad_out, clip, consts, inner, final):
    bands, rows, width = hidden.shape
    consts = tuple(consts)
    starts = sum_shapes(
        (width, 3 * HEAD_WIDTH), (width, inner), (width, inner), (width, HEAD_WIDTH),
        (LANES, width), (1, inner), (3, width), (1, LANES),
    )
    frames = math.gcd(rows, BAND_FRAMES)
    seq_spec = pl.BlockSpec((bands, frames, width), lambda i: (0, i, 0))
    frame_spec = pl.BlockSpec((frames, 1, bands, width), lambda i: (i, clip, 0, 0))
    return pl.pallas_call(
        band_kernel,
        grid=(rows // frames,),
        in_specs=[seq_spec, frame_spec]
        + [const_spec(c) for c in consts]
        + [pl.BlockSpec(memory_space=pl.ANY)] * len(final),
        out_specs=[frame_spec, seq_spec] + [const_spec(s) for s in starts],
        out_shape=[
            jax.ShapeDtypeStruct(grad_out.shape, BF),
            jax.ShapeDtypeStruct((bands, rows, width), BF),
        ]
        + starts,
        scratch_shapes=[pltpu.VMEM((6 * HEAD_WIDTH, width), BF)],
        input_output_aliases={2 + len(consts): 0} if final else {},
        compiler_params=params(62),
        cost_estimate=cost(bands * rows, width * (4 * HEAD_WIDTH + 2 * inner) * 13, 1 << 20),
        name="band_layer",
    )(hidden, grad_out, *map(operand, consts), *final)


def flip_kernel(terms, *refs):
    target, start = refs[-1], 0
    count = (len(refs) - 1) // terms
    devices, _, width = target.shape
    for index in range(count):
        total = refs[index][...]
        for term in range(1, terms):
            total = total + refs[term * count + index][...]
        size = total.shape[1] // devices
        rows = total.T.astype(target.dtype).reshape(devices, size, width)
        target[:, start : start + size] = rows
        start += size


def flip(groups, devices, dtype, weight=256):
    width = groups[0][0].shape[0]
    sizes = [array.shape[1] // devices for array in groups[0]]
    if any(size % 16 for size in sizes):
        parts = [add_up(list(arrays)).T.astype(dtype) for arrays in zip(*groups)]
        return jnp.concatenate([p.reshape(devices, -1, width) for p in parts], axis=1)
    return pl.pallas_call(
        partial(flip_kernel, len(groups)),
        out_shape=jax.ShapeDtypeStruct((devices, sum(sizes), width), dtype),
        compiler_params=params(56),
        cost_estimate=cost(4096, weight, 1 << 20),
        name="flip_sums",
    )(*[array for group in groups for array in group])


def add_up(arrays):
    return sum(arrays[1:], arrays[0])


def rotary_tables(positions):
    steps = np.exp(np.arange(HALF, dtype=np.float32) * np.float32(-math.log(10000.0) / HALF))
    angles = positions.astype(np.float32)[:, None] * steps[None, :]
    cos = np.tile(np.cos(angles), (1, LANES // HALF)).astype(np.float32)
    sin = np.tile(np.sin(angles), (1, LANES // HALF)).astype(np.float32)
    scale = np.float32(QUERY_SCALE)
    return cos * scale, sin * scale, cos, sin


def tile_permutation(bands):
    rows = bands * TILE_FRAMES
    row = np.arange(rows)
    source = (row % TILE_FRAMES) * bands + row // TILE_FRAMES
    return (source[:, None] == row[None, :]).astype(BF)


def head_sums():
    lane = np.arange(HEAD_WIDTH)
    heads = (lane[:, None] // HEAD_DIM == np.arange(LANES)[None, :]).astype(BF)
    swapped = (lane[:, None] // HEAD_DIM == (lane[None, :] // HEAD_DIM) ^ 1).astype(BF)
    return heads, swapped


def swap_matrix():
    lane = np.arange(LANES)
    same = lane[:, None] // HEAD_DIM == lane[None, :] // HEAD_DIM
    i, j = lane[:, None] % HEAD_DIM, lane[None, :] % HEAD_DIM
    forward = np.where(j == i + HALF, 1.0, 0.0) + np.where(j == i - HALF, -1.0, 0.0)
    return np.where(same, forward, 0.0).T.astype(BF)


def band_extras(bands):
    rows = bands * TILE_FRAMES
    frame = np.arange(rows) % TILE_FRAMES
    inner = np.arange(LANES) % HEAD_DIM
    mine = inner[None, :] == frame[:, None]
    slot = inner < TILE_FRAMES
    extra_k = np.where(slot[None, :] & ~mine, NEGATIVE, 0.0)
    return mine.astype(BF), extra_k.astype(BF)


def xor_pairs(count, bit):
    return [(i, i ^ bit) for i in range(count)]


def gather_first(block, split, unpack, chunks, send):
    chunk, later = chunks[0], chunks[1:]
    steps = []
    for axis in ("fsdp", "dp"):
        size = lax.axis_size(axis)
        bits = [1 << k for k in range(1, size.bit_length() - 1)] + [1]
        steps += [(axis, bit) for bit in bits if bit < size]

    def double(tensor, axis, bit):
        other = lax.ppermute(tensor, axis, xor_pairs(lax.axis_size(axis), bit))
        mine_first = (lax.axis_index(axis) // bit) % 2 == 0
        return jnp.stack(
            [jnp.where(mine_first, tensor, other), jnp.where(mine_first, other, tensor)]
        )

    order = list(reversed(steps))
    wanted = sorted(range(len(order)), key=lambda k: (order[k][0] != "dp", -order[k][1]))

    def arrange(tensor):
        rank = len(order)
        tensor = tensor.transpose(*wanted, rank, rank + 1)
        return tensor.reshape((lax.axis_size("dp"), lax.axis_size("fsdp")) + tensor.shape[-2:])

    tensor = block
    for index, (axis, bit) in enumerate(steps[:-1]):
        tensor = double(tensor, axis, bit)
        if index == 1:
            tensor, chunk = lax.optimization_barrier((tensor, chunk))
            chunk = send(chunk)
        if index == 2:
            tensor, later = lax.optimization_barrier((tensor, later))
    rest = unpack(arrange(double(tensor[..., split:, :], *steps[-1])))
    tensor, chunk, rest = lax.optimization_barrier((tensor[..., :split, :], chunk, rest))
    return arrange(double(tensor, *steps[-1])), rest, [chunk] + later


def after(tensors, done):
    return lax.optimization_barrier((tensors, done))[0]


def pick(tensor, index):
    return lax.dynamic_index_in_dim(tensor, index, 0, keepdims=False)


def shed(tensor, place, axis, unit):
    parts = [
        lax.ppermute(
            pick(tensor, place ^ step), axis, xor_pairs(lax.axis_size(axis), step * unit)
        )
        for step in range(1, tensor.shape[0])
    ]
    return pick(tensor, place), parts


def gain(pending, before):
    own, parts = pending
    parts, before = lax.optimization_barrier((parts, before))
    total = own.astype(F32)
    for part in parts:
        total = total + part.astype(F32)
    return total, before


def shed_cores(blocks):
    dp, groups = lax.axis_size("dp"), lax.axis_size("fsdp")
    tensor = blocks.astype(BF).reshape((dp // 2, 2, groups) + blocks.shape[1:]).swapaxes(0, 1)
    return shed(tensor, lax.axis_index("dp") % 2, "dp", 1)


def shed_chips(total):
    return shed(total.astype(BF), lax.axis_index("dp") // 2, "dp", 2)


def shed_last(total):
    return shed(total.astype(BF), lax.axis_index("fsdp"), "fsdp", 1)


def vector_parts(rows, bias, gate_bias):
    dp, groups = lax.axis_size("dp"), lax.axis_size("fsdp")
    devices, count, shard = dp * groups, rows.shape[0], rows.shape[1] // groups
    own = rows.reshape(count, groups, shard).swapaxes(0, 1).reshape(1, groups, count * shard)
    own = jnp.broadcast_to(own, (dp, groups, count * shard)).reshape(devices, -1)
    gate_bias = jnp.broadcast_to(gate_bias, (devices, gate_bias.shape[-1]))
    return jnp.concatenate([own, bias.reshape(devices, -1), gate_bias], axis=1).astype(BF)


def cut(tensor, sizes):
    parts, start = [], 0
    for size in sizes:
        parts.append(tensor[start : start + size])
        start += size
    return parts


def on_device(
    frames_in, lengths, w_qkv, w_out, w_up, b_up, w_down, gains, b_down, w_gate, b_gate, grad_out
):
    rows, clips, bands, width = frames_in.shape
    dp, groups = lax.axis_size("dp"), lax.axis_size("fsdp")
    position = lax.axis_index("fsdp")
    everyone = ("dp", "fsdp")
    devices, shard = dp * groups, width // groups
    hidden = w_up.shape[2] * devices
    seq_count = clips * bands // groups
    by_clip = bands % groups == 0
    chunk_count = clips if by_clip else 1
    chunk_seqs = seq_count // chunk_count

    wq_t, wu_t = w_qkv.swapaxes(1, 2), w_up.swapaxes(1, 2)
    sizes = [wq_t.shape[1], wu_t.shape[1], w_down.shape[1], w_out.shape[1]]
    small = jnp.concatenate(
        [gains.reshape(-1), b_down.reshape(-1), w_gate.reshape(-1), b_up.reshape(-1)]
    )
    total = -(-(sizes[0] * width + small.shape[0]) // (16 * width)) * 16
    small_rows = total - sizes[0]
    small = jnp.pad(small, (0, small_rows * width - small.shape[0])).reshape(-1, width)
    perm = tile_permutation(bands)
    clip_seqs = [to_sequences(frames_in, clip, perm) for clip in range(clips)]
    first = after(jnp.concatenate([wq_t[0], small], axis=0), clip_seqs[0])
    if by_clip:
        chunks = [seqs.reshape(groups, chunk_seqs, rows, width) for seqs in clip_seqs]
    else:
        chunks = [jnp.concatenate(clip_seqs).reshape(groups, chunk_seqs, rows, width)]
    def exchange(tensor):
        return lax.all_to_all(tensor, "fsdp", split_axis=0, concat_axis=0, tiled=True)

    def unpack_small(small):
        small = small.reshape(dp, groups, -1)
        vector_count = 4 + 2 + 2 * HEADS
        vectors = small[0, :, : vector_count * shard].reshape(groups, vector_count, shard)
        vectors = vectors.swapaxes(0, 1).reshape(vector_count, width)
        gates = jnp.pad(
            vectors[6:].reshape(2, HEADS, width), ((0, 0), (0, LANES - HEADS), (0, 0))
        )
        bias = small[:, :, vector_count * shard :][:, :, : 2 * sizes[1]]
        bias = bias.reshape(devices, 2, -1).swapaxes(0, 1).reshape(2, 1, -1).astype(F32)
        return (
            [[vectors[2 * t + k].reshape(1, width).astype(F32) for k in range(2)] for t in range(2)],
            [vectors[4 + t].reshape(1, width).astype(F32) for t in range(2)],
            [gates[t] for t in range(2)],
            [bias[t] for t in range(2)],
            [jnp.repeat(b_gate[t].astype(F32), HEAD_DIM)[None] for t in range(2)],
        )

    wq, small, chunks = gather_first(first, sizes[0], unpack_small, chunks, exchange)
    wq = wq.reshape(-1, width)
    gains_full, b_down_full, gates_full, b_up_full, b_gate_full = small

    def unpack(gathered, parts):
        start, found = 0, []
        for size in parts:
            if size % 16 or start % size:
                found.append(gathered[:, start : start + size].reshape(-1, width))
            else:
                found.append((gathered, start, size))
            start += size
        return found

    rest = after((w_up, w_down, w_out), clip_seqs[0])
    rest = jnp.concatenate([rest[0].swapaxes(1, 2)[0], rest[1][0], rest[2][0]], axis=0)
    second = jnp.concatenate([wq_t[1], wu_t[1], w_down[1], w_out[1]], axis=0)

    heads, swapped = head_sums()
    swap_t = swap_matrix()
    frame_tables = rotary_tables(np.arange(groups * rows))
    frame_tables = tuple(t.reshape(groups, rows, LANES) for t in frame_tables)
    band_tables = rotary_tables(np.arange(bands * TILE_FRAMES) // TILE_FRAMES)
    extra_q, extra_k = band_extras(bands)

    saved, returned = [], []
    arrived = [chunks[0]] + [exchange(chunk) for chunk in chunks[1:]]
    rest = lax.all_gather(rest, everyone, axis=0)
    arrived[0], wq, second = lax.optimization_barrier((arrived[0], wq, second))
    second = lax.all_gather(second, everyone, axis=0)
    wu, wd, wo = unpack(rest, sizes[1:])
    mlp_weights = (wo, wu, wd, gains_full[0][1], b_up_full[0], b_down_full[0])
    for chunk in range(chunk_count):
        x = arrived[chunk]
        if by_clip:
            lens = jnp.broadcast_to(lengths[chunk], (chunk_seqs,))
        else:
            lens = lengths[(position * chunk_seqs + jnp.arange(chunk_seqs)) // bands]
        qkv, gate = time_project(
            x, frame_tables, wq, gates_full[0], gains_full[0][0], b_gate_full[0]
        )
        attended, inverse, probs = time_attend(qkv, lens)
        h1, middle, act, slope = time_mlp(x, attended, gate, mlp_weights)
        saved.append((x, qkv, gate, attended, inverse, probs, middle, act, slope))
        returned.append(exchange(h1))
    if by_clip:
        band_inputs = [h.reshape(bands, rows, width) for h in returned]
    else:
        whole = returned[0].reshape(clips, bands, rows, width)
        band_inputs = [whole[clip] for clip in range(clips)]

    wq1, wu1, wd1, wo1 = unpack(second, sizes)
    consts = (
        (perm, perm.T) + band_tables + (extra_q, extra_k, swap_t, heads, swapped)
        + (wq1, wo1, wu1, wd1, gates_full[1], gains_full[1][0], gains_full[1][1])
        + (b_up_full[1], b_down_full[1], b_gate_full[1])
    )
    final = []
    grads, sums = [], []
    for clip in range(clips):
        done, grad_hidden, *parts = band_layer(
            band_inputs[clip], grad_out, clip, consts, hidden, final
        )
        final = [done]
        grads.append(grad_hidden)
        sums.append(parts)
    band_parts = sums
    b_gate_, b_bias, b_vec, b_gbias = (add_up(t) for t in list(zip(*sums))[4:])
    band_rows = jnp.concatenate([b_vec[2:3], b_vec[1:2], b_vec[0:1], b_gate_[:HEADS]])
    band_vectors = vector_parts(band_rows, b_bias, b_gbias[:, :HEADS])

    if by_clip:
        grads = [g.reshape(groups, chunk_seqs, rows, width) for g in grads]
    else:
        grads = [jnp.concatenate(grads).reshape(groups, chunk_seqs, rows, width)]
    grads = [exchange(g) for g in grads]
    band_sums = flip([parts[:4] for parts in band_parts], devices, BF)
    band_sums, grads[0] = lax.optimization_barrier((band_sums, grads[0]))
    band_sums = lax.psum_scatter(
        band_sums.reshape(-1, width), everyone, scatter_dimension=0, tiled=True
    )
    sums, sums_back, halves = [], [], []
    for chunk in range(chunk_count):
        x, qkv, gate, attended, inverse, probs, middle, act, slope = saved[chunk]
        grad_middle, grad_aug, logit, *parts = time_mlp_back(
            grads[chunk], middle, act, slope, attended, gate, inverse,
            (wo, wu, wd, gains_full[0][1]), (heads, swapped),
        )
        sums.append(parts)
        halves.append((grad_middle, grad_aug, logit))
    last_chunk = chunk_count - 1
    t_bias, t_vec = (add_up(t) for t in list(zip(*sums))[3:])
    mlp_sums = flip([(up, down, out) for down, up, out, _, _ in sums], devices, BF)
    sequences = []
    for chunk in range(chunk_count):
        x, qkv, gate, attended, inverse, probs, middle, act, slope = saved[chunk]
        grad_middle, grad_aug, logit = halves[chunk]
        if chunk == 0:
            mlp_sums, grad_aug = lax.optimization_barrier((mlp_sums, grad_aug))
            mlp_sums = shed_cores(mlp_sums)
        else:
            grad_aug, grad_x = lax.optimization_barrier((grad_aug, grad_x))
        packed_grads = time_attend_back(
            probs, qkv, grad_aug, frame_tables[2], frame_tables[3], swap_t
        )
        if chunk == 0:
            mlp_sums, packed_grads = gain(mlp_sums, packed_grads)
            mlp_sums = shed_chips(mlp_sums)
        if chunk == last_chunk:
            mlp_sums, packed_grads = gain(mlp_sums, packed_grads)
        grad_x, *parts = time_project_back(
            x, packed_grads, logit, grad_middle, (wq, gates_full[0], gains_full[0][0])
        )
        sums_back.append(parts)
        sequences.append(exchange(grad_x).reshape(-1, bands, rows, width))
    t_gate, t_vec0, t_gbias = (add_up(t) for t in list(zip(*sums_back))[1:])
    time_rows = jnp.concatenate([t_vec0, t_vec[1:2], t_vec[0:1], t_gate[:HEADS]])
    time_vectors = vector_parts(time_rows, t_bias, t_gbias[:, :HEADS])
    vectors = jnp.concatenate([time_vectors, band_vectors], axis=1)
    sequences[0], sums_back = lax.optimization_barrier((sequences[0], sums_back))
    last = flip([parts[:1] for parts in sums_back], devices, BF, 6 << 20)
    total = -(-(sizes[0] * width + vectors.shape[1]) // (16 * width)) * 16 - sizes[0]
    vectors = jnp.pad(vectors, ((0, 0), (0, total * width - vectors.shape[1])))
    sequences = [s[k] for s in sequences for k in range(s.shape[0])]
    grad_input = to_frames(sequences[0], 0, clips, perm.T, [])
    last = jnp.concatenate([last, vectors.reshape(devices, total, width)], axis=1)
    last, _ = gain(shed_cores(last), ())
    last, grad_input = gain(shed_chips(last), grad_input)
    last, _ = gain(shed_last(jnp.concatenate([mlp_sums, last], axis=1)), ())
    mlp_sums, last = last[: sum(sizes[1:])], last[sum(sizes[1:]) :]
    grad_input = [grad_input]
    for clip in range(1, clips):
        grad_input = [to_frames(sequences[clip], clip, clips, perm.T, grad_input)]

    tq, vectors = last[: sizes[0]], last[sizes[0] :].reshape(-1)
    bq, bu, bd, bo = cut(band_sums.astype(F32), sizes)
    tu, td, to = cut(mlp_sums, sizes[1:])
    lengths_each = (2 * shard, shard, HEADS * shard, sizes[1], HEADS)
    time_parts = cut(vectors, lengths_each)
    band_parts = cut(vectors[sum(lengths_each) :], lengths_each)
    g_gains, g_b_down, g_gate, g_b_up, g_b_gate = (
        jnp.stack(both) for both in zip(time_parts, band_parts)
    )
    return (
        final[0],
        grad_input[0],
        jnp.stack([tq.T, bq.T]),
        jnp.stack([to, bo]),
        jnp.stack([tu.T, bu.T]),
        g_b_up,
        jnp.stack([td, bd]),
        g_gains.reshape(2, 2, shard),
        g_b_down,
        g_gate.reshape(2, HEADS, shard),
        g_b_gate,
    )


def solution(mesh):
    everyone = ("dp", "fsdp")
    rows = P("fsdp", "dp", None, None)
    last, middle = P(None, None, everyone), P(None, everyone, None)
    return jax.shard_map(
        on_device,
        mesh=mesh,
        in_specs=(
            rows, P("dp"), last, middle, last, P(None, everyone), middle,
            P(None, None, "fsdp"), P(None, "fsdp"), P(None, None, "fsdp"), P(), rows,
        ),
        out_specs=(
            rows, rows, last, middle, last, P(None, everyone), middle,
            P(None, None, "fsdp"), P(None, "fsdp"), P(None, None, "fsdp"), P(),
        ),
        check_vma=False,
    )
```

```python
from functools import partial
import math

import jax
import jax.numpy as jnp
import numpy as np
from jax import lax
from jax.experimental import pallas as pl
from jax.experimental.pallas import tpu as pltpu
from jax.sharding import PartitionSpec as P

HEADS = 8
HEAD_DIM = 64
HALF = HEAD_DIM // 2
HEAD_WIDTH = HEADS * HEAD_DIM
PAIRS = HEADS // 2
LANES = 2 * HEAD_DIM
TILE_FRAMES = 16
EPSILON = 1e-06
NEGATIVE = -1e30
LOG2E = 1.0 / math.log(2.0)
LN2 = math.log(2.0)
QUERY_SCALE = HEAD_DIM**-0.5 * LOG2E
BLOCK_Q = 128
BLOCK_Q_BACK = 256
BAND_FRAMES = 32
ROW_TARGET = 512
MOVE_FRAMES = 64
FLIP_DEVICES = 8

BF = jnp.bfloat16
F32 = jnp.float32


def nn(a, b):
    return jnp.dot(a, b, preferred_element_type=F32)


def nt(a, b):
    return lax.dot_general(a, b, (((1,), (1,)), ((), ())), preferred_element_type=F32)


def tn(a, b):
    return lax.dot_general(a, b, (((0,), (0,)), ((), ())), preferred_element_type=F32)


def rms(hidden):
    scale = lax.rsqrt(jnp.mean(hidden * hidden, axis=-1, keepdims=True) + EPSILON)
    return hidden * scale, scale


def rms_back(unit, scale, gain, grad):
    weighted = grad * gain
    inner = jnp.mean(weighted * unit, axis=-1, keepdims=True)
    return scale * (weighted - unit * inner)


def gelu_pair(up):
    cdf = 0.5 + 0.5 * lax.erf(up * math.sqrt(0.5))
    bell = jnp.exp2((-0.5 * LOG2E) * (up * up))
    return up * cdf, cdf + (up * bell) * (1.0 / math.sqrt(2.0 * math.pi))


def project(normed, w_ext, tables, b_gate):
    cos_q, sin_q, cos_k, sin_k = tables
    width = HEAD_WIDTH
    plain = nt(normed, w_ext[: 2 * width])
    by_weights = w_ext.shape[0] > 4 * width
    swapped = nt(normed, w_ext[4 * width :]) if by_weights else None
    value = nt(normed, w_ext[2 * width : 3 * width]).astype(BF)
    gate = jax.nn.sigmoid(nt(normed, w_ext[3 * width : 4 * width]) + b_gate)
    first_half = lax.broadcasted_iota(jnp.int32, (1, LANES), 1) % HEAD_DIM < HALF
    queries, keys = [], []
    for pair in range(2 * PAIRS):
        at = slice(pair * LANES, (pair + 1) * LANES)
        cos, sin = (cos_q, sin_q) if pair < PAIRS else (cos_k, sin_k)
        own = plain[:, at]
        if by_weights:
            partner = swapped[:, at]
        else:
            partner = jnp.where(
                first_half, pltpu.roll(own, LANES - HALF, 1), pltpu.roll(own, HALF, 1)
            )
        turned = (own * cos + partner * sin).astype(BF)
        (queries if pair < PAIRS else keys).append(turned)
    return queries, keys, value, gate


def attend_pair(query, key_augs, value_ones, extra_q, low, high):
    outs, inverses, kept = [], [], []
    for slot in range(2):
        own, other = (low, high) if slot == 0 else (high, low)
        scores = nt(query * own + extra_q * other, key_augs[slot])
        probs = jnp.exp2(scores - jnp.max(scores, axis=-1, keepdims=True)).astype(BF)
        mixed = nn(probs, value_ones[slot])
        inverse = 1.0 / mixed[:, LANES:]
        outs.append(mixed[:, :LANES] * inverse)
        inverses.append(inverse)
        kept.append(probs)
    is_low = lax.broadcasted_iota(jnp.int32, (1, LANES), 1) < HEAD_DIM
    return outs[0] + outs[1], jnp.where(is_low, *inverses), kept


def pair_operands(keys, values, extra_k, low, high):
    ones = jnp.ones(values.shape, BF)
    key_augs = (keys * low + extra_k * high, keys * high + extra_k * low)
    value_ones = (
        jnp.concatenate([values * low, ones], axis=1),
        jnp.concatenate([values * high, ones], axis=1),
    )
    return key_augs, value_ones


def unrotate(grad, cos, sin, swap_t):
    return grad * cos + nn((grad * sin).astype(BF), swap_t)


def lane_masks():
    lane = lax.broadcasted_iota(jnp.int32, (1, LANES), 1)
    inner = lane % HEAD_DIM
    low = jnp.where(lane < HEAD_DIM, 1.0, 0.0).astype(BF)
    high = jnp.where(lane < HEAD_DIM, 0.0, 1.0).astype(BF)
    picks = tuple(jnp.where(inner == k, 1.0, 0.0).astype(BF) for k in range(2))
    return low, high, picks, inner


def pair_back(probs_of, queries, keys, values, grads, low, high, picks, block_q):
    rows = queries.shape[0]
    query_t = queries.T
    grad_t = (grads[0] * low + grads[1] * high).T
    is_low = lax.broadcasted_iota(jnp.int32, (1, LANES), 1) < HEAD_DIM
    two = picks[0] + picks[1]
    query_parts, key_sums, value_sums = [], [], []
    for slot in range(2):
        own, other = (low, high) if slot == 0 else (high, low)
        value_aug = values * own + two * other
        head = slice(slot * HEAD_DIM, (slot + 1) * HEAD_DIM)
        key_sum = value_sum = None
        parts = []
        for start in range(0, rows, block_q):
            at = slice(start, start + block_q)
            probs = probs_of(slot, at)
            grad_scores = (probs.astype(F32) * nt(grads[slot][at], value_aug)).astype(BF)
            grad_value = nn(grad_t[head, at], probs)
            grad_key = nn(query_t[head, at], grad_scores)
            parts.append(nn(grad_scores, keys))
            key_sum = grad_key if key_sum is None else key_sum + grad_key
            value_sum = grad_value if value_sum is None else value_sum + grad_value
        query_parts.append(parts)
        key_sums.append(key_sum)
        value_sums.append(value_sum)
    blocks = [jnp.where(is_low, *both) for both in zip(*query_parts)]
    grad_query = jnp.concatenate(blocks, axis=0) if len(blocks) > 1 else blocks[0]
    grad_key = jnp.concatenate(key_sums, axis=0).T * LN2
    return grad_query * HEAD_DIM**-0.5, grad_key, jnp.concatenate(value_sums, axis=0).T


def feed_forward(middle, gain, w_up, b_up, w_down, b_down):
    unit, scale = rms(middle)
    normed = (unit * gain).astype(BF)
    act, slope = gelu_pair(nt(normed, w_up) + b_up)
    act, slope = act.astype(BF), slope.astype(BF)
    return middle + (nn(act, w_down) + b_down), normed, unit, scale, act, slope


def branch_back(grad_branch, w_out, attended, gate, inverse, sum_heads, sum_swapped):
    grad_gated = nt(grad_branch, w_out)
    att = attended.astype(F32)
    grad_att = (grad_gated * (gate * inverse)).astype(BF)
    logit_terms = (grad_gated * att * (gate * (1.0 - gate))).astype(BF)
    grad_logit = nn(logit_terms, sum_heads).astype(BF)
    delta = nn((grad_att.astype(F32) * att).astype(BF), sum_swapped)
    return grad_att, grad_logit, delta


def grads_with_delta(grad_att, delta, low, high, picks):
    hi = delta.astype(BF)
    mid = (delta - hi.astype(F32)).astype(BF)
    extra = -(hi * picks[0] + mid * picks[1])
    return grad_att * low + extra * high, grad_att * high + extra * low


def col_sum(values):
    return jnp.sum(values.astype(F32), axis=0, keepdims=True)


def flat(ref):
    value = ref[...]
    return value.reshape(-1, value.shape[-1])


def gather_kernel(perm_ref, x_ref, o_ref):
    for start in range(0, x_ref.shape[0], TILE_FRAMES):
        span = slice(start, start + TILE_FRAMES)
        moved = nn(perm_ref[...], flat(x_ref.at[span])).astype(BF)
        o_ref[:, span] = moved.reshape((-1, TILE_FRAMES) + moved.shape[1:])


def to_sequences(frames, clip, perm):
    rows, _, bands, width = frames.shape
    step = math.gcd(rows, MOVE_FRAMES)
    return pl.pallas_call(
        gather_kernel,
        grid=(rows // step,),
        in_specs=[
            pl.BlockSpec(perm.shape, lambda i: (0, 0)),
            pl.BlockSpec((step, 1, bands, width), lambda i: (i, clip, 0, 0)),
        ],
        out_specs=pl.BlockSpec((bands, step, width), lambda i: (0, i, 0)),
        out_shape=jax.ShapeDtypeStruct((bands, rows, width), BF),
        name="frames_to_sequences",
    )(perm, frames)


def fill_kernel(perm_ref, x_ref, *refs):
    o_ref = refs[-1]
    for start in range(0, o_ref.shape[0], TILE_FRAMES):
        span = slice(start, start + TILE_FRAMES)
        moved = nn(perm_ref[...], flat(x_ref.at[:, span]))
        o_ref[span] = moved.reshape((TILE_FRAMES,) + o_ref.shape[1:])


def to_frames(sequences, clip, clips, perm_back, target):
    bands, rows, width = sequences.shape
    step = math.gcd(rows, MOVE_FRAMES)
    return pl.pallas_call(
        fill_kernel,
        grid=(rows // step,),
        in_specs=[
            pl.BlockSpec(perm_back.shape, lambda i: (0, 0)),
            pl.BlockSpec((bands, step, width), lambda i: (0, i, 0)),
        ]
        + [pl.BlockSpec(memory_space=pl.ANY)] * len(target),
        out_specs=pl.BlockSpec((step, 1, bands, width), lambda i: (i, clip, 0, 0)),
        out_shape=jax.ShapeDtypeStruct((rows, clips, bands, width), F32),
        input_output_aliases={2: 0} if target else {},
        name="sequences_to_frames",
    )(perm_back, sequences, *target)


def operand(const):
    return const[0] if isinstance(const, tuple) else const


def row_count(const):
    return const[0].shape[0] * const[2] if isinstance(const, tuple) else const.shape[0]


def const_spec(array):
    if isinstance(array, tuple):
        array, first, size = array
        block = (array.shape[0], size, array.shape[2])
        return pl.BlockSpec(
            block, lambda *_: (0, first // size, 0), pipeline_mode=pl.Buffered(1)
        )
    zeros = (0,) * array.ndim
    return pl.BlockSpec(array.shape, lambda *_: zeros, pipeline_mode=pl.Buffered(1))


def cost(rows, per_row, nbytes):
    return pl.CostEstimate(flops=int(2 * rows * per_row), bytes_accessed=nbytes, transcendentals=0)


def params(megabytes, semantics=None):
    return pltpu.CompilerParams(vmem_limit_bytes=megabytes << 20, dimension_semantics=semantics)


def extend_weights(w_ref, wg_ref, scratch):
    width = HEAD_WIDTH
    w_ref = flat(w_ref)
    scratch[: 3 * width] = w_ref
    gates = wg_ref[...].astype(F32)
    for head in range(HEADS):
        at = 3 * width + head * HEAD_DIM
        row = jnp.broadcast_to(gates[head : head + 1], (HEAD_DIM, gates.shape[1]))
        scratch[at : at + HEAD_DIM] = row.astype(BF)
    if scratch.shape[0] > 4 * width:
        for start in range(0, 2 * width, HEAD_DIM):
            at = 4 * width + start
            scratch[at : at + HALF] = -w_ref[start + HALF : start + HEAD_DIM]
            scratch[at + HALF : at + HEAD_DIM] = w_ref[start : start + HALF]


def project_kernel(
    x_ref, cq, sq, ck, sk, wq_ref, wg_ref, gain_ref, bg_ref, qkv_ref, gate_ref, w_ref
):
    seqs = x_ref.shape[1]

    @pl.when(pl.program_id(0) == 0)
    def _():
        extend_weights(wq_ref, wg_ref, w_ref)

    unit, _ = rms(flat(x_ref).astype(F32))
    normed = (unit * gain_ref[...]).astype(BF)

    def table(ref):
        value = ref[...]
        if seqs > 1:
            value = jnp.broadcast_to(value[:, None], (value.shape[0], seqs) + value.shape[1:])
        return value.reshape(-1, LANES)

    queries, keys, value, gate = project(
        normed, w_ref, (table(cq), table(sq), table(ck), table(sk)), bg_ref[...]
    )
    lead = qkv_ref.shape[:-1]
    for pair, tensor in enumerate(queries + keys):
        qkv_ref[..., pair * LANES : (pair + 1) * LANES] = tensor.reshape(lead + (LANES,))
    qkv_ref[..., 2 * HEAD_WIDTH :] = value.reshape(lead + (HEAD_WIDTH,))
    gate_ref[...] = gate.astype(gate_ref.dtype).reshape(gate_ref.shape)


def source_block(groups, seqs, rows, target):
    block = max(1, target // (seqs * rows))
    return math.gcd(groups, block)


def time_project(x, tables, wq, wg, gain, b_gate):
    groups, seqs, rows, width = x.shape
    sb = source_block(groups, seqs, rows, ROW_TARGET)

    def rows_spec(lanes):
        return pl.BlockSpec((sb, seqs, rows, lanes), lambda i: (i, 0, 0, 0))

    table_spec = pl.BlockSpec((sb, rows, LANES), lambda i: (i, 0, 0))
    return pl.pallas_call(
        project_kernel,
        grid=(groups // sb,),
        in_specs=[rows_spec(width)]
        + [table_spec] * 4
        + [const_spec(wq), const_spec(wg), const_spec(gain), const_spec(b_gate)],
        out_specs=[rows_spec(3 * HEAD_WIDTH), rows_spec(HEAD_WIDTH)],
        scratch_shapes=[pltpu.VMEM((4 * HEAD_WIDTH, width), BF)],
        out_shape=[
            jax.ShapeDtypeStruct((groups, seqs, rows, 3 * HEAD_WIDTH), BF),
            jax.ShapeDtypeStruct((groups, seqs, rows, HEAD_WIDTH), BF),
        ],
        compiler_params=params(56),
        cost_estimate=cost(groups * seqs * rows, 4 * HEAD_WIDTH * width * 3, 1 << 20),
        name="time_project",
    )(x, *tables, wq, wg, gain, b_gate)


def time_attend_kernel(len_ref, q_ref, k_ref, v_ref, att_ref, inv_ref, p_ref):
    low, high, _, inner = lane_masks()
    keys, values, queries = flat(k_ref), flat(v_ref), flat(q_ref)
    rows = keys.shape[0]
    position = lax.broadcasted_iota(jnp.int32, (rows, LANES), 0)
    beyond = position >= len_ref[pl.program_id(0)]
    extra_k = jnp.where((inner == 0) & beyond, NEGATIVE, 0.0).astype(BF)
    extra_q = jnp.where(inner == 0, 1.0, 0.0).astype(BF)
    block = math.gcd(rows, BLOCK_Q)
    per_source = q_ref.shape[2]
    key_augs, value_ones = pair_operands(keys, values, extra_k, low, high)
    for start in range(0, rows, block):
        at = slice(start, start + block)
        src = slice(start // per_source, (start + block) // per_source)
        shape = (block // per_source, 1, per_source, LANES)
        out, inverse, kept = attend_pair(queries[at], key_augs, value_ones, extra_q, low, high)
        for slot in range(2):
            p_ref[0, slot, at] = kept[slot]
        att_ref[src] = out.astype(BF).reshape(shape)
        inv_ref[src] = inverse.reshape(shape)


def time_attend(qkv, lens):
    groups, seqs, rows, _ = qkv.shape
    frames = groups * rows

    def spec(first):
        return pl.BlockSpec((groups, 1, rows, LANES), lambda s, p, *_: (0, s, 0, first + p))

    return pl.pallas_call(
        time_attend_kernel,
        grid_spec=pltpu.PrefetchScalarGridSpec(
            num_scalar_prefetch=1,
            grid=(seqs, PAIRS),
            in_specs=[spec(0), spec(PAIRS), spec(2 * PAIRS)],
            out_specs=[
                spec(0),
                spec(0),
                pl.BlockSpec((1, 2, frames, frames), lambda s, p, *_: (s, p, 0, 0)),
            ],
        ),
        out_shape=[
            jax.ShapeDtypeStruct((groups, seqs, rows, HEAD_WIDTH), BF),
            jax.ShapeDtypeStruct((groups, seqs, rows, HEAD_WIDTH), F32),
            jax.ShapeDtypeStruct((seqs, HEADS, frames, frames), BF),
        ],
        compiler_params=params(60),
        cost_estimate=cost(
            groups * seqs * rows, groups * rows * HEADS * 2 * 256 * 2, 1 << 20
        ),
        name="time_attend",
    )(lens, qkv, qkv, qkv)


def time_mlp_kernel(
    x_ref, att_ref, gate_ref, wo, wu, wd, gain, bu, bd, h_ref, mid_ref, act_ref, slope_ref
):
    gated = (flat(att_ref).astype(F32) * flat(gate_ref).astype(F32)).astype(BF)
    middle = flat(x_ref).astype(F32) + nn(gated, flat(wo))
    result, _, _, _, act, slope = feed_forward(
        middle, gain[...], flat(wu), bu[...], flat(wd), bd[...]
    )
    h_ref[...] = result.astype(BF).reshape(h_ref.shape)
    mid_ref[...] = middle.reshape(mid_ref.shape)
    act_ref[...] = act.reshape(act_ref.shape)
    slope_ref[...] = slope.reshape(slope_ref.shape)


def time_mlp(x, attended, gate, weights):
    groups, seqs, rows, width = x.shape
    hidden = row_count(weights[1])
    sb = source_block(groups, seqs, rows, ROW_TARGET)

    def rows_spec(lanes):
        return pl.BlockSpec((sb, seqs, rows, lanes), lambda i: (i, 0, 0, 0))

    def out(lanes, dtype):
        return jax.ShapeDtypeStruct((groups, seqs, rows, lanes), dtype)

    return pl.pallas_call(
        time_mlp_kernel,
        grid=(groups // sb,),
        in_specs=[rows_spec(width), rows_spec(HEAD_WIDTH), rows_spec(HEAD_WIDTH)]
        + [const_spec(w) for w in weights],
        out_specs=[rows_spec(width), rows_spec(width), rows_spec(hidden), rows_spec(hidden)],
        out_shape=[out(width, BF), out(width, F32), out(hidden, BF), out(hidden, BF)],
        compiler_params=params(56),
        cost_estimate=cost(groups * seqs * rows, width * (HEAD_WIDTH + 2 * hidden) * 3, 1 << 20),
        name="time_mlp",
    )(x, attended, gate, *map(operand, weights))


def accumulate(first, pairs):
    @pl.when(first)
    def _():
        for ref, _ in pairs:
            ref[...] = jnp.zeros_like(ref)

    for ref, value in pairs:
        ref[...] += value


def time_mlp_back_kernel(
    g_ref, mid_ref, act_ref, slope_ref, att_ref, gate_ref, inv_ref,
    wo, wu, wd, gain_ref, heads, swapped,
    gmid_ref, gatt_ref, logit_ref, a_down, a_up, a_out, a_bias, a_vec,
):
    first = pl.program_id(0) == 0
    gain = gain_ref[...]
    grad_last = flat(g_ref)
    act = flat(act_ref)
    grad_up = (nt(grad_last, flat(wd)) * flat(slope_ref).astype(F32)).astype(BF)
    unit, scale = rms(flat(mid_ref))
    normed = (unit * gain).astype(BF)
    grad_normed = nn(grad_up, flat(wu))
    gradient = grad_last.astype(F32)
    grad_middle = gradient + rms_back(unit, scale, gain, grad_normed)
    grad_branch = grad_middle.astype(BF)
    att = flat(att_ref)
    gate = flat(gate_ref).astype(F32)
    gated = (att.astype(F32) * gate).astype(BF)
    grad_att, grad_logit, delta = branch_back(
        grad_branch, flat(wo), att, gate, flat(inv_ref), heads[...], swapped[...]
    )
    low, high, picks, _ = lane_masks()
    lead = gatt_ref.shape[:-1]
    for pair in range(PAIRS):
        at = slice(pair * LANES, (pair + 1) * LANES)
        both = grads_with_delta(grad_att[:, at], delta[:, at], low, high, picks)
        for slot in range(2):
            where = 2 * pair + slot
            gatt_ref[..., where * LANES : (where + 1) * LANES] = both[slot].reshape(lead + (LANES,))
    gmid_ref[...] = grad_middle.reshape(gmid_ref.shape)
    logit_ref[...] = grad_logit.reshape(logit_ref.shape)
    vec = jnp.concatenate([col_sum(gradient), col_sum(grad_normed * unit)], axis=0)
    accumulate(
        first,
        (
            (a_down, tn(grad_last, act)),
            (a_up, tn(normed, grad_up)),
            (a_out, tn(grad_branch, gated)),
            (a_bias, col_sum(grad_up)),
            (a_vec, vec),
        ),
    )


def sum_shapes(*shapes):
    return [jax.ShapeDtypeStruct(shape, F32) for shape in shapes]


def time_mlp_back(grad, middle, act, slope, attended, gate, inverse, weights, sums):
    groups, seqs, rows, width = grad.shape
    hidden = act.shape[-1]
    sb = source_block(groups, seqs, rows, ROW_TARGET)

    def rows_spec(lanes):
        return pl.BlockSpec((sb, seqs, rows, lanes), lambda i: (i, 0, 0, 0))

    def out(lanes, dtype):
        return jax.ShapeDtypeStruct((groups, seqs, rows, lanes), dtype)

    consts = tuple(weights) + tuple(sums)
    starts = sum_shapes((width, hidden), (width, hidden), (width, HEAD_WIDTH), (1, hidden), (2, width))
    return pl.pallas_call(
        time_mlp_back_kernel,
        grid=(groups // sb,),
        in_specs=[rows_spec(width), rows_spec(width), rows_spec(hidden), rows_spec(hidden)]
        + [rows_spec(HEAD_WIDTH)] * 3
        + [const_spec(w) for w in consts],
        out_specs=[rows_spec(width), rows_spec(2 * HEAD_WIDTH), rows_spec(LANES)]
        + [const_spec(s) for s in starts],
        out_shape=[out(width, F32), out(2 * HEAD_WIDTH, BF), out(LANES, BF)]
        + starts,
        compiler_params=params(60),
        cost_estimate=cost(groups * seqs * rows, width * (HEAD_WIDTH + 2 * hidden) * 5, 1 << 20),
        name="time_mlp_back",
    )(grad, middle, act, slope, attended, gate, inverse, *map(operand, consts))


def time_attend_back_kernel(
    p_ref, q_ref, k_ref, v_ref, gatt_ref, cos_ref, sin_ref, swap_ref, dq_ref, dk_ref, dv_ref
):
    low, high, picks, _ = lane_masks()
    grads = flat(gatt_ref)
    grad_query, grad_key, grad_value = pair_back(
        lambda slot, at: p_ref[0, slot, at],
        flat(q_ref),
        flat(k_ref),
        flat(v_ref),
        (grads[:, :LANES], grads[:, LANES:]),
        low,
        high,
        picks,
        math.gcd(grads.shape[0], BLOCK_Q_BACK),
    )
    cos, sin, swap_t = flat(cos_ref), flat(sin_ref), swap_ref[...]
    dq_ref[...] = unrotate(grad_query, cos, sin, swap_t).astype(BF).reshape(dq_ref.shape)
    dk_ref[...] = unrotate(grad_key, cos, sin, swap_t).astype(BF).reshape(dk_ref.shape)
    dv_ref[...] = grad_value.astype(BF).reshape(dv_ref.shape)


def time_attend_back(probs, qkv, grad_aug, cos, sin, swap_t):
    groups, seqs, rows, _ = qkv.shape
    frames = groups * rows

    def spec(lanes, first):
        return pl.BlockSpec((groups, 1, rows, lanes), lambda s, p: (0, s, 0, first + p))

    out = jax.ShapeDtypeStruct((groups, seqs, rows, HEAD_WIDTH), BF)
    return pl.pallas_call(
        time_attend_back_kernel,
        grid=(seqs, PAIRS),
        in_specs=[
            pl.BlockSpec((1, 2, frames, frames), lambda s, p: (s, p, 0, 0)),
            spec(LANES, 0),
            spec(LANES, PAIRS),
            spec(LANES, 2 * PAIRS),
            spec(2 * LANES, 0),
            const_spec(cos),
            const_spec(sin),
            const_spec(swap_t),
        ],
        out_specs=[spec(LANES, 0)] * 3,
        out_shape=[out] * 3,
        compiler_params=params(60),
        cost_estimate=cost(
            groups * seqs * rows, groups * rows * HEADS * 5 * 256 * 3 // 2, 1 << 20
        ),
        name="time_attend_back",
    )(probs, qkv, qkv, qkv, grad_aug, cos, sin, swap_t)


def time_project_back_kernel(
    x_ref, dq_ref, dk_ref, dv_ref, logit_ref, gmid_ref,
    wq, wg, gain_ref,
    gx_ref, a_qkv, a_gate, a_vec, a_bias,
):
    gain = gain_ref[...]
    unit, scale = rms(flat(x_ref).astype(F32))
    normed = (unit * gain).astype(BF)
    packed = jnp.concatenate([flat(dq_ref), flat(dk_ref), flat(dv_ref)], axis=1)
    logit = flat(logit_ref)
    grad_normed = nn(packed, wq[...]) + nn(logit, wg[...])
    grad_x = flat(gmid_ref) + rms_back(unit, scale, gain, grad_normed)
    gx_ref[...] = grad_x.astype(BF).reshape(gx_ref.shape)
    accumulate(
        pl.program_id(0) == 0,
        (
            (a_qkv, tn(normed, packed)),
            (a_gate, tn(logit, normed)),
            (a_vec, col_sum(grad_normed * unit)),
            (a_bias, col_sum(logit)),
        ),
    )


def time_project_back(x, grads, logit, grad_middle, weights):
    groups, seqs, rows, width = x.shape
    starts = sum_shapes((width, 3 * HEAD_WIDTH), (LANES, width), (1, width), (1, LANES))
    sb = source_block(groups, seqs, rows, ROW_TARGET)

    def rows_spec(lanes):
        return pl.BlockSpec((sb, seqs, rows, lanes), lambda i: (i, 0, 0, 0))

    consts = tuple(weights)
    return pl.pallas_call(
        time_project_back_kernel,
        grid=(groups // sb,),
        in_specs=[rows_spec(width)]
        + [rows_spec(HEAD_WIDTH)] * 3
        + [rows_spec(LANES), rows_spec(width)]
        + [const_spec(w) for w in consts],
        out_specs=[rows_spec(width)] + [const_spec(s) for s in starts],
        out_shape=[jax.ShapeDtypeStruct((groups, seqs, rows, width), BF)]
        + starts,
        compiler_params=params(60),
        cost_estimate=cost(groups * seqs * rows, width * 6 * HEAD_WIDTH * 5 // 2, 1 << 20),
        name="time_project_back",
    )(x, *grads, logit, grad_middle, *consts)


def band_kernel(
    h_ref, g_ref, perm_ref, back_ref, cq, sq, ck, sk, exq_ref, exk_ref, swap_ref, heads, swapped,
    wq, wo, wu, wd, wg, gain0_ref, gain1_ref, bu, bd, bg,
    *refs,
):
    out_ref, gh_ref, a_qkv, a_up, a_down, a_out, a_gate, a_bias, a_vec, a_gbias, w_ext = refs[-11:]
    first = pl.program_id(0) == 0

    @pl.when(first)
    def _():
        extend_weights(wq, wg, w_ext)

    gain0, gain1 = gain0_ref[...], gain1_ref[...]
    low, high, picks, _ = lane_masks()
    bands, frames, _ = h_ref.shape
    spans = [slice(k, k + TILE_FRAMES) for k in range(0, frames, TILE_FRAMES)]
    size = bands * TILE_FRAMES
    tiles = [slice(k * size, (k + 1) * size) for k in range(len(spans))]

    def stacked(values, axis=0):
        return values[0] if len(values) == 1 else jnp.concatenate(values, axis=axis)

    def table(ref):
        return stacked([ref[...]] * len(spans))

    hidden = stacked([flat(h_ref.at[:, span]) for span in spans]).astype(F32)
    unit0, scale0 = rms(hidden)
    normed0 = (unit0 * gain0).astype(BF)
    queries, keys, value, gate = project(
        normed0, w_ext, (table(cq), table(sq), table(ck), table(sk)), bg[...]
    )
    extra_q, extra_k = exq_ref[...], exk_ref[...]
    attended, inverse, kept = [], [], []
    for tile in tiles:
        outs, inverses = [], []
        for pair in range(PAIRS):
            at = slice(pair * LANES, (pair + 1) * LANES)
            key_augs, value_ones = pair_operands(
                keys[pair][tile], value[tile, at], extra_k, low, high
            )
            out, one_over, probs = attend_pair(
                queries[pair][tile], key_augs, value_ones, extra_q, low, high
            )
            outs.append(out.astype(BF))
            inverses.append(one_over)
            kept.append(probs)
        attended.append(jnp.concatenate(outs, axis=1))
        inverse.append(jnp.concatenate(inverses, axis=1))
    attended, inverse = stacked(attended), stacked(inverse)
    gated = (attended.astype(F32) * gate).astype(BF)
    middle = hidden + nn(gated, flat(wo))
    result, normed1, unit1, scale1, act, slope = feed_forward(
        middle, gain1, flat(wu), bu[...], flat(wd), bd[...]
    )
    result = result.astype(BF)
    gradient = []
    for span, tile in zip(spans, tiles):
        out = nn(back_ref[...], result[tile]).astype(BF)
        out_ref[span] = out.reshape((TILE_FRAMES,) + out_ref.shape[1:])
        gradient.append(nn(perm_ref[...], flat(g_ref.at[span])))
    gradient = stacked(gradient)
    grad_last = gradient.astype(BF)
    grad_up = (nt(grad_last, flat(wd)) * slope.astype(F32)).astype(BF)
    grad_normed1 = nn(grad_up, flat(wu))
    grad_middle = gradient + rms_back(unit1, scale1, gain1, grad_normed1)
    grad_branch = grad_middle.astype(BF)
    grad_att, grad_logit, delta = branch_back(
        grad_branch, flat(wo), attended, gate, inverse, heads[...], swapped[...]
    )
    swap_t = swap_ref[...]
    packed = []
    for index, tile in enumerate(tiles):
        grads_q, grads_k, grads_v = [], [], []
        for pair in range(PAIRS):
            at = slice(pair * LANES, (pair + 1) * LANES)
            both = grads_with_delta(grad_att[tile, at], delta[tile, at], low, high, picks)
            grad_query, grad_key, grad_value = pair_back(
                lambda slot, _, probs=kept[index * PAIRS + pair]: probs[slot],
                queries[pair][tile], keys[pair][tile], value[tile, at], both,
                low, high, picks, size,
            )
            grads_q.append(unrotate(grad_query, ck[...], sk[...], swap_t).astype(BF))
            grads_k.append(unrotate(grad_key, ck[...], sk[...], swap_t).astype(BF))
            grads_v.append(grad_value.astype(BF))
        packed.append(jnp.concatenate(grads_q + grads_k + grads_v, axis=1))
    packed = stacked(packed)
    width = HEAD_WIDTH
    grad_normed0 = (
        nn(packed, w_ext[: 3 * width])
        + nn(grad_logit, wg[...])
    )
    grad_hidden = grad_middle + rms_back(unit0, scale0, gain0, grad_normed0)
    for span, tile in zip(spans, tiles):
        gh_ref[:, span] = grad_hidden[tile].astype(BF).reshape(bands, TILE_FRAMES, -1)
    vec = jnp.concatenate(
        [col_sum(gradient), col_sum(grad_normed1 * unit1), col_sum(grad_normed0 * unit0)], axis=0
    )
    accumulate(
        first,
        (
            (a_qkv, tn(normed0, packed)),
            (a_up, tn(normed1, grad_up)),
            (a_down, tn(grad_last, act)),
            (a_out, tn(grad_branch, gated)),
            (a_gate, tn(grad_logit, normed0)),
            (a_bias, col_sum(grad_up)),
            (a_vec, vec),
            (a_gbias, col_sum(grad_logit)),
        ),
    )


def band_layer(hidden, grad_out, clip, consts, inner, final):
    bands, rows, width = hidden.shape
    consts = tuple(consts)
    starts = sum_shapes(
        (width, 3 * HEAD_WIDTH), (width, inner), (width, inner), (width, HEAD_WIDTH),
        (LANES, width), (1, inner), (3, width), (1, LANES),
    )
    frames = math.gcd(rows, BAND_FRAMES)
    seq_spec = pl.BlockSpec((bands, frames, width), lambda i: (0, i, 0))
    frame_spec = pl.BlockSpec((frames, 1, bands, width), lambda i: (i, clip, 0, 0))
    return pl.pallas_call(
        band_kernel,
        grid=(rows // frames,),
        in_specs=[seq_spec, frame_spec]
        + [const_spec(c) for c in consts]
        + [pl.BlockSpec(memory_space=pl.ANY)] * len(final),
        out_specs=[frame_spec, seq_spec] + [const_spec(s) for s in starts],
        out_shape=[
            jax.ShapeDtypeStruct(grad_out.shape, BF),
            jax.ShapeDtypeStruct((bands, rows, width), BF),
        ]
        + starts,
        scratch_shapes=[pltpu.VMEM((6 * HEAD_WIDTH, width), BF)],
        input_output_aliases={2 + len(consts): 0} if final else {},
        compiler_params=params(62),
        cost_estimate=cost(bands * rows, width * (4 * HEAD_WIDTH + 2 * inner) * 13, 1 << 20),
        name="band_layer",
    )(hidden, grad_out, *map(operand, consts), *final)


def flip_kernel(terms, *refs):
    target, start = refs[-1], 0
    count = (len(refs) - 1) // terms
    devices, _, width = target.shape
    for index in range(count):
        total = refs[index][...]
        for term in range(1, terms):
            total = total + refs[term * count + index][...]
        size = total.shape[1] // devices
        rows = total.T.astype(target.dtype).reshape(devices, size, width)
        target[:, start : start + size] = rows
        start += size


def flip(groups, devices, dtype, weight=256):
    width = groups[0][0].shape[0]
    sizes = [array.shape[1] // devices for array in groups[0]]
    if any(size % 16 for size in sizes):
        parts = [add_up(list(arrays)).T.astype(dtype) for arrays in zip(*groups)]
        return jnp.concatenate([p.reshape(devices, -1, width) for p in parts], axis=1)
    each = math.gcd(devices, FLIP_DEVICES)
    arrays = [array for group in groups for array in group]
    return pl.pallas_call(
        partial(flip_kernel, len(groups)),
        grid=(devices // each,),
        in_specs=[
            pl.BlockSpec((width, each * (array.shape[1] // devices)), lambda i: (0, i))
            for array in arrays
        ],
        out_specs=pl.BlockSpec((each, sum(sizes), width), lambda i: (i, 0, 0)),
        out_shape=jax.ShapeDtypeStruct((devices, sum(sizes), width), dtype),
        compiler_params=params(56),
        cost_estimate=cost(4096, weight, 1 << 20),
        name="flip_sums",
    )(*arrays)


def add_up(arrays):
    return sum(arrays[1:], arrays[0])


def rotary_tables(positions):
    steps = np.exp(np.arange(HALF, dtype=np.float32) * np.float32(-math.log(10000.0) / HALF))
    angles = positions.astype(np.float32)[:, None] * steps[None, :]
    cos = np.tile(np.cos(angles), (1, LANES // HALF)).astype(np.float32)
    sin = np.tile(np.sin(angles), (1, LANES // HALF)).astype(np.float32)
    scale = np.float32(QUERY_SCALE)
    return cos * scale, sin * scale, cos, sin


def signed(tables):
    sign = np.where(np.arange(LANES) % HEAD_DIM < HALF, -1.0, 1.0).astype(np.float32)
    cos_q, sin_q, cos_k, sin_k = tables
    return cos_q, sin_q * sign, cos_k, sin_k * sign


def tile_permutation(bands):
    rows = bands * TILE_FRAMES
    row = np.arange(rows)
    source = (row % TILE_FRAMES) * bands + row // TILE_FRAMES
    return (source[:, None] == row[None, :]).astype(BF)


def head_sums():
    lane = np.arange(HEAD_WIDTH)
    heads = (lane[:, None] // HEAD_DIM == np.arange(LANES)[None, :]).astype(BF)
    swapped = (lane[:, None] // HEAD_DIM == (lane[None, :] // HEAD_DIM) ^ 1).astype(BF)
    return heads, swapped


def swap_matrix():
    lane = np.arange(LANES)
    same = lane[:, None] // HEAD_DIM == lane[None, :] // HEAD_DIM
    i, j = lane[:, None] % HEAD_DIM, lane[None, :] % HEAD_DIM
    forward = np.where(j == i + HALF, 1.0, 0.0) + np.where(j == i - HALF, -1.0, 0.0)
    return np.where(same, forward, 0.0).T.astype(BF)


def band_extras(bands):
    rows = bands * TILE_FRAMES
    frame = np.arange(rows) % TILE_FRAMES
    inner = np.arange(LANES) % HEAD_DIM
    mine = inner[None, :] == frame[:, None]
    slot = inner < TILE_FRAMES
    extra_k = np.where(slot[None, :] & ~mine, NEGATIVE, 0.0)
    return mine.astype(BF), extra_k.astype(BF)


def xor_pairs(count, bit):
    return [(i, i ^ bit) for i in range(count)]


def gather_first(block, split, unpack, chunks, send):
    chunk, later = chunks[0], chunks[1:]
    steps = []
    for axis in ("fsdp", "dp"):
        size = lax.axis_size(axis)
        bits = [1 << k for k in range(1, size.bit_length() - 1)] + [1]
        steps += [(axis, bit) for bit in bits if bit < size]

    def double(tensor, axis, bit):
        other = lax.ppermute(tensor, axis, xor_pairs(lax.axis_size(axis), bit))
        mine_first = (lax.axis_index(axis) // bit) % 2 == 0
        return jnp.stack(
            [jnp.where(mine_first, tensor, other), jnp.where(mine_first, other, tensor)]
        )

    order = list(reversed(steps))
    wanted = sorted(range(len(order)), key=lambda k: (order[k][0] != "dp", -order[k][1]))

    def arrange(tensor):
        rank = len(order)
        tensor = tensor.transpose(*wanted, rank, rank + 1)
        return tensor.reshape((lax.axis_size("dp"), lax.axis_size("fsdp")) + tensor.shape[-2:])

    tensor = block
    for index, (axis, bit) in enumerate(steps[:-1]):
        tensor = double(tensor, axis, bit)
        if index == 1:
            tensor, chunk = lax.optimization_barrier((tensor, chunk))
            chunk = send(chunk)
        if index == 2:
            tensor, later = lax.optimization_barrier((tensor, later))
    rest = unpack(arrange(double(tensor[..., split:, :], *steps[-1])))
    tensor, chunk, rest = lax.optimization_barrier((tensor[..., :split, :], chunk, rest))
    return arrange(double(tensor, *steps[-1])), rest, [chunk] + later


def after(tensors, done):
    return lax.optimization_barrier((tensors, done))[0]


def pick(tensor, index):
    return lax.dynamic_index_in_dim(tensor, index, 0, keepdims=False)


def shed(tensor, place, axis, unit):
    parts = [
        lax.ppermute(
            pick(tensor, place ^ step), axis, xor_pairs(lax.axis_size(axis), step * unit)
        )
        for step in range(1, tensor.shape[0])
    ]
    return pick(tensor, place), parts


def gain(pending, before):
    own, parts = pending
    parts, before = lax.optimization_barrier((parts, before))
    total = own.astype(F32)
    for part in parts:
        total = total + part.astype(F32)
    return total, before


def shed_cores(blocks):
    dp, groups = lax.axis_size("dp"), lax.axis_size("fsdp")
    tensor = blocks.astype(BF).reshape((dp // 2, 2, groups) + blocks.shape[1:]).swapaxes(0, 1)
    return shed(tensor, lax.axis_index("dp") % 2, "dp", 1)


def shed_chips(total):
    return shed(total.astype(BF), lax.axis_index("dp") // 2, "dp", 2)


def shed_last(total):
    return shed(total.astype(BF), lax.axis_index("fsdp"), "fsdp", 1)


def vector_parts(rows, bias, gate_bias):
    dp, groups = lax.axis_size("dp"), lax.axis_size("fsdp")
    devices, count, shard = dp * groups, rows.shape[0], rows.shape[1] // groups
    own = rows.reshape(count, groups, shard).swapaxes(0, 1).reshape(1, groups, count * shard)
    own = jnp.broadcast_to(own, (dp, groups, count * shard)).reshape(devices, -1)
    gate_bias = jnp.broadcast_to(gate_bias, (devices, gate_bias.shape[-1]))
    return jnp.concatenate([own, bias.reshape(devices, -1), gate_bias], axis=1).astype(BF)


def cut(tensor, sizes):
    parts, start = [], 0
    for size in sizes:
        parts.append(tensor[start : start + size])
        start += size
    return parts


def on_device(
    frames_in, lengths, w_qkv, w_out, w_up, b_up, w_down, gains, b_down, w_gate, b_gate, grad_out
):
    rows, clips, bands, width = frames_in.shape
    dp, groups = lax.axis_size("dp"), lax.axis_size("fsdp")
    position = lax.axis_index("fsdp")
    everyone = ("dp", "fsdp")
    devices, shard = dp * groups, width // groups
    hidden = w_up.shape[2] * devices
    seq_count = clips * bands // groups
    by_clip = bands % groups == 0
    chunk_count = clips if by_clip else 1
    chunk_seqs = seq_count // chunk_count

    wq_t, wu_t = w_qkv.swapaxes(1, 2), w_up.swapaxes(1, 2)
    sizes = [wq_t.shape[1], wu_t.shape[1], w_down.shape[1], w_out.shape[1]]
    small = jnp.concatenate(
        [gains.reshape(-1), b_down.reshape(-1), w_gate.reshape(-1), b_up.reshape(-1)]
    )
    total = -(-(sizes[0] * width + small.shape[0]) // (16 * width)) * 16
    small_rows = total - sizes[0]
    small = jnp.pad(small, (0, small_rows * width - small.shape[0])).reshape(-1, width)
    perm = tile_permutation(bands)
    clip_seqs = [to_sequences(frames_in, clip, perm) for clip in range(clips)]
    first = after(jnp.concatenate([wq_t[0], small], axis=0), clip_seqs[0])
    if by_clip:
        chunks = [seqs.reshape(groups, chunk_seqs, rows, width) for seqs in clip_seqs]
    else:
        chunks = [jnp.concatenate(clip_seqs).reshape(groups, chunk_seqs, rows, width)]
    def exchange(tensor):
        return lax.all_to_all(tensor, "fsdp", split_axis=0, concat_axis=0, tiled=True)

    def unpack_small(small):
        small = small.reshape(dp, groups, -1)
        vector_count = 4 + 2 + 2 * HEADS
        vectors = small[0, :, : vector_count * shard].reshape(groups, vector_count, shard)
        vectors = vectors.swapaxes(0, 1).reshape(vector_count, width)
        gates = jnp.pad(
            vectors[6:].reshape(2, HEADS, width), ((0, 0), (0, LANES - HEADS), (0, 0))
        )
        bias = small[:, :, vector_count * shard :][:, :, : 2 * sizes[1]]
        bias = bias.reshape(devices, 2, -1).swapaxes(0, 1).reshape(2, 1, -1).astype(F32)
        return (
            [[vectors[2 * t + k].reshape(1, width).astype(F32) for k in range(2)] for t in range(2)],
            [vectors[4 + t].reshape(1, width).astype(F32) for t in range(2)],
            [gates[t] for t in range(2)],
            [bias[t] for t in range(2)],
            [jnp.repeat(b_gate[t].astype(F32), HEAD_DIM)[None] for t in range(2)],
        )

    wq, small, chunks = gather_first(first, sizes[0], unpack_small, chunks, exchange)
    wq = wq.reshape(-1, width)
    gains_full, b_down_full, gates_full, b_up_full, b_gate_full = small

    def unpack(gathered, parts):
        start, found = 0, []
        for size in parts:
            if size % 16 or start % size:
                found.append(gathered[:, start : start + size].reshape(-1, width))
            else:
                found.append((gathered, start, size))
            start += size
        return found

    rest = after((w_up, w_down, w_out), clip_seqs[0])
    rest = jnp.concatenate([rest[0].swapaxes(1, 2)[0], rest[1][0], rest[2][0]], axis=0)
    second = jnp.concatenate([wq_t[1], wu_t[1], w_down[1], w_out[1]], axis=0)

    heads, swapped = head_sums()
    swap_t = swap_matrix()
    frame_tables = rotary_tables(np.arange(groups * rows))
    frame_tables = tuple(t.reshape(groups, rows, LANES) for t in frame_tables)
    signed_tables = signed(frame_tables)
    band_tables = rotary_tables(np.arange(bands * TILE_FRAMES) // TILE_FRAMES)
    extra_q, extra_k = band_extras(bands)

    saved, returned = [], []
    arrived = [chunks[0]] + [exchange(chunk) for chunk in chunks[1:]]
    rest = lax.all_gather(rest, everyone, axis=0)
    arrived[0], wq, second = lax.optimization_barrier((arrived[0], wq, second))
    second = lax.all_gather(second, everyone, axis=0)
    wu, wd, wo = unpack(rest, sizes[1:])
    mlp_weights = (wo, wu, wd, gains_full[0][1], b_up_full[0], b_down_full[0])
    for chunk in range(chunk_count):
        x = arrived[chunk]
        if by_clip:
            lens = jnp.broadcast_to(lengths[chunk], (chunk_seqs,))
        else:
            lens = lengths[(position * chunk_seqs + jnp.arange(chunk_seqs)) // bands]
        qkv, gate = time_project(
            x, signed_tables, wq, gates_full[0], gains_full[0][0], b_gate_full[0]
        )
        attended, inverse, probs = time_attend(qkv, lens)
        h1, middle, act, slope = time_mlp(x, attended, gate, mlp_weights)
        saved.append((x, qkv, gate, attended, inverse, probs, middle, act, slope))
        returned.append(exchange(h1))
    if by_clip:
        band_inputs = [h.reshape(bands, rows, width) for h in returned]
    else:
        whole = returned[0].reshape(clips, bands, rows, width)
        band_inputs = [whole[clip] for clip in range(clips)]

    wq1, wu1, wd1, wo1 = unpack(second, sizes)
    consts = (
        (perm, perm.T) + band_tables + (extra_q, extra_k, swap_t, heads, swapped)
        + (wq1, wo1, wu1, wd1, gates_full[1], gains_full[1][0], gains_full[1][1])
        + (b_up_full[1], b_down_full[1], b_gate_full[1])
    )
    final = []
    grads, sums = [], []
    for clip in range(clips):
        done, grad_hidden, *parts = band_layer(
            band_inputs[clip], grad_out, clip, consts, hidden, final
        )
        final = [done]
        grads.append(grad_hidden)
        sums.append(parts)
    band_parts = sums
    b_gate_, b_bias, b_vec, b_gbias = (add_up(t) for t in list(zip(*sums))[4:])
    band_rows = jnp.concatenate([b_vec[2:3], b_vec[1:2], b_vec[0:1], b_gate_[:HEADS]])
    band_vectors = vector_parts(band_rows, b_bias, b_gbias[:, :HEADS])

    if by_clip:
        grads = [g.reshape(groups, chunk_seqs, rows, width) for g in grads]
    else:
        grads = [jnp.concatenate(grads).reshape(groups, chunk_seqs, rows, width)]
    grads = [exchange(g) for g in grads]
    band_sums = flip([parts[:4] for parts in band_parts], devices, BF)
    band_sums, grads[0] = lax.optimization_barrier((band_sums, grads[0]))
    band_sums = lax.psum_scatter(
        band_sums.reshape(-1, width), everyone, scatter_dimension=0, tiled=True
    )
    sums, sums_back, halves = [], [], []
    for chunk in range(chunk_count):
        x, qkv, gate, attended, inverse, probs, middle, act, slope = saved[chunk]
        grad_middle, grad_aug, logit, *parts = time_mlp_back(
            grads[chunk], middle, act, slope, attended, gate, inverse,
            (wo, wu, wd, gains_full[0][1]), (heads, swapped),
        )
        sums.append(parts)
        halves.append((grad_middle, grad_aug, logit))
    last_chunk = chunk_count - 1
    t_bias, t_vec = (add_up(t) for t in list(zip(*sums))[3:])
    mlp_sums = flip([(up, down, out) for down, up, out, _, _ in sums], devices, BF)
    sequences = []
    for chunk in range(chunk_count):
        x, qkv, gate, attended, inverse, probs, middle, act, slope = saved[chunk]
        grad_middle, grad_aug, logit = halves[chunk]
        if chunk == 0:
            mlp_sums, grad_aug = lax.optimization_barrier((mlp_sums, grad_aug))
            mlp_sums = shed_cores(mlp_sums)
        else:
            grad_aug, grad_x = lax.optimization_barrier((grad_aug, grad_x))
        packed_grads = time_attend_back(
            probs, qkv, grad_aug, frame_tables[2], frame_tables[3], swap_t
        )
        if chunk == 0:
            mlp_sums, packed_grads = gain(mlp_sums, packed_grads)
            mlp_sums = shed_chips(mlp_sums)
        if chunk == last_chunk:
            mlp_sums, packed_grads = gain(mlp_sums, packed_grads)
        grad_x, *parts = time_project_back(
            x, packed_grads, logit, grad_middle, (wq, gates_full[0], gains_full[0][0])
        )
        sums_back.append(parts)
        sequences.append(exchange(grad_x).reshape(-1, bands, rows, width))
    t_gate, t_vec0, t_gbias = (add_up(t) for t in list(zip(*sums_back))[1:])
    time_rows = jnp.concatenate([t_vec0, t_vec[1:2], t_vec[0:1], t_gate[:HEADS]])
    time_vectors = vector_parts(time_rows, t_bias, t_gbias[:, :HEADS])
    vectors = jnp.concatenate([time_vectors, band_vectors], axis=1)
    sequences[0], sums_back = lax.optimization_barrier((sequences[0], sums_back))
    last = flip([parts[:1] for parts in sums_back], devices, BF, 6 << 20)
    total = -(-(sizes[0] * width + vectors.shape[1]) // (16 * width)) * 16 - sizes[0]
    vectors = jnp.pad(vectors, ((0, 0), (0, total * width - vectors.shape[1])))
    sequences = [s[k] for s in sequences for k in range(s.shape[0])]
    grad_input = to_frames(sequences[0], 0, clips, perm.T, [])
    last = jnp.concatenate([last, vectors.reshape(devices, total, width)], axis=1)
    last, _ = gain(shed_cores(last), ())
    last, grad_input = gain(shed_chips(last), grad_input)
    last, _ = gain(shed_last(jnp.concatenate([mlp_sums, last], axis=1)), ())
    mlp_sums, last = last[: sum(sizes[1:])], last[sum(sizes[1:]) :]
    grad_input = [grad_input]
    for clip in range(1, clips):
        grad_input = [to_frames(sequences[clip], clip, clips, perm.T, grad_input)]

    tq, vectors = last[: sizes[0]], last[sizes[0] :].reshape(-1)
    bq, bu, bd, bo = cut(band_sums.astype(F32), sizes)
    tu, td, to = cut(mlp_sums, sizes[1:])
    lengths_each = (2 * shard, shard, HEADS * shard, sizes[1], HEADS)
    time_parts = cut(vectors, lengths_each)
    band_parts = cut(vectors[sum(lengths_each) :], lengths_each)
    g_gains, g_b_down, g_gate, g_b_up, g_b_gate = (
        jnp.stack(both) for both in zip(time_parts, band_parts)
    )
    return (
        final[0],
        grad_input[0],
        jnp.stack([tq.T, bq.T]),
        jnp.stack([to, bo]),
        jnp.stack([tu.T, bu.T]),
        g_b_up,
        jnp.stack([td, bd]),
        g_gains.reshape(2, 2, shard),
        g_b_down,
        g_gate.reshape(2, HEADS, shard),
        g_b_gate,
    )


def solution(mesh):
    everyone = ("dp", "fsdp")
    rows = P("fsdp", "dp", None, None)
    last, middle = P(None, None, everyone), P(None, everyone, None)
    return jax.shard_map(
        on_device,
        mesh=mesh,
        in_specs=(
            rows, P("dp"), last, middle, last, P(None, everyone), middle,
            P(None, None, "fsdp"), P(None, "fsdp"), P(None, None, "fsdp"), P(), rows,
        ),
        out_specs=(
            rows, rows, last, middle, last, P(None, everyone), middle,
            P(None, None, "fsdp"), P(None, "fsdp"), P(None, None, "fsdp"), P(),
        ),
        check_vma=False,
    )
```
